32 devices in a mesh: parts: 2 (over y), gx: 4 (over z), gy: 2 (over x), gz: 2 (over core).
Axes of the slice: x: 2, y: 2, z: 4, core: 2. Of those that a mesh axis runs over, the one named last changes fastest.
Arguments:
- populations: float32 [19, 128, 4, 512], P(None, ('parts', 'gz'), 'gy', 'gx'), parts along dimension 1, may hold values from 0 to 4
- solid_mask: int32 [128, 4, 512], P(('parts', 'gz'), 'gy', 'gx'), parts along dimension 0, may hold values 0 or 1
- recycle_plane: int32 [1], replicated, may hold values from 256 to 511
- fringe_bounds: int32 [2], replicated, may hold values from 0 to 383, as said below
- interp_rows: int32 [4], P('gy'), may hold values from 0 to 2
- interp_weights: float32 [4], P('gy'), may hold values from 0 to 1
- mean_scale: float32 [4], P('gy'), may hold values from 0.4 to 0.9
- fluct_scale: float32 [4], P('gy'), may hold values from 1 to 2
Outputs:
- final_populations: float32 [19, 128, 4, 512], P(None, ('parts', 'gz'), 'gy', 'gx'), parts along dimension 1
The draws below stay inside these ranges and needn't reach their ends.
There are 2 independent parts, one for each index of `parts`. The reference program is written for one: setup_inputs(seed, part) draws one part's arguments, and reference() takes and returns one part's arrays. A program takes and returns all parts, laid end to end along the dimension named above; an argument that names none is the same for every part. Nothing has to cross between parts.
Inputs may be any that keep to these rules, and one draw needn't show every extreme that they name: `fringe_bounds`: the second entry is 383; the first lies below 128.
All inputs are finite; a program needn't handle non-finite values. No bound on the sum of `solid_mask` on one device may be relied on, other than what follows from the above.
Results may differ from the reference program's by a relative error of at most 0.0001.
Values sent between devices are 32-bit elements; how exact they have to be, the bound alone decides.
No kernel may reach another device: no remote copies, remote signals or barrier semaphores. Data moves between devices by JAX's collectives and lax.ppermute only.
A program may use at most 64 MiB of HBM per device.

```python
import math
import jax
import jax.numpy as jnp
from jax import lax

STEPS = 2
NX = 512
NY = 4
NZ = 64


lattice_vel = ((0, 0, 0), (1, 0, 0), (-1, 0, 0), (0, 1, 0), (0, -1, 0), (0, 0, 1), (0, 0, -1), (1, 1, 0), (-1, -1, 0), (1, -1, 0), (-1, 1, 0), (1, 0, 1), (-1, 0, -1), (1, 0, -1), (-1, 0, 1), (0, 1, 1), (0, -1, -1), (0, 1, -1), (0, -1, 1))


def draw_populations(key, part):
    subkeys = jax.random.split(key, 5)
    grid_shape = (NZ, NY, NX)
    span_pos = (jnp.arange(NZ, dtype=jnp.float32)[:, None, None] + 0.5) / NZ
    height = (jnp.arange(NY, dtype=jnp.float32)[None, :, None] + 0.5) / NY
    streak_amp = 0.5
    density = jax.random.uniform(subkeys[0], grid_shape, jnp.float32, 0.9, 1.1)
    disorder = jax.random.uniform(subkeys[4], (19,) + grid_shape, jnp.float32, -0.15, 0.15)
    profile = 0.15 * height ** (1.0 / 7.0)
    speed_x = profile * (1.0 + streak_amp * jnp.sin(2.0 * math.pi * span_pos)) + jax.random.uniform(subkeys[1], grid_shape, jnp.float32, -0.04, 0.04)
    speed_y = jax.random.uniform(subkeys[2], grid_shape, jnp.float32, -0.04, 0.04)
    speed_z = jax.random.uniform(subkeys[3], grid_shape, jnp.float32, -0.04, 0.04)
    lattice = jnp.array(lattice_vel, dtype=jnp.float32)
    projected = lattice[:, 0, None, None, None] * speed_x[None] + lattice[:, 1, None, None, None] * speed_y[None] + lattice[:, 2, None, None, None] * speed_z[None]
    speed_sq = speed_x * speed_x + speed_y * speed_y + speed_z * speed_z
    balanced = density[None] * (1.0 + 3.0 * projected + 4.5 * projected * projected - 1.5 * speed_sq[None])
    return (balanced + disorder).astype(jnp.float32)


def draw_fringe_bounds(key, part):
    start_key = jax.random.fold_in(key, 7)
    zone_start = jax.random.randint(start_key, (1,), 0, NX // 4)
    zone_end = jnp.zeros((1,), jnp.int32) + (NX // 4 + NX // 2 - 1)
    return jnp.concatenate([zone_start, zone_end]).astype(jnp.int32)


def place_ends(values, stream_key, smallest, top_value):
    spot = [jax.random.randint(jax.random.fold_in(stream_key, axis), (), 0, length) for axis, length in enumerate(values.shape)]
    longest = values.shape.index(max(values.shape))
    beside = spot[:longest] + [(spot[longest] + 1) % values.shape[longest]] + spot[longest + 1:]
    return values.at[tuple(spot)].set(smallest).at[tuple(beside)].set(top_value)


def steps_of(stream_key, extent, cuts, least, high):
    def one(axis_at, shards_of):
        steps = jax.random.uniform(jax.random.fold_in(jax.random.fold_in(stream_key, 6), axis_at), (shards_of,), jnp.float32, least / len(cuts), high / len(cuts))
        return jnp.repeat(jnp.exp(steps), extent[axis_at] // shards_of).reshape((-1,) + (1,) * (len(extent) - axis_at - 1))

    gain = one(*cuts[0])
    for cut in cuts[1:]:
        gain = gain * one(*cut)
    return gain


def setup_inputs(seed: int = 0, part: int = 0) -> dict:
    keys = jax.random.split(jax.random.key(seed), 9)
    part_splits = jax.random.split(jax.random.fold_in(keys[8], part), 9)
    return {
        "populations": draw_populations(jax.random.fold_in(jax.random.fold_in(keys[8], part), 71), part),
        "solid_mask": place_ends((jax.random.randint(part_splits[1], (NZ, NY, NX), 0, 8) < 1).astype(jnp.int32), jax.random.fold_in(part_splits[1], 1), 0, 1),
        "recycle_plane": jax.random.randint(keys[2], (1,), NX // 2, NX).astype(jnp.int32),
        "fringe_bounds": draw_fringe_bounds(jax.random.fold_in(keys[8], 71), part),
        "interp_rows": place_ends(jax.random.randint(keys[4], (NY,), 0, NY - 1), jax.random.fold_in(keys[4], 1), 0, (NY - 1) - 1).astype(jnp.int32),
        "interp_weights": jnp.clip(1.0 * jax.random.uniform(keys[5], (NY,), jnp.float32) ** steps_of(keys[5], (NY,), ((0, 2),), -0.2, 0.2), 0.0, 1.0),
        "mean_scale": jnp.clip(jnp.exp(math.log(0.9) - 0.8109302 * jax.random.uniform(keys[6], (NY,), jnp.float32) ** steps_of(keys[6], (NY,), ((0, 2),), -0.2, 0.2)), 0.4, 0.9),
        "fluct_scale": jnp.clip(jnp.exp(math.log(2.0) - 0.6931472 * jax.random.uniform(keys[7], (NY,), jnp.float32) ** steps_of(keys[7], (NY,), ((0, 2),), -0.2, 0.2)), 1.0, 2.0),
    }


lattice_vel = ((0, 0, 0), (1, 0, 0), (-1, 0, 0), (0, 1, 0), (0, -1, 0), (0, 0, 1), (0, 0, -1),
               (1, 1, 0), (-1, -1, 0), (1, -1, 0), (-1, 1, 0), (1, 0, 1), (-1, 0, -1),
               (1, 0, -1), (-1, 0, 1), (0, 1, 1), (0, -1, -1), (0, 1, -1), (0, -1, 1))
lattice_weight = (1.0 / 3.0,) + (1.0 / 18.0,) * 6 + (1.0 / 36.0,) * 12
opposite = (0, 2, 1, 4, 3, 6, 5, 8, 7, 10, 9, 12, 11, 14, 13, 16, 15, 18, 17)
mirror_pop = (0, 1, 2, 4, 3, 5, 6, 9, 10, 7, 8, 11, 12, 13, 14, 18, 17, 16, 15)
relax_rate = 1.25
fringe_peak = 0.8


def moments(current):
    density = lattice_weight[0] * current[0]
    moment = [jnp.zeros_like(density), jnp.zeros_like(density), jnp.zeros_like(density)]
    for population in range(1, 19):
        weighted = lattice_weight[population] * current[population]
        density = density + weighted
        for direction in range(3):
            component = lattice_vel[population][direction]
            if component != 0:
                moment[direction] = moment[direction] + component * weighted
    return density, moment[0] / density, moment[1] / density, moment[2] / density


def equilibrium(density, vel_x, vel_y, vel_z, population):
    step_x, step_y, step_z = lattice_vel[population]
    projected = step_x * vel_x + step_y * vel_y + step_z * vel_z
    speed_sq = vel_x * vel_x + vel_y * vel_y + vel_z * vel_z
    return density * (1.0 + 3.0 * projected + 4.5 * projected * projected - 1.5 * speed_sq)


def fringe_ramp(x_global, bounds):
    zone_start = bounds[0]
    finish = bounds[1]
    zone_width = (finish - zone_start).astype(jnp.float32)
    angle_arg = math.pi * ((x_global - zone_start).astype(jnp.float32) + 0.5) / zone_width
    inside = (x_global >= zone_start) & (x_global < finish)
    return jnp.where(inside, fringe_peak * jnp.sin(angle_arg) ** 2, 0.0)


def rescale(plane, plane_mean, row_index, row_weight, mean_gain, fluct_gain):
    lower = jnp.take(plane, row_index, axis=2)
    upper = jnp.take(plane, row_index + 1, axis=2)
    blended = (1.0 - row_weight) * lower + row_weight * upper
    mean_lower = jnp.take(plane_mean, row_index, axis=1)
    mean_upper = jnp.take(plane_mean, row_index + 1, axis=1)
    mean_part = ((1.0 - row_weight) * mean_lower + row_weight * mean_upper)[:, None, :]
    speeds = mean_gain * mean_part[1:] + fluct_gain * (blended[1:] - mean_part[1:])
    return blended[0], speeds[0], speeds[1], speeds[2]


def reference(populations, solid_mask, recycle_plane, fringe_bounds, interp_rows, interp_weights, mean_scale, fluct_scale):
    current = [populations[population] for population in range(19)]
    solid_cell = solid_mask == 1
    x_global = jnp.arange(NX, dtype=jnp.int32)[None, None, :]
    y_global = jnp.arange(NY, dtype=jnp.int32)[None, :, None]
    fringe_weight = fringe_ramp(x_global, fringe_bounds)
    for time_step in range(STEPS):
        density, vel_x, vel_y, vel_z = moments(current)
        plane = jnp.stack([lax.dynamic_index_in_dim(moment_field, recycle_plane[0], 2, False)
                           for moment_field in (density, vel_x, vel_y, vel_z)])
        plane_mean = jnp.sum(plane, axis=1) / NZ
        target = rescale(plane, plane_mean, interp_rows, interp_weights, mean_scale, fluct_scale)
        target_eq = [equilibrium(target[0][:, :, None], target[1][:, :, None], target[2][:, :, None],
                                 target[3][:, :, None], population) for population in range(19)]
        collided = []
        for population in range(19):
            local_eq = equilibrium(density, vel_x, vel_y, vel_z, population)
            relaxed = current[population] - relax_rate * (current[population] - local_eq)
            forced = relaxed + fringe_weight * (target_eq[population] - relaxed)
            collided.append(jnp.where(solid_cell, current[opposite[population]], forced))
        current = []
        for population in range(19):
            step_x, step_y, step_z = lattice_vel[population]
            pulled = jnp.roll(collided[population], (step_z, step_y, step_x), axis=(0, 1, 2))
            if step_x == 1:
                pulled = jnp.where(x_global == 0, target_eq[population], pulled)
            if step_x == -1:
                pulled = jnp.where(x_global == NX - 1, collided[population], pulled)
            if step_y == 1:
                pulled = jnp.where(y_global == 0, collided[opposite[population]], pulled)
            if step_y == -1:
                pulled = jnp.where(y_global == NY - 1, collided[mirror_pop[population]], pulled)
            current.append(pulled)
    return jnp.stack(current)
```

```python
import functools
import math

import jax
import jax.numpy as jnp
from jax import lax
from jax.experimental import pallas as pl
from jax.experimental.pallas import tpu as pltpu
from jax.sharding import PartitionSpec as P

lattice_vel = (
    (0, 0, 0),
    (1, 0, 0),
    (-1, 0, 0),
    (0, 1, 0),
    (0, -1, 0),
    (0, 0, 1),
    (0, 0, -1),
    (1, 1, 0),
    (-1, -1, 0),
    (1, -1, 0),
    (-1, 1, 0),
    (1, 0, 1),
    (-1, 0, -1),
    (1, 0, -1),
    (-1, 0, 1),
    (0, 1, 1),
    (0, -1, -1),
    (0, 1, -1),
    (0, -1, 1),
)
lattice_weight = (1.0 / 3.0,) + (1.0 / 18.0,) * 6 + (1.0 / 36.0,) * 12
opposite = (0, 2, 1, 4, 3, 6, 5, 8, 7, 10, 9, 12, 11, 14, 13, 16, 15, 18, 17)
mirror_pop = (0, 1, 2, 4, 3, 5, 6, 9, 10, 7, 8, 11, 12, 13, 14, 18, 17, 16, 15)
relax_rate = 1.25
fringe_peak = 0.8

DEPTH, ROWS, COLS = 32, 2, 128
SPAN = 2 * DEPTH
MASK = 19
EAST = tuple(i for i in range(19) if lattice_vel[i][0] == 1)
WEST = tuple(i for i in range(19) if lattice_vel[i][0] == -1)
FLAT_X = tuple(i for i in range(19) if lattice_vel[i][0] == 0)
UP = tuple(i for i in range(19) if lattice_vel[i][1] == 1)
DOWN = tuple(i for i in range(19) if lattice_vel[i][1] == -1)
FLAT_Y = tuple(i for i in range(19) if lattice_vel[i][1] == 0)

COLUMN = EAST + (MASK,) + WEST + FLAT_X + (20, 21, 22, 23)
PLACE = {field: at for at, field in enumerate(COLUMN)}
HALF = len(COLUMN) // 2
TROWS = HALF * 8
SIDE = 20
PLANE = 40
EDGE = 4
INNER = DEPTH - EDGE
YFIELDS = 21


def up_down(rows_up):
    moving = UP if rows_up else DOWN
    near = FLAT_Y + moving + (MASK,)
    far = moving + (MASK,)
    return [(f, True) for f in near] + [(f, False) for f in far]


def moments(g):
    w0, w1, w2 = lattice_weight[0], lattice_weight[1], lattice_weight[7]
    axis = g[1] + g[2] + g[3] + g[4] + g[5] + g[6]
    diag = (g[7] + g[8] + g[9] + g[10]) + (g[11] + g[12] + g[13] + g[14]) + (g[15] + g[16] + g[17] + g[18])
    density = w0 * g[0] + w1 * axis + w2 * diag
    inverse = 1.0 / density
    d78, d910 = g[7] - g[8], g[9] - g[10]
    d1112, d1314 = g[11] - g[12], g[13] - g[14]
    d1516, d1718 = g[15] - g[16], g[17] - g[18]
    mx = w1 * (g[1] - g[2]) + w2 * ((d78 + d910) + (d1112 + d1314))
    my = w1 * (g[3] - g[4]) + w2 * ((d78 - d910) + (d1516 + d1718))
    mz = w1 * (g[5] - g[6]) + w2 * ((d1112 - d1314) + (d1516 - d1718))
    return density, mx * inverse, my * inverse, mz * inverse


def equilibria(density, vx, vy, vz, wanted=range(19)):
    base = density - 1.5 * density * (vx * vx + vy * vy + vz * vz)
    linear = 3.0 * density
    square = 4.5 * density
    out = {}
    for i in wanted:
        if i in out:
            continue
        if i == 0:
            out[0] = base
            continue
        first = i if i % 2 == 1 else i - 1
        cx, cy, cz = lattice_vel[first]
        p = None
        for c, v in ((cx, vx), (cy, vy), (cz, vz)):
            if c == 0:
                continue
            p = (v if c == 1 else -v) if p is None else (p + v if c == 1 else p - v)
        even = base + square * p * p
        odd = linear * p
        out[first] = even + odd
        out[first + 1] = even - odd
    return out


def lanes(shape):
    return lax.broadcasted_iota(jnp.int32, shape, len(shape) - 1)


def ramp(x, start, finish):
    width = (finish - start).astype(jnp.float32)
    angle = math.pi * ((x - start).astype(jnp.float32) + 0.5) / width
    inside = (x >= start) & (x < finish)
    return jnp.where(inside, fringe_peak * jnp.sin(angle) ** 2, 0.0)


def relax_kernel(ways, sc, prm, pops, solid, relaxed, lam, zmsg, *rest):
    ysm, ymn, grid = rest[: len(ways)], rest[len(ways) : 2 * len(ways)], rest[-1]
    gx, gy, rp = sc[0], sc[1], sc[2]
    x0 = gx * COLS
    off = rp - x0
    lane = lanes((8, 128))
    sub = lax.broadcasted_iota(jnp.int32, (8, 128), 0)
    special = jnp.where(
        lane < 3, x0 - 2 + lane, jnp.where(lane < 6, x0 + COLS - 4 + lane, rp - 7 + lane)
    )
    lam[...] = ramp(jnp.where(sub == 0, x0 + lane, special), sc[3], sc[4])

    col = lane % 8
    slot = lane // 8
    place = off + col - 5
    here = (place >= 0) & (place < COLS) & (col >= 4) & (col < 7)
    owner = (off >= 0) & (off < COLS)
    static = col < 4
    shift0 = 5 - off + 8 * 128 * 64
    for y in range(ROWS):
        values = jnp.zeros((8, 128), jnp.float32)
        for k in range(4):
            values = jnp.where((slot == k) & (col == 7) & owner, prm[k, y], values)
        for chunk in range(DEPTH // 8):
            rows = pl.ds(16 * chunk + y, 8, stride=2)
            g = [pops[i, rows, :] for i in range(19)]
            wall = solid[rows, :] == 1
            density, vx, vy, vz = moments(g)
            eq = equilibria(density, vx, vy, vz)
            field = {}
            for i in range(19):
                loose = g[i] - relax_rate * (g[i] - eq[i])
                field[i] = jnp.where(wall, g[opposite[i]], loose)
            field[MASK] = jnp.where(wall, 1.0, 0.0)
            field[20], field[21], field[22], field[23] = density, vx, vy, vz
            here_z = pl.ds(8 * chunk, 8)
            for f in range(20):
                relaxed[f, y, here_z, :] = field[f]
            for half in range(2):
                fixed = jnp.zeros((8, 128), jnp.float32)
                moving = jnp.zeros((8, 128), jnp.float32)
                for k in range(HALF):
                    v = field[COLUMN[half * HALF + k]]
                    mine = slot == k
                    if half * HALF + k < SIDE:
                        fixed = jnp.where(mine, pltpu.roll(v, 2 + 8 * k, 1), fixed)
                    moving = jnp.where(mine, pltpu.roll(v, (shift0 + 8 * k) % 128, 1), moving)
                rest_of = values if half == 0 else jnp.zeros((8, 128), jnp.float32)
                packed = jnp.where(static, fixed, jnp.where(here, moving, rest_of))
                grid[pl.ds((y * 2 + half) * DEPTH + 8 * chunk, 8), :] = packed
    columns = grid[...].T[:TROWS]
    zmsg[pl.ds(0, TROWS), :] = columns
    for f in range(20):
        for y in range(ROWS):
            at = TROWS + (f * 2 + y) * EDGE
            zmsg[pl.ds(at, 2), :] = relaxed[f, y, pl.ds(0, 2), :]
            zmsg[pl.ds(at + 2, 2), :] = relaxed[f, y, pl.ds(DEPTH - 2, 2), :]

    def pack(way, small, bulk):
        for n, (f, near) in enumerate(up_down(way)):
            y = 1 if near == way else 0
            at = TROWS + n * EDGE
            small[pl.ds(at, 2), :] = relaxed[f, y, pl.ds(0, 2), :]
            small[pl.ds(at + 2, 2), :] = relaxed[f, y, pl.ds(DEPTH - 2, 2), :]
            bulk[pl.ds(n * INNER, INNER), :] = relaxed[f, y, pl.ds(2, INNER), :]

    for at, way in enumerate(ways):
        ysm[at][pl.ds(0, TROWS), :] = columns
        if way is None:

            @pl.when(gy == 0)
            def _():
                pack(True, ysm[at], ymn[at])

            @pl.when(gy != 0)
            def _():
                pack(False, ysm[at], ymn[at])

        else:
            pack(way, ysm[at], ymn[at])


def join(mine, other):
    even = (lanes(mine.shape) // DEPTH) % 2 == 0
    first = jnp.where(even, mine, pltpu.roll(other, DEPTH, 1))
    second = jnp.where(even, pltpu.roll(mine, 128 - DEPTH, 1), other)
    return first, second


def cross_kernel(pairs, swap, sc, *refs):
    blocks = refs[: 2 * pairs]
    full, right, left, plane = refs[2 * pairs :]
    gy = sc[1]
    for n in range(pairs):
        first, second = join(
            blocks[2 * n][pl.ds(0, TROWS), :], blocks[2 * n + 1][pl.ds(0, TROWS), :]
        )
        full[n, pl.ds(0, TROWS), :] = first
        full[n, pl.ds(TROWS, TROWS), :] = second
        for c in range(2):
            at = (n * 2 + c) * SIDE
            right[pl.ds(at, SIDE), :] = full[n, pl.ds(c, SIDE, stride=8), :]
            left[pl.ds(at, SIDE), :] = full[n, pl.ds(2 + c, SIDE, stride=8), :]
        if n == 0 or swap:
            base = 0
            if swap:
                base = pl.multiple_of((gy if n == 0 else 1 - gy) * PLANE, 8)
            plane[pl.ds(base, 6), :] = full[n, pl.ds(4, 6, stride=8), :]
            plane[pl.ds(base + 6, 24), :] = full[n, pl.ds(5, 24, stride=8), :]
            plane[pl.ds(base + 30, 6), :] = full[n, pl.ds(5 * 8 + 6, 6, stride=8), :]
            plane[pl.ds(base + 36, 4), :] = full[n, pl.ds(7, 4, stride=8), :]
    if swap:
        tail = pairs * 2 * SIDE
        right[pl.ds(tail, 2 * PLANE), :] = plane[...]
        left[pl.ds(tail, 2 * PLANE), :] = plane[...]


def strips_kernel(pairs, slots, total_y, total_x, sc, lam, full, west, east, plane_in, out, side, deck, shelf):
    gx, gy, rp = sc[0], sc[1], sc[2]
    last_x = sc[5]
    deep = deck.shape[0] // PLANE
    side[...] = jnp.zeros_like(side)
    deck[...] = jnp.zeros_like(deck)
    shelf[...] = jnp.zeros_like(shelf)

    def apart(v):
        low = lanes(v.shape) < SPAN
        turned = pltpu.roll(v, SPAN, 1)
        return jnp.where(low, v, turned), jnp.where(low, turned, v)

    def lay(strip, c, first, v):
        top, bottom = apart(v)
        side[strip, c, pl.ds(first, SIDE, stride=8), :] = top
        side[strip, c, pl.ds(first + 1, SIDE, stride=8), :] = bottom

    def spread(n, first):
        sides = (n * 2) * SIDE
        lay(0, 0, first, west[pl.ds(sides, SIDE), :])
        lay(0, 1, first, west[pl.ds(sides + SIDE, SIDE), :])
        lay(0, 2, first, full[n, pl.ds(2, SIDE, stride=8), :])
        lay(1, 0, first, full[n, pl.ds(1, SIDE, stride=8), :])
        lay(1, 1, first, east[pl.ds(sides, SIDE), :])
        lay(1, 2, first, east[pl.ds(sides + SIDE, SIDE), :])

    for n in range(pairs):
        if slots[n] is None:

            @pl.when(gy == 0)
            def _():
                spread(n, 4)

            @pl.when(gy != 0)
            def _():
                spread(n, 0)

        else:
            spread(n, slots[n])
    for n in range(total_y // 2):
        top, bottom = apart(plane_in[pl.ds(n * PLANE, PLANE), :])
        deck[pl.ds(2 * n, PLANE, stride=deep), :] = top
        deck[pl.ds(2 * n + 1, PLANE, stride=deep), :] = bottom

    def deck_at(row):
        return deck[pl.ds(row * deep, deep), :]

    which, ratio, mean_gain, fluct_gain = (deck_at(36 + k) for k in range(4))

    def target(fields):
        def blend(v):
            low, high = v[0:1], v[1:2]
            low = jnp.broadcast_to(low, v.shape)
            high = jnp.broadcast_to(high, v.shape)
            for r in range(1, total_y - 1):
                chosen = which == float(r)
                low = jnp.where(chosen, jnp.broadcast_to(v[r : r + 1], v.shape), low)
                high = jnp.where(chosen, jnp.broadcast_to(v[r + 1 : r + 2], v.shape), high)
            return (1.0 - ratio) * low + ratio * high

        result = [blend(fields[0])]
        for v in fields[1:]:
            mean = jnp.sum(v, axis=1, keepdims=True) * (1.0 / 128.0)
            mean = blend(jnp.broadcast_to(mean, v.shape))
            result.append(mean_gain * mean + fluct_gain * (blend(v) - mean))
        return result

    def local(fields):
        got = []
        for k, v in enumerate(fields):
            shelf[k, pl.ds(8, deep), :] = v
            got.append(shelf[k, pl.ds(6 + 2 * gy, 8), :])
        return got

    def shifted(v, i):
        _, cy, cz = lattice_vel[i]
        if cz:
            v = pltpu.roll(v, cz % 128, 1)
        if cy:
            v = pltpu.roll(v, cy % v.shape[0], 0)
        return v

    def forced(value, gate, goal):
        return value + gate * (goal - value)

    def strip(read, gates, teq, row, edge):
        gate = [(1.0 - read(c, MASK)) * gates[c] for c in range(3)]
        middle = [forced(read(1, i), gate[1], teq[i]) for i in range(19)]
        bottom, top = row == 0, row == total_y - 1
        g = []
        for i in range(19):
            cx, cy, _ = lattice_vel[i]
            if cx == 0:
                v = shifted(middle[i], i)
            else:
                c = 1 - cx
                v = shifted(forced(read(c, i), gate[c], teq[i]), i)
                if cx == -1 and edge is not None:
                    v = jnp.where(edge, middle[i], v)
            if cy == 1:
                v = jnp.where(bottom, middle[opposite[i]], v)
            if cy == -1:
                v = jnp.where(top, middle[mirror_pop[i]], v)
            g.append(v)
        return middle, g, gate

    def lam_at(c, rows):
        return jnp.broadcast_to(lam[1:2, c : c + 1], (rows, 128))

    target0 = target([deck_at(6 + 20 + k) for k in range(4)])
    teq0 = equilibria(*target0)
    start = {0: (0, 0), 1: (6, 0), 2: (30, 5)}

    def read_plane(c, f):
        base, less = start[c]
        return deck_at(base + PLACE[f] - less)

    row = lax.broadcasted_iota(jnp.int32, (deep, 128), 0)
    _, g1, _ = strip(
        read_plane, [lam_at(6 + c, deep) for c in range(3)], teq0, row, rp == total_x - 1
    )
    target1 = target(list(moments(g1)))
    near0, near1 = local(target0), local(target1)
    goal0, goal1 = equilibria(*near0), equilibria(*near1)

    row = lax.broadcasted_iota(jnp.int32, (8, 128), 0) + 2 * gy - 2
    first, second = [], []
    for s, wanted in ((0, EAST), (1, WEST)):

        def read_side(c, f):
            return side[s, c, pl.ds(PLACE[f] * 8, 8), :]

        middle, g1, gate = strip(
            read_side, [lam_at(3 * s + c, 8) for c in range(3)], goal0, row, None
        )
        density, vx, vy, vz = moments(g1)
        eq = equilibria(density, vx, vy, vz, wanted)
        wall = read_side(1, MASK) == 1.0
        for i in wanted:
            loose = g1[i] - relax_rate * (g1[i] - eq[i])
            later = forced(jnp.where(wall, g1[opposite[i]], loose), gate[1], goal1[i])
            a, b = shifted(middle[i], i), shifted(later, i)
            if s == 0:
                a, b = jnp.where(gx == 0, goal0[i], a), jnp.where(gx == 0, goal1[i], b)
            else:
                a = jnp.where(gx == last_x, forced(read_side(0, i), gate[0], goal0[i]), a)
            first.append(a)
            second.append(b)
    blank = [jnp.zeros((16, 128), jnp.float32)]
    for n, rows in enumerate((first + near0 + blank, second + near1 + blank)):
        turned = pltpu.roll(jnp.concatenate(rows, axis=0), 2, 1).T
        out[pl.ds(48 * n, 48), :] = turned[:48]


def steps_kernel(ways, total_y, sc, lam, relaxed, zmsg, cols, *rest):
    count = len(ways)
    bulk, small, small_other = rest[:count], rest[count : 2 * count], rest[2 * count : 3 * count]
    out, early, late = rest[3 * count :]
    gx, gy = sc[0], sc[1]
    at_end = gx == sc[5]
    bottom, top = gy == 0, gy == sc[6]
    lane = lanes((8, 128))
    at_first, at_last = lane == 0, lane == COLS - 1
    zone = jnp.broadcast_to(lam[0:1, :], (8, 128))

    def column(step, index, at):
        return jnp.broadcast_to(cols[pl.ds(48 * step + at, 8), index : index + 1], (8, 128))

    def goals(step, slot, at, wanted):
        return equilibria(*(column(step, 80 + 8 * k + slot, at) for k in range(4)), wanted)

    def finish(slot, fields):
        for chunk in range(5):
            rows = pl.ds(8 * chunk, 8)
            gate = (1.0 - early[MASK, slot, rows, :]) * zone
            goal = goals(0, slot, 8 * chunk, fields)
            for i in fields:
                v = early[i, slot, rows, :]
                early[i, slot, rows, :] = v + gate * (goal[i] - v)

    def pull(ref, slot, lead, step, at, lift, mine):
        r = at - lift
        g = []
        for i in range(19):
            cx, cy, cz = lattice_vel[i]
            v = ref[i, slot - cy - lead, pl.ds(r - cz, 8), :]
            if cx == 1:
                edge = column(step, EAST.index(i) * 8 + slot, at)
                v = jnp.where(at_first, edge, pltpu.roll(v, 1, 1))
            if cx == -1:
                edge = column(step, 40 + WEST.index(i) * 8 + slot, at)
                if step == 1:
                    edge = jnp.where(at_end, ref[i, slot - lead, pl.ds(r, 8), :], edge)
                v = jnp.where(at_last, edge, pltpu.roll(v, COLS - 1, 1))
            if mine and cy == 1 and slot == 2:
                v = jnp.where(bottom, ref[opposite[i], slot - lead, pl.ds(r, 8), :], v)
            if mine and cy == -1 and slot == 3:
                v = jnp.where(top, ref[mirror_pop[i], slot - lead, pl.ds(r, 8), :], v)
            g.append(v)
        return g

    def collide(slot, wanted, mine):
        for chunk in range(5):
            at = 1 + 8 * chunk
            g = pull(early, slot, 0, 0, at, 0, mine)
            density, vx, vy, vz = moments(g)
            eq = equilibria(density, vx, vy, vz, wanted)
            goal = goals(1, slot, at, wanted)
            solid = early[MASK, slot, pl.ds(at, 8), :]
            gate = (1.0 - solid) * zone
            wall = solid == 1.0
            for i in wanted:
                loose = g[i] - relax_rate * (g[i] - eq[i])
                v = jnp.where(wall, g[opposite[i]], loose)
                late[i, slot - 1, pl.ds(8 * chunk, 8), :] = v + gate * (goal[i] - v)

    for f in range(20):
        for y in range(ROWS):
            slot = 2 + y
            at = TROWS + (f * 2 + y) * EDGE
            early[f, slot, pl.ds(2, DEPTH), :] = relaxed[f, y, :, :]
            early[f, slot, pl.ds(DEPTH + 2, 2), :] = zmsg[pl.ds(at, 2), :]
            early[f, slot, pl.ds(0, 2), :] = zmsg[pl.ds(at + 2, 2), :]
    for slot in (2, 3):
        finish(slot, range(19))

    def beside(n, came_up):
        near_slot, far_slot = (1, 0) if came_up else (4, 5)
        for k, (f, near) in enumerate(up_down(came_up)):
            slot = near_slot if near else far_slot
            at = TROWS + k * EDGE
            early[f, slot, pl.ds(0, 2), :] = small_other[n][pl.ds(at + 2, 2), :]
            early[f, slot, pl.ds(2, 2), :] = small[n][pl.ds(at, 2), :]
            early[f, slot, pl.ds(4, INNER), :] = bulk[n][pl.ds(k * INNER, INNER), :]
            early[f, slot, pl.ds(DEPTH, 2), :] = small[n][pl.ds(at + 2, 2), :]
            early[f, slot, pl.ds(DEPTH + 2, 2), :] = small_other[n][pl.ds(at, 2), :]
        moving = UP if came_up else DOWN
        finish(near_slot, FLAT_Y + moving)
        finish(far_slot, moving)
        collide(near_slot, moving, False)

    for n, way in enumerate(ways):
        if way is not False:

            @pl.when(jnp.logical_not(bottom))
            def _():
                beside(n, True)

        if way is not True:

            @pl.when(jnp.logical_not(top))
            def _():
                beside(n, False)

    for slot in (2, 3):
        collide(slot, range(19), True)
    for y in range(ROWS):
        for chunk in range(DEPTH // 8):
            g = pull(late, 2 + y, 1, 1, 2 + 8 * chunk, 1, True)
            for i in range(19):
                out[i, pl.ds(16 * chunk + y, 8, stride=2), :] = g[i]


def call(kernel, outs, scratch, limit, *args, scalars=1):
    smem = pl.BlockSpec(memory_space=pltpu.SMEM)
    vmem = pl.BlockSpec(memory_space=pltpu.VMEM)
    return pl.pallas_call(
        kernel,
        out_shape=[jax.ShapeDtypeStruct(s, jnp.float32) for s in outs],
        in_specs=[smem] * scalars + [vmem] * (len(args) - scalars),
        out_specs=[vmem] * len(outs),
        scratch_shapes=[pltpu.VMEM(s, jnp.float32) for s in scratch],
        compiler_params=pltpu.CompilerParams(vmem_limit_bytes=limit << 20),
    )(*args)


def ring(count, step):
    return [(i, (i + step) % count) for i in range(count)]


def body(populations, solid_mask, recycle_plane, fringe_bounds, interp_rows, interp_weights, mean_scale, fluct_scale):
    size_x, size_y = lax.axis_size("gx"), lax.axis_size("gy")
    total_x, total_y = COLS * size_x, ROWS * size_y
    gx, gy = lax.axis_index("gx"), lax.axis_index("gy")
    swap = size_y == 2
    ways = (None,) if swap else (True, False)
    pairs = 1 + len(ways)
    sc = jnp.stack([gx, gy, recycle_plane[0], fringe_bounds[0], fringe_bounds[1], jnp.int32(size_x - 1), jnp.int32(size_y - 1)])
    prm = jnp.stack([interp_rows.astype(jnp.float32), interp_weights, mean_scale, fluct_scale])
    pops = populations.reshape(19, DEPTH * ROWS, COLS)
    solid = solid_mask.reshape(DEPTH * ROWS, COLS)

    small_rows = TROWS + 88
    bulk_rows = 592
    z_rows = TROWS + 40 * EDGE
    made = call(
        functools.partial(relax_kernel, ways),
        [(20, ROWS, DEPTH, COLS), (8, 128), (z_rows, 128)] + [(small_rows, 128)] * len(ways) + [(bulk_rows, 128)] * len(ways),
        [(128, 128)],
        8,
        sc,
        prm,
        pops,
        solid,
        scalars=2,
    )
    relaxed, lam, z_out = made[:3]
    small_out, bulk_out = made[3 : 3 + len(ways)], made[3 + len(ways) :]

    def across(v, way):
        if way is None:
            return lax.ppermute(v, "gy", ring(2, 1))
        step = 1 if way else -1
        return lax.ppermute(v, "gy", [(i, i + step) for i in range(size_y) if 0 <= i + step < size_y])

    small = [across(v, way) for v, way in zip(small_out, ways)]
    bulk = [across(v, way) for v, way in zip(bulk_out, ways)]
    z_in = lax.ppermute(z_out, "gz", ring(2, 1))
    small_other = [lax.ppermute(v, "gz", ring(2, 1)) for v in small]

    blocks = [z_out, z_in]
    for a, b in zip(small, small_other):
        blocks += [a, b]
    edge_rows = pairs * 2 * SIDE + (2 * PLANE if swap else 0)
    full, right, left, plane = call(
        functools.partial(cross_kernel, pairs, swap),
        [(pairs, 2 * TROWS, 128), (edge_rows, 128), (edge_rows, 128), (PLANE * (2 if swap else 1), 128)],
        [],
        4,
        sc,
        *blocks,
    )
    west = lax.ppermute(right, "gx", ring(size_x, 1))
    east = lax.ppermute(left, "gx", ring(size_x, -1))
    if swap and size_x == 4:
        tail = pairs * 2 * SIDE
        far = lax.ppermute(plane, "gx", ring(4, 2))
        plane = plane + far + west[tail:] + east[tail:]
    elif swap:
        plane = lax.psum(plane, "gx")
    else:
        spot = jnp.zeros((size_y, PLANE, 128), jnp.float32)
        spot = lax.dynamic_update_slice(spot, plane[None], (gy, 0, 0))
        plane = lax.psum(spot, ("gx", "gy")).reshape(size_y * PLANE, 128)

    deep = max(8, total_y)
    slots = (2,) + ((None,) if swap else (0, 4))
    (cols,) = call(
        functools.partial(strips_kernel, pairs, slots, total_y, total_x),
        [(96, 128)],
        [(2, 3, SIDE * 8, 128), (PLANE * deep, 128), (4, 16 + deep, 128)],
        8,
        sc,
        lam,
        full,
        west,
        east,
        plane,
    )
    (out,) = call(
        functools.partial(steps_kernel, ways, total_y),
        [(19, DEPTH * ROWS, COLS)],
        [(20, 6, 48, 128), (19, 4, 48, 128)],
        12,
        sc,
        lam,
        relaxed,
        z_in,
        cols,
        *bulk,
        *small,
        *small_other,
    )
    return out.reshape(populations.shape)


def solution(mesh):
    placed = (
        P(None, ("parts", "gz"), "gy", "gx"),
        P(("parts", "gz"), "gy", "gx"),
        P(),
        P(),
        P("gy"),
        P("gy"),
        P("gy"),
        P("gy"),
    )
    return jax.shard_map(
        body,
        mesh=mesh,
        in_specs=placed,
        out_specs=P(None, ("parts", "gz"), "gy", "gx"),
        check_vma=False,
    )
```

```python
import functools
import math

import jax
import jax.numpy as jnp
from jax import lax
from jax.experimental import pallas as pl
from jax.experimental.pallas import tpu as pltpu
from jax.sharding import PartitionSpec as P

lattice_vel = (
    (0, 0, 0),
    (1, 0, 0),
    (-1, 0, 0),
    (0, 1, 0),
    (0, -1, 0),
    (0, 0, 1),
    (0, 0, -1),
    (1, 1, 0),
    (-1, -1, 0),
    (1, -1, 0),
    (-1, 1, 0),
    (1, 0, 1),
    (-1, 0, -1),
    (1, 0, -1),
    (-1, 0, 1),
    (0, 1, 1),
    (0, -1, -1),
    (0, 1, -1),
    (0, -1, 1),
)
lattice_weight = (1.0 / 3.0,) + (1.0 / 18.0,) * 6 + (1.0 / 36.0,) * 12
opposite = (0, 2, 1, 4, 3, 6, 5, 8, 7, 10, 9, 12, 11, 14, 13, 16, 15, 18, 17)
mirror_pop = (0, 1, 2, 4, 3, 5, 6, 9, 10, 7, 8, 11, 12, 13, 14, 18, 17, 16, 15)
relax_rate = 1.25
fringe_peak = 0.8

DEPTH, ROWS, COLS = 32, 2, 128
SPAN = 2 * DEPTH
MASK = 19
EAST = (1, 11, 13, 7, 9)
WEST = (8, 10, 2, 12, 14)
FLAT_X = tuple(i for i in range(19) if lattice_vel[i][0] == 0)
UP = tuple(i for i in range(19) if lattice_vel[i][1] == 1)
DOWN = tuple(i for i in range(19) if lattice_vel[i][1] == -1)
FLAT_Y = tuple(i for i in range(19) if lattice_vel[i][1] == 0)

COLUMN = EAST + (MASK,) + WEST + FLAT_X + (20, 21, 22, 23)
PLACE = {field: at for at, field in enumerate(COLUMN)}
HALF = len(COLUMN) // 2
TROWS = HALF * 8
SIDE = 20
TO_EAST = ((0, 0, 8), (0, 11, 9), (1, 0, 6))
TO_WEST = ((0, 3, 8), (0, 11, 9), (1, 5, 6))
TRAVEL = 23
DECK = ((4, 0, 6), (5, 0, 24), (6, 5, 6), (7, 0, 4))
DECK_AT = {4: 0, 5: 6, 6: 30 - 5, 7: 36}
DECK_ROWS = 40
SUMS = 11
EDGE = 4
INNER = DEPTH - EDGE
PIECES = 2


def up_down(rows_up):
    moving = UP if rows_up else DOWN
    near = FLAT_Y + moving + (MASK,)
    far = moving + (MASK,)
    return [(f, True) for f in near] + [(f, False) for f in far]


def sums(g):
    w0, w1, w2 = lattice_weight[0], lattice_weight[1], lattice_weight[7]
    axis = g[1] + g[2] + g[3] + g[4] + g[5] + g[6]
    diag = (g[7] + g[8] + g[9] + g[10]) + (g[11] + g[12] + g[13] + g[14]) + (g[15] + g[16] + g[17] + g[18])
    density = w0 * g[0] + w1 * axis + w2 * diag
    d78, d910 = g[7] - g[8], g[9] - g[10]
    d1112, d1314 = g[11] - g[12], g[13] - g[14]
    d1516, d1718 = g[15] - g[16], g[17] - g[18]
    mx = w1 * (g[1] - g[2]) + w2 * ((d78 + d910) + (d1112 + d1314))
    my = w1 * (g[3] - g[4]) + w2 * ((d78 - d910) + (d1516 + d1718))
    mz = w1 * (g[5] - g[6]) + w2 * ((d1112 - d1314) + (d1516 - d1718))
    return density, mx, my, mz


def velocity(density, mx, my, mz):
    inverse = 1.0 / density
    return density, mx * inverse, my * inverse, mz * inverse


def moments(g):
    return velocity(*sums(g))


def equilibria(density, vx, vy, vz, wanted=range(19)):
    base = density - 1.5 * density * (vx * vx + vy * vy + vz * vz)
    linear = 3.0 * density
    square = 4.5 * density
    out = {}
    for i in wanted:
        if i in out:
            continue
        if i == 0:
            out[0] = base
            continue
        first = i if i % 2 == 1 else i - 1
        cx, cy, cz = lattice_vel[first]
        p = None
        for c, v in ((cx, vx), (cy, vy), (cz, vz)):
            if c == 0:
                continue
            p = (v if c == 1 else -v) if p is None else (p + v if c == 1 else p - v)
        even = base + square * p * p
        odd = linear * p
        out[first] = even + odd
        out[first + 1] = even - odd
    return out


def lanes(shape):
    return lax.broadcasted_iota(jnp.int32, shape, len(shape) - 1)


def ramp(x, start, finish):
    width = (finish - start).astype(jnp.float32)
    angle = math.pi * ((x - start).astype(jnp.float32) + 0.5) / width
    inside = (x >= start) & (x < finish)
    return jnp.where(inside, fringe_peak * jnp.sin(angle) ** 2, 0.0)


def relax_kernel(ways, total_x, *refs):
    recycle, pops_in, solid_in = refs[:3]
    small_in = refs[3:8]
    relaxed, lam, zmsg = refs[8:11]
    rest = refs[11:]
    ysm, ymn = rest[: len(ways)], rest[len(ways) : 2 * len(ways)]
    grid, pops, solid = rest[2 * len(ways) : 2 * len(ways) + 3]
    small, sem = rest[2 * len(ways) + 3 : -1], rest[-1]
    loads = [
        [pltpu.make_async_copy(a.at[..., rows, :], b.at[..., rows, :], sem.at[2 * n + m]) for m, (a, b) in enumerate(((pops_in, pops), (solid_in, solid)))]
        for n, rows in enumerate(pl.ds(n * 2 * DEPTH // PIECES, 2 * DEPTH // PIECES) for n in range(PIECES))
    ]
    pieces = DEPTH // 8
    scalars = [pltpu.make_async_copy(a, b, sem.at[2 * PIECES + n]) for n, (a, b) in enumerate(zip(small_in, small))]
    for copy in loads[0] + scalars:
        copy.start()
    for load in loads[1:]:
        for copy in load:
            copy.start()
    for copy in scalars:
        copy.wait()
    bounds, rows_in, weights_in, mean_in, fluct_in = small
    gx, gy, rp = lax.axis_index("gx"), lax.axis_index("gy"), recycle[0]
    x0 = gx * COLS
    off = rp - x0
    lane = lanes((8, 128))
    sub = lax.broadcasted_iota(jnp.int32, (8, 128), 0)
    special = jnp.where(
        lane < 3, x0 - 2 + lane, jnp.where(lane < 6, x0 + COLS - 4 + lane, rp - 7 + lane)
    )
    shares = ramp(jnp.where(sub == 0, x0 + lane, special), bounds[0], bounds[1])
    lam[...] = jnp.where(sub < 2, shares, jnp.where(rp == total_x - 1, 1.0, 0.0))

    col = lane % 8
    slot = lane // 8
    place = off + col - 5
    here = (place >= 0) & (place < COLS) & (col >= 4) & (col < 7)
    static = col < 4
    shift0 = 5 - off + 8 * 128 * 64
    extras = []
    for y in range(ROWS):
        values = jnp.zeros((8, 128), jnp.float32)
        for k, v in enumerate((rows_in[y].astype(jnp.float32), weights_in[y], mean_in[y], fluct_in[y])):
            values = jnp.where((slot == k) & (col == 7), v, values)
        extras.append(values)
    for chunk in range(pieces):
        if chunk % (pieces // PIECES) == 0:
            for copy in loads[chunk // (pieces // PIECES)]:
                copy.wait()
        for y in range(ROWS):
            rows = pl.ds(16 * chunk + y, 8, stride=2)
            g = [pops[i, rows, :] for i in range(19)]
            wall = solid[rows, :] == 1
            density, vx, vy, vz = moments(g)
            eq = equilibria(density, vx, vy, vz)
            field = {}
            for i in range(19):
                loose = g[i] - relax_rate * (g[i] - eq[i])
                field[i] = jnp.where(wall, g[opposite[i]], loose)
            field[MASK] = jnp.where(wall, 1.0, 0.0)
            field[20], field[21], field[22], field[23] = density, vx, vy, vz
            here_z = pl.ds(8 * chunk, 8)
            for f in range(20):
                relaxed[f, y, here_z, :] = field[f]
            for half in range(2):
                fixed = jnp.zeros((8, 128), jnp.float32)
                moving = jnp.zeros((8, 128), jnp.float32)
                for k in range(HALF):
                    v = field[COLUMN[half * HALF + k]]
                    mine = slot == k
                    if half * HALF + k < SIDE:
                        fixed = jnp.where(mine, pltpu.roll(v, 2 + 8 * k, 1), fixed)
                    moving = jnp.where(mine, pltpu.roll(v, (shift0 + 8 * k) % 128, 1), moving)
                rest_of = extras[y] if half == 0 else jnp.zeros((8, 128), jnp.float32)
                packed = jnp.where(static, fixed, jnp.where(here, moving, rest_of))
                grid[pl.ds((y * 2 + half) * DEPTH + 8 * chunk, 8), :] = packed
    columns = grid[...].T[:TROWS]
    zmsg[pl.ds(0, TROWS), :] = columns
    for f in range(20):
        for y in range(ROWS):
            at = TROWS + (f * 2 + y) * EDGE
            zmsg[pl.ds(at, 2), :] = relaxed[f, y, pl.ds(0, 2), :]
            zmsg[pl.ds(at + 2, 2), :] = relaxed[f, y, pl.ds(DEPTH - 2, 2), :]

    def pack(way, small, bulk):
        for n, (f, near) in enumerate(up_down(way)):
            y = 1 if near == way else 0
            at = TROWS + n * EDGE
            small[pl.ds(at, 2), :] = relaxed[f, y, pl.ds(0, 2), :]
            small[pl.ds(at + 2, 2), :] = relaxed[f, y, pl.ds(DEPTH - 2, 2), :]
            bulk[pl.ds(n * INNER, INNER), :] = relaxed[f, y, pl.ds(2, INNER), :]

    for at, way in enumerate(ways):
        ysm[at][pl.ds(0, TROWS), :] = columns
        if way is None:

            @pl.when(gy == 0)
            def _():
                pack(True, ysm[at], ymn[at])

            @pl.when(gy != 0)
            def _():
                pack(False, ysm[at], ymn[at])

        else:
            pack(way, ysm[at], ymn[at])


def join(mine, other):
    even = (lanes(mine.shape) // DEPTH) % 2 == 0
    first = jnp.where(even, mine, pltpu.roll(other, DEPTH, 1))
    second = jnp.where(even, pltpu.roll(mine, 128 - DEPTH, 1), other)
    return first, second


def apart(v):
    low = lanes(v.shape) < SPAN
    turned = pltpu.roll(v, SPAN, 1)
    return jnp.where(low, v, turned), jnp.where(low, turned, v)


def shifted(v, i):
    _, cy, cz = lattice_vel[i]
    if cz:
        v = pltpu.roll(v, cz % 128, 1)
    if cy:
        v = pltpu.roll(v, cy % v.shape[0], 0)
    return v


def strip(value, row, total_y, edge):
    held = {}

    def middle(i):
        if i not in held:
            held[i] = value(1, i)
        return held[i]

    bottom, top = row == 0, row == total_y - 1
    g = []
    for i in range(19):
        cx, cy, _ = lattice_vel[i]
        v = shifted(middle(i) if cx == 0 else value(1 - cx, i), i)
        if cx == -1 and edge is not None:
            v = jnp.where(edge, middle(i), v)
        if cy == 1:
            v = jnp.where(bottom, middle(opposite[i]), v)
        if cy == -1:
            v = jnp.where(top, middle(mirror_pop[i]), v)
        g.append(v)
    return middle, g


def lam_at(lam, c, rows):
    return jnp.broadcast_to(lam[1:2, c : c + 1], (rows, 128))


def at_outlet(lam, rows):
    return jnp.broadcast_to(lam[2:3, 0:1], (rows, 128)) == 1.0


def cross_kernel(slots, swap, total_y, lam, *refs):
    pairs = len(slots)
    blocks = refs[: 2 * pairs]
    full, right, left, plane, gains, deck = refs[2 * pairs :]
    gy = lax.axis_index("gy")
    if swap:
        deck[...] = jnp.zeros_like(deck)
    for n in range(pairs):
        first, second = join(
            blocks[2 * n][pl.ds(0, TROWS), :], blocks[2 * n + 1][pl.ds(0, TROWS), :]
        )
        full[n, pl.ds(0, TROWS), :] = first
        full[n, pl.ds(TROWS, TROWS), :] = second
        at = n * TRAVEL
        for (c, place, many), (d, spot, count) in zip(TO_EAST, TO_WEST):
            right[pl.ds(at, many), :] = full[n, pl.ds(8 * place + 1 - c, many, stride=8), :]
            left[pl.ds(at, count), :] = full[n, pl.ds(8 * spot + 2 + d, count, stride=8), :]
            at += many
        slot = 4 - 4 * gy if slots[n] is None else slots[n]
        at = 0
        for c, place, many in DECK:
            top, bottom = apart(full[n, pl.ds(8 * place + c, many, stride=8), :])
            deck[pl.ds(8 * at + slot, many, stride=8), :] = top
            deck[pl.ds(8 * at + slot + 1, many, stride=8), :] = bottom
            at += many

    def deck_at(row):
        return deck[pl.ds(8 * row, 8), :]

    def read(c, f):
        return deck_at(DECK_AT[4 + c] + PLACE[f])

    keep = [1.0 - (1.0 - read(c, MASK)) * lam_at(lam, 6 + c, 8) for c in range(3)]
    row = lax.broadcasted_iota(jnp.int32, (8, 128), 0) + 2 * gy - 2
    _, g = strip(lambda c, i: read(c, i) * keep[c], row, total_y, at_outlet(lam, 8))
    fields = list(sums(g)) + [read(c, MASK) for c in range(3)] + [read(1, 20 + k) for k in range(4)]
    params = [deck_at(36 + k) for k in range(4)]
    if not swap:
        for n, v in enumerate(fields + params):
            plane[pl.ds(8 * n, 8), :] = v
        return

    def settle(v):
        return jnp.where(gy == 0, pltpu.roll(v, 6, 0), v)

    for n, v in enumerate(params):
        gains[pl.ds(8 * n, 8), :] = settle(v)
    fields = [settle(v) for v in fields] + [jnp.zeros((8, 128), jnp.float32)]
    low, upper = lanes((8, 128)) < SPAN, lax.broadcasted_iota(jnp.int32, (8, 128), 0) < 4
    for n in range(3):
        a, b, c, d = fields[4 * n : 4 * n + 4]
        lower = pltpu.roll(jnp.where(low, c, d), 4, 0)
        plane[pl.ds(8 * n, 8), :] = jnp.where(upper, jnp.where(low, a, b), lower)
    tail = right.shape[0] - 24
    right[pl.ds(tail, 24), :] = plane[...]
    left[pl.ds(tail, 24), :] = plane[...]


def strips_kernel(slots, swap, total_y, total_x, lam, full, west, east, plane, gains, out, side, shelf):
    gx, gy = lax.axis_index("gx"), lax.axis_index("gy")
    last_x = total_x // COLS - 1
    deep = max(8, total_y)
    if swap:
        side[...] = jnp.zeros_like(side)
        shelf[...] = jnp.zeros_like(shelf)

    def lay(s, c, first, place, v):
        top, bottom = apart(v)
        many = v.shape[0]
        side[s, c, pl.ds(8 * place + first, many, stride=8), :] = top
        side[s, c, pl.ds(8 * place + first + 1, many, stride=8), :] = bottom

    for n, slot in enumerate(slots):
        slot = 4 - 4 * gy if slot is None else slot
        lay(0, 2, slot, 0, full[n, pl.ds(2, SIDE, stride=8), :])
        lay(1, 0, slot, 0, full[n, pl.ds(1, SIDE, stride=8), :])
        at = n * TRAVEL
        for (c, place, many), (d, spot, count) in zip(TO_EAST, TO_WEST):
            lay(0, 1 - c, slot, place, west[pl.ds(at, many), :])
            lay(1, 1 + d, slot, spot, east[pl.ds(at, count), :])
            at += many

    if swap:
        fields = []
        low = lanes((8, 128)) < SPAN
        for n in range(3):
            v = plane[pl.ds(8 * n, 8), :]
            for w in (v, pltpu.roll(v, 4, 0)):
                turned = pltpu.roll(w, SPAN, 1)
                fields += [jnp.where(low, w, turned), jnp.where(low, turned, w)]
        which, ratio, mean_gain, fluct_gain = (gains[pl.ds(8 * k, 8), :] for k in range(4))
    else:
        fields = [plane[pl.ds(deep * n, deep), :] for n in range(SUMS + 4)]
        which, ratio, mean_gain, fluct_gain = fields[SUMS:]

    def target(fields):
        def blend(v):
            low, high = v[0:1], v[1:2]
            low = jnp.broadcast_to(low, v.shape)
            high = jnp.broadcast_to(high, v.shape)
            for r in range(1, total_y - 1):
                chosen = which == float(r)
                low = jnp.where(chosen, jnp.broadcast_to(v[r : r + 1], v.shape), low)
                high = jnp.where(chosen, jnp.broadcast_to(v[r + 1 : r + 2], v.shape), high)
            return (1.0 - ratio) * low + ratio * high

        result = [blend(fields[0])]
        for v in fields[1:]:
            mean = jnp.sum(v, axis=1, keepdims=True) * (1.0 / 128.0)
            mean = blend(jnp.broadcast_to(mean, v.shape))
            result.append(mean_gain * mean + fluct_gain * (blend(v) - mean))
        return result

    def local(fields):
        got = []
        for k, v in enumerate(fields):
            shelf[k, pl.ds(8, deep), :] = v
            got.append(shelf[k, pl.ds(6 + 2 * gy, 8), :])
        return got

    target0 = target(fields[7:11])
    teq0 = equilibria(*target0)
    gates = [(1.0 - fields[4 + c]) * lam_at(lam, 6 + c, deep) for c in range(3)]
    row = lax.broadcasted_iota(jnp.int32, (deep, 128), 0)
    _, g = strip(lambda c, i: gates[c] * teq0[i], row, total_y, at_outlet(lam, deep))
    total = [a + b for a, b in zip(sums(g), fields[:4])]
    target1 = target(list(velocity(*total)))
    near0, near1 = local(target0), local(target1)
    goal0, goal1 = equilibria(*near0), equilibria(*near1)

    row = lax.broadcasted_iota(jnp.int32, (8, 128), 0) + 2 * gy - 2
    first, second = [], []
    for s, wanted in ((0, EAST), (1, WEST)):

        def read(c, f):
            return side[s, c, pl.ds(PLACE[f] * 8, 8), :]

        gate = [(1.0 - read(c, MASK)) * lam_at(lam, 3 * s + c, 8) for c in range(3)]

        def value(c, i):
            v = read(c, i)
            return v + gate[c] * (goal0[i] - v)

        middle, g = strip(value, row, total_y, None)
        eq = equilibria(*moments(g), wanted)
        wall = read(1, MASK) == 1.0
        for i in wanted:
            loose = g[i] - relax_rate * (g[i] - eq[i])
            v = jnp.where(wall, g[opposite[i]], loose)
            a, b = shifted(middle(i), i), shifted(v + gate[1] * (goal1[i] - v), i)
            if s == 0:
                a, b = jnp.where(gx == 0, goal0[i], a), jnp.where(gx == 0, goal1[i], b)
            else:
                a = jnp.where(gx == last_x, value(0, i), a)
            first.append(a)
            second.append(b)
    blank = [jnp.zeros((16, 128), jnp.float32)]
    for n, rows in enumerate((first + near0 + blank, second + near1 + blank)):
        turned = pltpu.roll(jnp.concatenate(rows, axis=0), 2, 1).T
        out[pl.ds(48 * n, 48), :] = turned[:48]


def steps_kernel(ways, total_y, total_x, lam, relaxed, zmsg, cols, *rest):
    count = len(ways)
    bulk, small, small_other = rest[:count], rest[count : 2 * count], rest[2 * count : 3 * count]
    result, early, late, out, sem = rest[3 * count :]
    gx, gy = lax.axis_index("gx"), lax.axis_index("gy")
    at_end = gx == total_x // COLS - 1
    bottom, top = gy == 0, gy == total_y // ROWS - 1
    lane = lanes((8, 128))
    at_first, at_last = lane == 0, lane == COLS - 1
    zone = jnp.broadcast_to(lam[0:1, :], (8, 128))

    def column(step, index, at):
        return jnp.broadcast_to(cols[pl.ds(48 * step + at, 8), index : index + 1], (8, 128))

    def goals(step, slot, at, wanted):
        return equilibria(*(column(step, 80 + 8 * k + slot, at) for k in range(4)), wanted)

    def finish(slot, fields):
        for chunk in range(5):
            rows = pl.ds(8 * chunk, 8)
            gate = (1.0 - early[MASK, slot, rows, :]) * zone
            goal = goals(0, slot, 8 * chunk, fields)
            for i in fields:
                v = early[i, slot, rows, :]
                early[i, slot, rows, :] = v + gate * (goal[i] - v)

    def pull(ref, slot, lead, step, at, lift, mine):
        r = at - lift
        g = []
        for i in range(19):
            cx, cy, cz = lattice_vel[i]
            v = ref[i, slot - cy - lead, pl.ds(r - cz, 8), :]
            if cx == 1:
                edge = column(step, EAST.index(i) * 8 + slot, at)
                v = jnp.where(at_first, edge, pltpu.roll(v, 1, 1))
            if cx == -1:
                edge = column(step, 40 + WEST.index(i) * 8 + slot, at)
                if step == 1:
                    edge = jnp.where(at_end, ref[i, slot - lead, pl.ds(r, 8), :], edge)
                v = jnp.where(at_last, edge, pltpu.roll(v, COLS - 1, 1))
            if mine and cy == 1 and slot == 2:
                v = jnp.where(bottom, ref[opposite[i], slot - lead, pl.ds(r, 8), :], v)
            if mine and cy == -1 and slot == 3:
                v = jnp.where(top, ref[mirror_pop[i], slot - lead, pl.ds(r, 8), :], v)
            g.append(v)
        return g

    def collide(slot, wanted, mine):
        for chunk in range(5):
            at = 1 + 8 * chunk
            g = pull(early, slot, 0, 0, at, 0, mine)
            density, vx, vy, vz = moments(g)
            eq = equilibria(density, vx, vy, vz, wanted)
            goal = goals(1, slot, at, wanted)
            solid = early[MASK, slot, pl.ds(at, 8), :]
            gate = (1.0 - solid) * zone
            wall = solid == 1.0
            for i in wanted:
                loose = g[i] - relax_rate * (g[i] - eq[i])
                v = jnp.where(wall, g[opposite[i]], loose)
                late[i, slot - 1, pl.ds(8 * chunk, 8), :] = v + gate * (goal[i] - v)

    for f in range(20):
        for y in range(ROWS):
            slot = 2 + y
            at = TROWS + (f * 2 + y) * EDGE
            early[f, slot, pl.ds(2, DEPTH), :] = relaxed[f, y, :, :]
            early[f, slot, pl.ds(DEPTH + 2, 2), :] = zmsg[pl.ds(at, 2), :]
            early[f, slot, pl.ds(0, 2), :] = zmsg[pl.ds(at + 2, 2), :]
    for slot in (2, 3):
        finish(slot, range(19))

    def beside(n, came_up):
        near_slot, far_slot = (1, 0) if came_up else (4, 5)
        for k, (f, near) in enumerate(up_down(came_up)):
            slot = near_slot if near else far_slot
            at = TROWS + k * EDGE
            early[f, slot, pl.ds(0, 2), :] = small_other[n][pl.ds(at + 2, 2), :]
            early[f, slot, pl.ds(2, 2), :] = small[n][pl.ds(at, 2), :]
            early[f, slot, pl.ds(4, INNER), :] = bulk[n][pl.ds(k * INNER, INNER), :]
            early[f, slot, pl.ds(DEPTH, 2), :] = small[n][pl.ds(at + 2, 2), :]
            early[f, slot, pl.ds(DEPTH + 2, 2), :] = small_other[n][pl.ds(at, 2), :]
        moving = UP if came_up else DOWN
        finish(near_slot, FLAT_Y + moving)
        finish(far_slot, moving)
        collide(near_slot, moving, False)

    for n, way in enumerate(ways):
        if way is not False:

            @pl.when(jnp.logical_not(bottom))
            def _():
                beside(n, True)

        if way is not True:

            @pl.when(jnp.logical_not(top))
            def _():
                beside(n, False)

    for slot in (2, 3):
        collide(slot, range(19), True)
    stores = []
    for chunk in range(DEPTH // 8):
        for y in range(ROWS):
            g = pull(late, 2 + y, 1, 1, 2 + 8 * chunk, 1, True)
            for i in range(19):
                out[i, pl.ds(16 * chunk + y, 8, stride=2), :] = g[i]
        rows = pl.ds(16 * chunk, 16)
        stores.append(pltpu.make_async_copy(out.at[:, rows, :], result.at[:, rows, :], sem.at[chunk]))
        stores[-1].start()
    for copy in stores:
        copy.wait()


def call(kernel, outs, scratch, limit, *args, held=False, leave=False):
    near = pl.BlockSpec(memory_space=pltpu.VMEM)
    far = pl.BlockSpec(memory_space=pltpu.HBM)
    inputs = [near] * len(args)
    if held:
        inputs = [pl.BlockSpec(memory_space=pltpu.SMEM)] + [far] * (len(args) - 1)
        args = [args[0]] + [pltpu.with_memory_space_constraint(v, pltpu.HBM) for v in args[1:]]
    return pl.pallas_call(
        kernel,
        out_shape=[jax.ShapeDtypeStruct(s, jnp.float32) for s in outs],
        in_specs=inputs,
        out_specs=[far if leave else near] * len(outs),
        scratch_shapes=[pltpu.VMEM(s, jnp.float32) if isinstance(s, tuple) else s for s in scratch],
        compiler_params=pltpu.CompilerParams(vmem_limit_bytes=limit << 20),
    )(*args)


def ring(count, step):
    return [(i, (i + step) % count) for i in range(count)]


def body(populations, solid_mask, recycle_plane, fringe_bounds, interp_rows, interp_weights, mean_scale, fluct_scale):
    size_x, size_y = lax.axis_size("gx"), lax.axis_size("gy")
    total_x, total_y = COLS * size_x, ROWS * size_y
    swap = size_y == 2
    ways = (None,) if swap else (True, False)
    slots = (2,) + ((None,) if swap else (0, 4))
    pairs = len(slots)
    pops = populations.reshape(19, DEPTH * ROWS, COLS)
    solid = solid_mask.reshape(DEPTH * ROWS, COLS)

    made = call(
        functools.partial(relax_kernel, ways, total_x),
        [(20, ROWS, DEPTH, COLS), (8, 128), (TROWS + 40 * EDGE, 128)] + [(TROWS + 88, 128)] * len(ways) + [(592, 128)] * len(ways),
        [
            (128, 128),
            pops.shape,
            pltpu.VMEM(solid.shape, jnp.int32),
            pltpu.SMEM((2,), jnp.int32),
            pltpu.SMEM((ROWS,), jnp.int32),
            pltpu.SMEM((ROWS,), jnp.float32),
            pltpu.SMEM((ROWS,), jnp.float32),
            pltpu.SMEM((ROWS,), jnp.float32),
            pltpu.SemaphoreType.DMA((2 * PIECES + 5,)),
        ],
        8,
        recycle_plane,
        pops,
        solid,
        fringe_bounds,
        interp_rows,
        interp_weights,
        mean_scale,
        fluct_scale,
        held=True,
    )
    relaxed, lam, z_out = made[:3]
    small_out, bulk_out = made[3 : 3 + len(ways)], made[3 + len(ways) :]

    def across(v, way):
        if way is None:
            return lax.ppermute(v, "gy", ring(2, 1))
        step = 1 if way else -1
        return lax.ppermute(v, "gy", [(i, i + step) for i in range(size_y) if 0 <= i + step < size_y])

    small = [across(v, way) for v, way in zip(small_out, ways)]
    bulk = [across(v, way) for v, way in zip(bulk_out, ways)]
    z_in = lax.ppermute(z_out, "gz", ring(2, 1))
    small_other = [lax.ppermute(v, "gz", ring(2, 1)) for v in small]

    blocks = [z_out, z_in]
    for a, b in zip(small, small_other):
        blocks += [a, b]
    edge_rows = 72
    full, right, left, plane, gains = call(
        functools.partial(cross_kernel, slots, swap, total_y),
        [(pairs, 2 * TROWS, 128), (edge_rows, 128), (edge_rows, 128), (24 if swap else 8 * (SUMS + 4), 128), (32, 128)],
        [(8 * DECK_ROWS, 128)],
        4,
        lam,
        *blocks,
    )
    west = lax.ppermute(right, "gx", ring(size_x, 1))
    east = lax.ppermute(left, "gx", ring(size_x, -1))
    if swap and size_x == 4:
        far = lax.ppermute(plane, "gx", ring(4, 2))
        plane = plane + far + west[edge_rows - 24 :] + east[edge_rows - 24 :]
    elif swap:
        plane = lax.psum(plane, "gx")
    else:
        own = plane.reshape(SUMS + 4, 8, 128)[:, 2:4]
        first = (lax.axis_index("gx") == 0) | (jnp.arange(SUMS + 4) < SUMS)
        own = jnp.where(first[:, None, None], own, 0.0)
        whole = lax.dynamic_update_slice(
            jnp.zeros((SUMS + 4, total_y, 128), jnp.float32), own, (0, 2 * lax.axis_index("gy"), 0)
        )
        plane = lax.psum(whole, ("gx", "gy")).reshape((SUMS + 4) * total_y, 128)

    (cols,) = call(
        functools.partial(strips_kernel, slots, swap, total_y, total_x),
        [(96, 128)],
        [(2, 3, SIDE * 8, 128), (4, 16 + max(8, total_y), 128)],
        8,
        lam,
        full,
        west,
        east,
        plane,
        gains,
    )
    (out,) = call(
        functools.partial(steps_kernel, ways, total_y, total_x),
        [(19, DEPTH * ROWS, COLS)],
        [(20, 6, 48, 128), (19, 4, 48, 128), (19, DEPTH * ROWS, COLS), pltpu.SemaphoreType.DMA((DEPTH // 8,))],
        12,
        lam,
        relaxed,
        z_in,
        cols,
        *bulk,
        *small,
        *small_other,
        leave=True,
    )
    return out.reshape(populations.shape)


def solution(mesh):
    placed = (
        P(None, ("parts", "gz"), "gy", "gx"),
        P(("parts", "gz"), "gy", "gx"),
        P(),
        P(),
        P("gy"),
        P("gy"),
        P("gy"),
        P("gy"),
    )
    return jax.shard_map(
        body,
        mesh=mesh,
        in_specs=placed,
        out_specs=P(None, ("parts", "gz"), "gy", "gx"),
        check_vma=False,
    )
```

```python
import functools
import math

import jax
import jax.numpy as jnp
from jax import lax
from jax.experimental import pallas as pl
from jax.experimental.pallas import tpu as pltpu
from jax.sharding import PartitionSpec as P

lattice_vel = (
    (0, 0, 0),
    (1, 0, 0),
    (-1, 0, 0),
    (0, 1, 0),
    (0, -1, 0),
    (0, 0, 1),
    (0, 0, -1),
    (1, 1, 0),
    (-1, -1, 0),
    (1, -1, 0),
    (-1, 1, 0),
    (1, 0, 1),
    (-1, 0, -1),
    (1, 0, -1),
    (-1, 0, 1),
    (0, 1, 1),
    (0, -1, -1),
    (0, 1, -1),
    (0, -1, 1),
)
lattice_weight = (1.0 / 3.0,) + (1.0 / 18.0,) * 6 + (1.0 / 36.0,) * 12
opposite = (0, 2, 1, 4, 3, 6, 5, 8, 7, 10, 9, 12, 11, 14, 13, 16, 15, 18, 17)
mirror_pop = (0, 1, 2, 4, 3, 5, 6, 9, 10, 7, 8, 11, 12, 13, 14, 18, 17, 16, 15)
relax_rate = 1.25
fringe_peak = 0.8

DEPTH, ROWS, COLS = 32, 2, 128
SPAN = 2 * DEPTH
MASK = 19
EAST = (1, 11, 13, 7, 9)
WEST = (8, 10, 2, 12, 14)
FLAT_X = tuple(i for i in range(19) if lattice_vel[i][0] == 0)
UP = tuple(i for i in range(19) if lattice_vel[i][1] == 1)
DOWN = tuple(i for i in range(19) if lattice_vel[i][1] == -1)
FLAT_Y = tuple(i for i in range(19) if lattice_vel[i][1] == 0)

COLUMN = EAST + (MASK,) + WEST + FLAT_X + (20, 21, 22, 23)
PLACE = {field: at for at, field in enumerate(COLUMN)}
HALF = len(COLUMN) // 2
TROWS = HALF * 8
SIDE = 20
TO_EAST = ((0, 0, 8), (0, 11, 9), (1, 0, 6))
TO_WEST = ((0, 3, 8), (0, 11, 9), (1, 5, 6))
TRAVEL = 23
DECK = ((4, 0, 6), (5, 0, 24), (6, 5, 6), (7, 0, 4))
DECK_AT = {4: 0, 5: 6, 6: 30 - 5, 7: 36}
DECK_ROWS = 40
SUMS = 11
EDGE = 4
BLOCK_AT = 88
SUMS_AT = BLOCK_AT + 12 * DEPTH
BULK = 656
PIECES = 2


def up_down(rows_up):
    moving = UP if rows_up else DOWN
    near = FLAT_Y + moving + (MASK,)
    far = moving + (MASK,)
    return [(f, True) for f in near] + [(f, False) for f in far]


def sums(g):
    w0, w1, w2 = lattice_weight[0], lattice_weight[1], lattice_weight[7]
    axis = g[1] + g[2] + g[3] + g[4] + g[5] + g[6]
    diag = (g[7] + g[8] + g[9] + g[10]) + (g[11] + g[12] + g[13] + g[14]) + (g[15] + g[16] + g[17] + g[18])
    density = w0 * g[0] + w1 * axis + w2 * diag
    d78, d910 = g[7] - g[8], g[9] - g[10]
    d1112, d1314 = g[11] - g[12], g[13] - g[14]
    d1516, d1718 = g[15] - g[16], g[17] - g[18]
    mx = w1 * (g[1] - g[2]) + w2 * ((d78 + d910) + (d1112 + d1314))
    my = w1 * (g[3] - g[4]) + w2 * ((d78 - d910) + (d1516 + d1718))
    mz = w1 * (g[5] - g[6]) + w2 * ((d1112 - d1314) + (d1516 - d1718))
    return density, mx, my, mz


def velocity(density, mx, my, mz):
    inverse = 1.0 / density
    return density, mx * inverse, my * inverse, mz * inverse


def moments(g):
    return velocity(*sums(g))


def equilibria(density, vx, vy, vz, wanted=range(19)):
    base = density - 1.5 * density * (vx * vx + vy * vy + vz * vz)
    linear = 3.0 * density
    square = 4.5 * density
    out = {}
    for i in wanted:
        if i in out:
            continue
        if i == 0:
            out[0] = base
            continue
        first = i if i % 2 == 1 else i - 1
        cx, cy, cz = lattice_vel[first]
        p = None
        for c, v in ((cx, vx), (cy, vy), (cz, vz)):
            if c == 0:
                continue
            p = (v if c == 1 else -v) if p is None else (p + v if c == 1 else p - v)
        even = base + square * p * p
        odd = linear * p
        out[first] = even + odd
        out[first + 1] = even - odd
    return out


def lanes(shape):
    return lax.broadcasted_iota(jnp.int32, shape, len(shape) - 1)


def ramp(x, start, finish):
    width = (finish - start).astype(jnp.float32)
    angle = math.pi * ((x - start).astype(jnp.float32) + 0.5) / width
    inside = (x >= start) & (x < finish)
    return jnp.where(inside, fringe_peak * jnp.sin(angle) ** 2, 0.0)


def relax_kernel(total_x, *refs):
    recycle, pops_in, solid_in = refs[:3]
    small_in = refs[3:8]
    relaxed, lam, columns, zmsg = refs[8:12]
    grid, pops, solid = refs[12:15]
    small, sem = refs[15:-1], refs[-1]
    loads = [
        [pltpu.make_async_copy(a.at[..., rows, :], b.at[..., rows, :], sem.at[2 * n + m]) for m, (a, b) in enumerate(((pops_in, pops), (solid_in, solid)))]
        for n, rows in enumerate(pl.ds(n * 2 * DEPTH // PIECES, 2 * DEPTH // PIECES) for n in range(PIECES))
    ]
    pieces = DEPTH // 8
    scalars = [pltpu.make_async_copy(a, b, sem.at[2 * PIECES + n]) for n, (a, b) in enumerate(zip(small_in, small))]
    for copy in loads[0] + scalars:
        copy.start()
    for load in loads[1:]:
        for copy in load:
            copy.start()
    for copy in scalars:
        copy.wait()
    bounds, rows_in, weights_in, mean_in, fluct_in = small
    gx, rp = lax.axis_index("gx"), recycle[0]
    x0 = gx * COLS
    off = rp - x0
    lane = lanes((8, 128))
    sub = lax.broadcasted_iota(jnp.int32, (8, 128), 0)
    special = jnp.where(
        lane < 3, x0 - 2 + lane, jnp.where(lane < 6, x0 + COLS - 4 + lane, rp - 7 + lane)
    )
    shares = ramp(jnp.where(sub == 0, x0 + lane, special), bounds[0], bounds[1])
    lam[...] = jnp.where(sub < 2, shares, jnp.where(rp == total_x - 1, 1.0, 0.0))

    col = lane % 8
    slot = lane // 8
    place = off + col - 5
    here = (place >= 0) & (place < COLS) & (col >= 4) & (col < 7)
    static = col < 4
    shift0 = 5 - off + 8 * 128 * 64
    extras = []
    for y in range(ROWS):
        values = jnp.zeros((8, 128), jnp.float32)
        for k, v in enumerate((rows_in[y].astype(jnp.float32), weights_in[y], mean_in[y], fluct_in[y])):
            values = jnp.where((slot == k) & (col == 7), v, values)
        extras.append(values)
    for chunk in range(pieces):
        if chunk % (pieces // PIECES) == 0:
            for copy in loads[chunk // (pieces // PIECES)]:
                copy.wait()
        for y in range(ROWS):
            rows = pl.ds(16 * chunk + y, 8, stride=2)
            g = [pops[i, rows, :] for i in range(19)]
            wall = solid[rows, :] == 1
            density, vx, vy, vz = moments(g)
            eq = equilibria(density, vx, vy, vz)
            field = {}
            for i in range(19):
                loose = g[i] - relax_rate * (g[i] - eq[i])
                field[i] = jnp.where(wall, g[opposite[i]], loose)
            field[MASK] = jnp.where(wall, 1.0, 0.0)
            field[20], field[21], field[22], field[23] = density, vx, vy, vz
            here_z = pl.ds(8 * chunk, 8)
            for f in range(20):
                relaxed[f, y, here_z, :] = field[f]
            for half in range(2):
                fixed = jnp.zeros((8, 128), jnp.float32)
                moving = jnp.zeros((8, 128), jnp.float32)
                for k in range(HALF):
                    v = field[COLUMN[half * HALF + k]]
                    mine = slot == k
                    if half * HALF + k < SIDE:
                        fixed = jnp.where(mine, pltpu.roll(v, 2 + 8 * k, 1), fixed)
                    moving = jnp.where(mine, pltpu.roll(v, (shift0 + 8 * k) % 128, 1), moving)
                rest_of = extras[y] if half == 0 else jnp.zeros((8, 128), jnp.float32)
                packed = jnp.where(static, fixed, jnp.where(here, moving, rest_of))
                grid[pl.ds((y * 2 + half) * DEPTH + 8 * chunk, 8), :] = packed
    columns[...] = grid[...].T[:TROWS]
    zmsg[pl.ds(0, TROWS), :] = columns[...]
    for f in range(20):
        for y in range(ROWS):
            at = TROWS + (f * 2 + y) * EDGE
            zmsg[pl.ds(at, 2), :] = relaxed[f, y, pl.ds(0, 2), :]
            zmsg[pl.ds(at + 2, 2), :] = relaxed[f, y, pl.ds(DEPTH - 2, 2), :]


def pack_kernel(ways, relaxed, lam, z_in, *rest):
    bulk, inside = rest[:-1], rest[-1]
    lane = lanes((8, 128))
    zone = jnp.broadcast_to(lam[0:1, :], (8, 128))
    zero = jnp.zeros((8, 128), jnp.float32)

    def pack(way, to):
        inner = 0
        for n, (f, near) in enumerate(up_down(way)):
            y = 1 if near == way else 0
            to[pl.ds(n * EDGE, EDGE), :] = z_in[pl.ds(TROWS + (f * 2 + y) * EDGE, EDGE), :]
            if f not in FLAT_Y:
                to[pl.ds(BLOCK_AT + inner * DEPTH, DEPTH), :] = relaxed[f, y, :, :]
                inner += 1
        y = 1 if way else 0
        for chunk in range(DEPTH // 8):
            rows = pl.ds(8 * chunk, 8)
            keep = 1.0 - (1.0 - relaxed[MASK, y, rows, :]) * zone
            for n, i in enumerate(FLAT_Y):
                inside[n, pl.ds(8 + 8 * chunk, 8), :] = relaxed[i, y, rows, :] * keep
        for n in range(len(FLAT_Y)):
            inside[n, pl.ds(0, 8), :] = zero
            inside[n, pl.ds(8 + DEPTH, 16), :] = jnp.zeros((16, 128), jnp.float32)
        for chunk in range(5):
            g = {}
            for n, i in enumerate(FLAT_Y):
                cx, _, cz = lattice_vel[i]
                v = inside[n, pl.ds(7 + 8 * chunk - cz, 8), :]
                if cx == 1:
                    v = jnp.where(lane == 0, 0.0, pltpu.roll(v, 1, 1))
                if cx == -1:
                    v = jnp.where(lane == COLS - 1, 0.0, pltpu.roll(v, COLS - 1, 1))
                g[i] = v
            w0, w1, w2 = lattice_weight[0], lattice_weight[1], lattice_weight[7]
            d12, d56 = g[1] - g[2], g[5] - g[6]
            d1112, d1314 = g[11] - g[12], g[13] - g[14]
            totals = (
                w0 * g[0] + w1 * ((g[1] + g[2]) + (g[5] + g[6])) + w2 * ((g[11] + g[12]) + (g[13] + g[14])),
                w1 * d12 + w2 * (d1112 + d1314),
                w1 * d56 + w2 * (d1112 - d1314),
            )
            many = min(8, DEPTH + 2 - 8 * chunk)
            for n, v in enumerate(totals):
                to[pl.ds(SUMS_AT + n * (DEPTH + 2) + 8 * chunk, many), :] = v[:many]

    for at, way in enumerate(ways):
        if way is None:
            gy = lax.axis_index("gy")

            @pl.when(gy == 0)
            def _():
                pack(True, bulk[at])

            @pl.when(gy != 0)
            def _():
                pack(False, bulk[at])

        else:
            pack(way, bulk[at])


def join(mine, other):
    even = (lanes(mine.shape) // DEPTH) % 2 == 0
    first = jnp.where(even, mine, pltpu.roll(other, DEPTH, 1))
    second = jnp.where(even, pltpu.roll(mine, 128 - DEPTH, 1), other)
    return first, second


def apart(v):
    low = lanes(v.shape) < SPAN
    turned = pltpu.roll(v, SPAN, 1)
    return jnp.where(low, v, turned), jnp.where(low, turned, v)


def shifted(v, i):
    _, cy, cz = lattice_vel[i]
    if cz:
        v = pltpu.roll(v, cz % 128, 1)
    if cy:
        v = pltpu.roll(v, cy % v.shape[0], 0)
    return v


def strip(value, row, total_y, edge):
    held = {}

    def middle(i):
        if i not in held:
            held[i] = value(1, i)
        return held[i]

    bottom, top = row == 0, row == total_y - 1
    g = []
    for i in range(19):
        cx, cy, _ = lattice_vel[i]
        v = shifted(middle(i) if cx == 0 else value(1 - cx, i), i)
        if cx == -1 and edge is not None:
            v = jnp.where(edge, middle(i), v)
        if cy == 1:
            v = jnp.where(bottom, middle(opposite[i]), v)
        if cy == -1:
            v = jnp.where(top, middle(mirror_pop[i]), v)
        g.append(v)
    return middle, g


def lam_at(lam, c, rows):
    return jnp.broadcast_to(lam[1:2, c : c + 1], (rows, 128))


def at_outlet(lam, rows):
    return jnp.broadcast_to(lam[2:3, 0:1], (rows, 128)) == 1.0


def cross_kernel(slots, swap, total_y, lam, *refs):
    pairs = len(slots)
    blocks = refs[: 2 * pairs]
    full, right, left, plane, gains, deck = refs[2 * pairs :]
    gy = lax.axis_index("gy")
    if swap:
        deck[...] = jnp.zeros_like(deck)
    for n in range(pairs):
        first, second = join(
            blocks[2 * n][pl.ds(0, TROWS), :], blocks[2 * n + 1][pl.ds(0, TROWS), :]
        )
        full[n, pl.ds(0, TROWS), :] = first
        full[n, pl.ds(TROWS, TROWS), :] = second
        at = n * TRAVEL
        for (c, place, many), (d, spot, count) in zip(TO_EAST, TO_WEST):
            right[pl.ds(at, many), :] = full[n, pl.ds(8 * place + 1 - c, many, stride=8), :]
            left[pl.ds(at, count), :] = full[n, pl.ds(8 * spot + 2 + d, count, stride=8), :]
            at += many
        slot = 4 - 4 * gy if slots[n] is None else slots[n]
        at = 0
        for c, place, many in DECK:
            top, bottom = apart(full[n, pl.ds(8 * place + c, many, stride=8), :])
            deck[pl.ds(8 * at + slot, many, stride=8), :] = top
            deck[pl.ds(8 * at + slot + 1, many, stride=8), :] = bottom
            at += many

    def deck_at(row):
        return deck[pl.ds(8 * row, 8), :]

    def read(c, f):
        return deck_at(DECK_AT[4 + c] + PLACE[f])

    keep = [1.0 - (1.0 - read(c, MASK)) * lam_at(lam, 6 + c, 8) for c in range(3)]
    row = lax.broadcasted_iota(jnp.int32, (8, 128), 0) + 2 * gy - 2
    _, g = strip(lambda c, i: read(c, i) * keep[c], row, total_y, at_outlet(lam, 8))
    fields = list(sums(g)) + [read(c, MASK) for c in range(3)] + [read(1, 20 + k) for k in range(4)]
    params = [deck_at(36 + k) for k in range(4)]
    if not swap:
        for n, v in enumerate(fields + params):
            plane[pl.ds(8 * n, 8), :] = v
        return

    def settle(v):
        return jnp.where(gy == 0, pltpu.roll(v, 6, 0), v)

    for n, v in enumerate(params):
        gains[pl.ds(8 * n, 8), :] = settle(v)
    fields = [settle(v) for v in fields] + [jnp.zeros((8, 128), jnp.float32)]
    low, upper = lanes((8, 128)) < SPAN, lax.broadcasted_iota(jnp.int32, (8, 128), 0) < 4
    for n in range(3):
        a, b, c, d = fields[4 * n : 4 * n + 4]
        lower = pltpu.roll(jnp.where(low, c, d), 4, 0)
        plane[pl.ds(8 * n, 8), :] = jnp.where(upper, jnp.where(low, a, b), lower)
    tail = right.shape[0] - 24
    right[pl.ds(tail, 24), :] = plane[...]
    left[pl.ds(tail, 24), :] = plane[...]


def strips_kernel(slots, swap, total_y, total_x, lam, full, west, east, plane, gains, out, side, shelf):
    gx, gy = lax.axis_index("gx"), lax.axis_index("gy")
    last_x = total_x // COLS - 1
    deep = max(8, total_y)
    if swap:
        side[...] = jnp.zeros_like(side)
        shelf[...] = jnp.zeros_like(shelf)

    def lay(s, c, first, place, v):
        top, bottom = apart(v)
        many = v.shape[0]
        side[s, c, pl.ds(8 * place + first, many, stride=8), :] = top
        side[s, c, pl.ds(8 * place + first + 1, many, stride=8), :] = bottom

    for n, slot in enumerate(slots):
        slot = 4 - 4 * gy if slot is None else slot
        lay(0, 2, slot, 0, full[n, pl.ds(2, SIDE, stride=8), :])
        lay(1, 0, slot, 0, full[n, pl.ds(1, SIDE, stride=8), :])
        at = n * TRAVEL
        for (c, place, many), (d, spot, count) in zip(TO_EAST, TO_WEST):
            lay(0, 1 - c, slot, place, west[pl.ds(at, many), :])
            lay(1, 1 + d, slot, spot, east[pl.ds(at, count), :])
            at += many

    if swap:
        fields = []
        low = lanes((8, 128)) < SPAN
        for n in range(3):
            v = plane[pl.ds(8 * n, 8), :]
            for w in (v, pltpu.roll(v, 4, 0)):
                turned = pltpu.roll(w, SPAN, 1)
                fields += [jnp.where(low, w, turned), jnp.where(low, turned, w)]
        which, ratio, mean_gain, fluct_gain = (gains[pl.ds(8 * k, 8), :] for k in range(4))
    else:
        fields = [plane[pl.ds(deep * n, deep), :] for n in range(SUMS + 4)]
        which, ratio, mean_gain, fluct_gain = fields[SUMS:]

    def target(fields):
        def blend(v):
            low, high = v[0:1], v[1:2]
            low = jnp.broadcast_to(low, v.shape)
            high = jnp.broadcast_to(high, v.shape)
            for r in range(1, total_y - 1):
                chosen = which == float(r)
                low = jnp.where(chosen, jnp.broadcast_to(v[r : r + 1], v.shape), low)
                high = jnp.where(chosen, jnp.broadcast_to(v[r + 1 : r + 2], v.shape), high)
            return (1.0 - ratio) * low + ratio * high

        result = [blend(fields[0])]
        for v in fields[1:]:
            mean = jnp.sum(v, axis=1, keepdims=True) * (1.0 / 128.0)
            mean = blend(jnp.broadcast_to(mean, v.shape))
            result.append(mean_gain * mean + fluct_gain * (blend(v) - mean))
        return result

    def local(fields):
        got = []
        for k, v in enumerate(fields):
            shelf[k, pl.ds(8, deep), :] = v
            got.append(shelf[k, pl.ds(6 + 2 * gy, 8), :])
        return got

    target0 = target(fields[7:11])
    teq0 = equilibria(*target0)
    gates = [(1.0 - fields[4 + c]) * lam_at(lam, 6 + c, deep) for c in range(3)]
    row = lax.broadcasted_iota(jnp.int32, (deep, 128), 0)
    _, g = strip(lambda c, i: gates[c] * teq0[i], row, total_y, at_outlet(lam, deep))
    total = [a + b for a, b in zip(sums(g), fields[:4])]
    target1 = target(list(velocity(*total)))
    near0, near1 = local(target0), local(target1)
    goal0, goal1 = equilibria(*near0), equilibria(*near1)

    row = lax.broadcasted_iota(jnp.int32, (8, 128), 0) + 2 * gy - 2
    first, second = [], []
    for s, wanted in ((0, EAST), (1, WEST)):

        def read(c, f):
            return side[s, c, pl.ds(PLACE[f] * 8, 8), :]

        gate = [(1.0 - read(c, MASK)) * lam_at(lam, 3 * s + c, 8) for c in range(3)]

        def value(c, i):
            v = read(c, i)
            return v + gate[c] * (goal0[i] - v)

        middle, g = strip(value, row, total_y, None)
        eq = equilibria(*moments(g), wanted)
        wall = read(1, MASK) == 1.0
        for i in wanted:
            loose = g[i] - relax_rate * (g[i] - eq[i])
            v = jnp.where(wall, g[opposite[i]], loose)
            a, b = shifted(middle(i), i), shifted(v + gate[1] * (goal1[i] - v), i)
            if s == 0:
                a, b = jnp.where(gx == 0, goal0[i], a), jnp.where(gx == 0, goal1[i], b)
            else:
                a = jnp.where(gx == last_x, value(0, i), a)
            first.append(a)
            second.append(b)
    blank = [jnp.zeros((16, 128), jnp.float32)]
    for n, rows in enumerate((first + near0 + blank, second + near1 + blank)):
        turned = pltpu.roll(jnp.concatenate(rows, axis=0), 2, 1).T
        out[pl.ds(48 * n, 48), :] = turned[:48]


def steps_kernel(ways, total_y, total_x, lam, relaxed, zmsg, cols, *rest):
    count = len(ways)
    bulk = rest[:count]
    result, early, late, out, sem = rest[count:]
    gx, gy = lax.axis_index("gx"), lax.axis_index("gy")
    at_end = gx == total_x // COLS - 1
    bottom, top = gy == 0, gy == total_y // ROWS - 1
    lane = lanes((8, 128))
    at_first, at_last = lane == 0, lane == COLS - 1
    zone = jnp.broadcast_to(lam[0:1, :], (8, 128))

    def column(step, index, at):
        return jnp.broadcast_to(cols[pl.ds(48 * step + at, 8), index : index + 1], (8, 128))

    def goals(step, slot, at, wanted):
        return equilibria(*(column(step, 80 + 8 * k + slot, at) for k in range(4)), wanted)

    def finish(slot, fields):
        for chunk in range(5):
            rows = pl.ds(8 * chunk, 8)
            gate = (1.0 - early[MASK, slot, rows, :]) * zone
            goal = goals(0, slot, 8 * chunk, fields)
            for i in fields:
                v = early[i, slot, rows, :]
                early[i, slot, rows, :] = v + gate * (goal[i] - v)

    def pull(ref, slot, lead, step, at, lift, mine):
        r = at - lift
        g = []
        for i in range(19):
            cx, cy, cz = lattice_vel[i]
            v = ref[i, slot - cy - lead, pl.ds(r - cz, 8), :]
            if cx == 1:
                edge = column(step, EAST.index(i) * 8 + slot, at)
                v = jnp.where(at_first, edge, pltpu.roll(v, 1, 1))
            if cx == -1:
                edge = column(step, 40 + WEST.index(i) * 8 + slot, at)
                if step == 1:
                    edge = jnp.where(at_end, ref[i, slot - lead, pl.ds(r, 8), :], edge)
                v = jnp.where(at_last, edge, pltpu.roll(v, COLS - 1, 1))
            if mine and cy == 1 and slot == 2:
                v = jnp.where(bottom, ref[opposite[i], slot - lead, pl.ds(r, 8), :], v)
            if mine and cy == -1 and slot == 3:
                v = jnp.where(top, ref[mirror_pop[i], slot - lead, pl.ds(r, 8), :], v)
            g.append(v)
        return g

    def collide(slot, wanted, chunk, came=None):
        at = 1 + 8 * chunk
        g = pull(early, slot, 0, 0, at, 0, came is None)
        total = sums(g)
        if came is not None:
            density, mx, mz = (came[pl.ds(SUMS_AT + n * (DEPTH + 2) + 8 * chunk, 8), :] for n in range(3))
            total = (total[0] + density, total[1] + mx, total[2], total[3] + mz)
        density, vx, vy, vz = velocity(*total)
        eq = equilibria(density, vx, vy, vz, wanted)
        goal = goals(1, slot, at, wanted)
        solid = early[MASK, slot, pl.ds(at, 8), :]
        gate = (1.0 - solid) * zone
        wall = solid == 1.0
        for i in wanted:
            loose = g[i] - relax_rate * (g[i] - eq[i])
            v = jnp.where(wall, g[opposite[i]], loose)
            late[i, slot - 1, pl.ds(8 * chunk, 8), :] = v + gate * (goal[i] - v)

    for f in range(20):
        for y in range(ROWS):
            slot = 2 + y
            at = TROWS + (f * 2 + y) * EDGE
            early[f, slot, pl.ds(2, DEPTH), :] = relaxed[f, y, :, :]
            early[f, slot, pl.ds(DEPTH + 2, 2), :] = zmsg[pl.ds(at, 2), :]
            early[f, slot, pl.ds(0, 2), :] = zmsg[pl.ds(at + 2, 2), :]
    for slot in (2, 3):
        finish(slot, range(19))

    def beside(n, came_up):
        near_slot, far_slot = (1, 0) if came_up else (4, 5)
        inner = 0
        for k, (f, near) in enumerate(up_down(came_up)):
            slot = near_slot if near else far_slot
            at = k * EDGE
            early[f, slot, pl.ds(0, 2), :] = bulk[n][pl.ds(at + 2, 2), :]
            early[f, slot, pl.ds(DEPTH + 2, 2), :] = bulk[n][pl.ds(at, 2), :]
            if f in FLAT_Y:
                early[f, slot, pl.ds(2, DEPTH), :] = jnp.zeros((DEPTH, 128), jnp.float32)
            else:
                early[f, slot, pl.ds(2, DEPTH), :] = bulk[n][pl.ds(BLOCK_AT + inner * DEPTH, DEPTH), :]
                inner += 1
        moving = UP if came_up else DOWN
        finish(near_slot, FLAT_Y + moving)
        finish(far_slot, moving)
        for chunk in range(5):
            collide(near_slot, moving, chunk, bulk[n])

    for n, way in enumerate(ways):
        if way is not False:

            @pl.when(jnp.logical_not(bottom))
            def _():
                beside(n, True)

        if way is not True:

            @pl.when(jnp.logical_not(top))
            def _():
                beside(n, False)

    stores = []
    for chunk in range(5):
        for slot in (2, 3):
            collide(slot, range(19), chunk)
        if chunk == 0:
            continue
        for y in range(ROWS):
            g = pull(late, 2 + y, 1, 1, 8 * chunk - 6, 1, True)
            for i in range(19):
                out[i, pl.ds(16 * (chunk - 1) + y, 8, stride=2), :] = g[i]
        rows = pl.ds(16 * (chunk - 1), 16)
        stores.append(pltpu.make_async_copy(out.at[:, rows, :], result.at[:, rows, :], sem.at[chunk - 1]))
        stores[-1].start()
    for copy in stores:
        copy.wait()


def call(kernel, outs, scratch, limit, *args, held=False, leave=False):
    near = pl.BlockSpec(memory_space=pltpu.VMEM)
    far = pl.BlockSpec(memory_space=pltpu.HBM)
    inputs = [near] * len(args)
    if held:
        inputs = [pl.BlockSpec(memory_space=pltpu.SMEM)] + [far] * (len(args) - 1)
        args = [args[0]] + [pltpu.with_memory_space_constraint(v, pltpu.HBM) for v in args[1:]]
    return pl.pallas_call(
        kernel,
        out_shape=[jax.ShapeDtypeStruct(s, jnp.float32) for s in outs],
        in_specs=inputs,
        out_specs=[far if leave else near] * len(outs),
        scratch_shapes=[pltpu.VMEM(s, jnp.float32) if isinstance(s, tuple) else s for s in scratch],
        compiler_params=pltpu.CompilerParams(vmem_limit_bytes=limit << 20),
    )(*args)


def ring(count, step):
    return [(i, (i + step) % count) for i in range(count)]


def body(populations, solid_mask, recycle_plane, fringe_bounds, interp_rows, interp_weights, mean_scale, fluct_scale):
    size_x, size_y = lax.axis_size("gx"), lax.axis_size("gy")
    total_x, total_y = COLS * size_x, ROWS * size_y
    swap = size_y == 2
    ways = (None,) if swap else (True, False)
    slots = (2,) + ((None,) if swap else (0, 4))
    pairs = len(slots)
    pops = populations.reshape(19, DEPTH * ROWS, COLS)
    solid = solid_mask.reshape(DEPTH * ROWS, COLS)

    relaxed, lam, columns, z_out = call(
        functools.partial(relax_kernel, total_x),
        [(20, ROWS, DEPTH, COLS), (8, 128), (TROWS, 128), (TROWS + 40 * EDGE, 128)],
        [
            (128, 128),
            pops.shape,
            pltpu.VMEM(solid.shape, jnp.int32),
            pltpu.SMEM((2,), jnp.int32),
            pltpu.SMEM((ROWS,), jnp.int32),
            pltpu.SMEM((ROWS,), jnp.float32),
            pltpu.SMEM((ROWS,), jnp.float32),
            pltpu.SMEM((ROWS,), jnp.float32),
            pltpu.SemaphoreType.DMA((2 * PIECES + 5,)),
        ],
        8,
        recycle_plane,
        pops,
        solid,
        fringe_bounds,
        interp_rows,
        interp_weights,
        mean_scale,
        fluct_scale,
        held=True,
    )
    def across(v, way):
        if way is None:
            return lax.ppermute(v, "gy", ring(2, 1))
        step = 1 if way else -1
        return lax.ppermute(v, "gy", [(i, i + step) for i in range(size_y) if 0 <= i + step < size_y])

    beside = [across(columns, way) for way in ways]
    z_in = lax.ppermute(z_out, "gz", ring(2, 1))
    bulk_out = call(
        functools.partial(pack_kernel, ways),
        [(BULK, 128)] * len(ways),
        [(len(FLAT_Y), DEPTH + 24, 128)],
        4,
        relaxed,
        lam,
        z_in,
    )
    bulk = [across(v, way) for v, way in zip(bulk_out, ways)]
    beside_other = [lax.ppermute(v, "gz", ring(2, 1)) for v in beside]

    blocks = [columns, z_in]
    for a, b in zip(beside, beside_other):
        blocks += [a, b]
    edge_rows = 72
    full, right, left, plane, gains = call(
        functools.partial(cross_kernel, slots, swap, total_y),
        [(pairs, 2 * TROWS, 128), (edge_rows, 128), (edge_rows, 128), (24 if swap else 8 * (SUMS + 4), 128), (32, 128)],
        [(8 * DECK_ROWS, 128)],
        4,
        lam,
        *blocks,
    )
    west = lax.ppermute(right, "gx", ring(size_x, 1))
    east = lax.ppermute(left, "gx", ring(size_x, -1))
    if swap and size_x == 4:
        far = lax.ppermute(plane, "gx", ring(4, 2))
        plane = plane + far + west[edge_rows - 24 :] + east[edge_rows - 24 :]
    elif swap:
        plane = lax.psum(plane, "gx")
    else:
        own = plane.reshape(SUMS + 4, 8, 128)[:, 2:4]
        first = (lax.axis_index("gx") == 0) | (jnp.arange(SUMS + 4) < SUMS)
        own = jnp.where(first[:, None, None], own, 0.0)
        whole = lax.dynamic_update_slice(
            jnp.zeros((SUMS + 4, total_y, 128), jnp.float32), own, (0, 2 * lax.axis_index("gy"), 0)
        )
        plane = lax.psum(whole, ("gx", "gy")).reshape((SUMS + 4) * total_y, 128)

    (cols,) = call(
        functools.partial(strips_kernel, slots, swap, total_y, total_x),
        [(96, 128)],
        [(2, 3, SIDE * 8, 128), (4, 16 + max(8, total_y), 128)],
        8,
        lam,
        full,
        west,
        east,
        plane,
        gains,
    )
    (out,) = call(
        functools.partial(steps_kernel, ways, total_y, total_x),
        [(19, DEPTH * ROWS, COLS)],
        [(20, 6, 48, 128), (19, 4, 48, 128), (19, DEPTH * ROWS, COLS), pltpu.SemaphoreType.DMA((DEPTH // 8,))],
        12,
        lam,
        relaxed,
        z_in,
        cols,
        *bulk,
        leave=True,
    )
    return out.reshape(populations.shape)


def solution(mesh):
    placed = (
        P(None, ("parts", "gz"), "gy", "gx"),
        P(("parts", "gz"), "gy", "gx"),
        P(),
        P(),
        P("gy"),
        P("gy"),
        P("gy"),
        P("gy"),
    )
    return jax.shard_map(
        body,
        mesh=mesh,
        in_specs=placed,
        out_specs=P(None, ("parts", "gz"), "gy", "gx"),
        check_vma=False,
    )
```

```python
import functools
import math

import jax
import jax.numpy as jnp
from jax import lax
from jax.experimental import pallas as pl
from jax.experimental.pallas import tpu as pltpu
from jax.sharding import PartitionSpec as P

lattice_vel = (
    (0, 0, 0),
    (1, 0, 0),
    (-1, 0, 0),
    (0, 1, 0),
    (0, -1, 0),
    (0, 0, 1),
    (0, 0, -1),
    (1, 1, 0),
    (-1, -1, 0),
    (1, -1, 0),
    (-1, 1, 0),
    (1, 0, 1),
    (-1, 0, -1),
    (1, 0, -1),
    (-1, 0, 1),
    (0, 1, 1),
    (0, -1, -1),
    (0, 1, -1),
    (0, -1, 1),
)
lattice_weight = (1.0 / 3.0,) + (1.0 / 18.0,) * 6 + (1.0 / 36.0,) * 12
opposite = (0, 2, 1, 4, 3, 6, 5, 8, 7, 10, 9, 12, 11, 14, 13, 16, 15, 18, 17)
mirror_pop = (0, 1, 2, 4, 3, 5, 6, 9, 10, 7, 8, 11, 12, 13, 14, 18, 17, 16, 15)
relax_rate = 1.25
fringe_peak = 0.8

DEPTH, ROWS, COLS = 32, 2, 128
SPAN = 2 * DEPTH
MASK = 19
EAST = (1, 11, 13, 7, 9)
WEST = (8, 10, 2, 12, 14)
FLAT_X = tuple(i for i in range(19) if lattice_vel[i][0] == 0)
UP = tuple(i for i in range(19) if lattice_vel[i][1] == 1)
DOWN = tuple(i for i in range(19) if lattice_vel[i][1] == -1)
FLAT_Y = tuple(i for i in range(19) if lattice_vel[i][1] == 0)

COLUMN = EAST + (MASK,) + WEST + FLAT_X + (20, 21, 22, 23)
PLACE = {field: at for at, field in enumerate(COLUMN)}
HALF = len(COLUMN) // 2
PACKED = ((1, 0, 12), (2, 0, 12), (5, 0, 12), (0, 0, 6), (4, 0, 6), (3, 5, 6), (6, 5, 6), (7, 0, 4))
WHOLE = 36
TROWS = 64
SIDE = 20
TO_EAST = ((0, 0, 8), (0, 11, 9), (1, 0, 6))
TO_WEST = ((0, 3, 8), (0, 11, 9), (1, 5, 6))
TRAVEL = 23
DECK = ((4, 0, 6), (5, 0, 24), (6, 5, 6), (7, 0, 4))
DECK_AT = {4: 0, 5: 6, 6: 30 - 5, 7: 36}
DECK_ROWS = 40
SUMS = 11
EDGE = 4
BLOCK_AT = 88
SUMS_AT = BLOCK_AT + 12 * DEPTH
BULK = SUMS_AT + 2 * (DEPTH + 2) + 44
PIECES = 2


def up_down(rows_up):
    moving = UP if rows_up else DOWN
    near = FLAT_Y + moving + (MASK,)
    far = moving + (MASK,)
    return [(f, True) for f in near] + [(f, False) for f in far]


def sums(g):
    w0, w1, w2 = lattice_weight[0], lattice_weight[1], lattice_weight[7]
    axis = g[1] + g[2] + g[3] + g[4] + g[5] + g[6]
    diag = (g[7] + g[8] + g[9] + g[10]) + (g[11] + g[12] + g[13] + g[14]) + (g[15] + g[16] + g[17] + g[18])
    density = w0 * g[0] + w1 * axis + w2 * diag
    d78, d910 = g[7] - g[8], g[9] - g[10]
    d1112, d1314 = g[11] - g[12], g[13] - g[14]
    d1516, d1718 = g[15] - g[16], g[17] - g[18]
    mx = w1 * (g[1] - g[2]) + w2 * ((d78 + d910) + (d1112 + d1314))
    my = w1 * (g[3] - g[4]) + w2 * ((d78 - d910) + (d1516 + d1718))
    mz = w1 * (g[5] - g[6]) + w2 * ((d1112 - d1314) + (d1516 - d1718))
    return density, mx, my, mz


def velocity(density, mx, my, mz):
    inverse = 1.0 / density
    return density, mx * inverse, my * inverse, mz * inverse


def moments(g):
    return velocity(*sums(g))


def equilibria(density, vx, vy, vz, wanted=range(19)):
    base = density - 1.5 * density * (vx * vx + vy * vy + vz * vz)
    linear = 3.0 * density
    square = 4.5 * density
    out = {}
    for i in wanted:
        if i in out:
            continue
        if i == 0:
            out[0] = base
            continue
        first = i if i % 2 == 1 else i - 1
        cx, cy, cz = lattice_vel[first]
        p = None
        for c, v in ((cx, vx), (cy, vy), (cz, vz)):
            if c == 0:
                continue
            p = (v if c == 1 else -v) if p is None else (p + v if c == 1 else p - v)
        even = base + square * p * p
        odd = linear * p
        out[first] = even + odd
        out[first + 1] = even - odd
    return out


def lanes(shape):
    return lax.broadcasted_iota(jnp.int32, shape, len(shape) - 1)


def ramp(x, start, finish):
    width = (finish - start).astype(jnp.float32)
    angle = math.pi * ((x - start).astype(jnp.float32) + 0.5) / width
    inside = (x >= start) & (x < finish)
    return jnp.where(inside, fringe_peak * jnp.sin(angle) ** 2, 0.0)


def relax_kernel(total_x, *refs):
    recycle, pops_in, solid_in = refs[:3]
    small_in = refs[3:8]
    relaxed, lam, columns, zmsg = refs[8:12]
    grid, pops, solid = refs[12:15]
    small, sem = refs[15:-1], refs[-1]
    loads = [
        [pltpu.make_async_copy(a.at[..., rows, :], b.at[..., rows, :], sem.at[2 * n + m]) for m, (a, b) in enumerate(((pops_in, pops), (solid_in, solid)))]
        for n, rows in enumerate(pl.ds(n * 2 * DEPTH // PIECES, 2 * DEPTH // PIECES) for n in range(PIECES))
    ]
    pieces = DEPTH // 8
    scalars = [pltpu.make_async_copy(a, b, sem.at[2 * PIECES + n]) for n, (a, b) in enumerate(zip(small_in, small))]
    for copy in loads[0] + scalars:
        copy.start()
    for load in loads[1:]:
        for copy in load:
            copy.start()
    for copy in scalars:
        copy.wait()
    bounds, rows_in, weights_in, mean_in, fluct_in = small
    gx, rp = lax.axis_index("gx"), recycle[0]
    x0 = gx * COLS
    off = rp - x0
    lane = lanes((8, 128))
    sub = lax.broadcasted_iota(jnp.int32, (8, 128), 0)
    special = jnp.where(
        lane < 3, x0 - 2 + lane, jnp.where(lane < 6, x0 + COLS - 4 + lane, rp - 7 + lane)
    )
    shares = ramp(jnp.where(sub == 0, x0 + lane, special), bounds[0], bounds[1])
    lam[...] = jnp.where(sub < 2, shares, jnp.where(rp == total_x - 1, 1.0, 0.0))

    col = lane % 8
    slot = lane // 8
    place = off + col - 5
    here = (place >= 0) & (place < COLS) & (col >= 4) & (col < 7)
    static = col < 4
    shift0 = 5 - off + 8 * 128 * 64
    extras = []
    for y in range(ROWS):
        values = jnp.zeros((8, 128), jnp.float32)
        for k, v in enumerate((rows_in[y].astype(jnp.float32), weights_in[y], mean_in[y], fluct_in[y])):
            values = jnp.where((slot == k) & (col == 7), v, values)
        extras.append(values)
    for chunk in range(pieces):
        if chunk % (pieces // PIECES) == 0:
            for copy in loads[chunk // (pieces // PIECES)]:
                copy.wait()
        for y in range(ROWS):
            rows = pl.ds(16 * chunk + y, 8, stride=2)
            g = [pops[i, rows, :] for i in range(19)]
            wall = solid[rows, :] == 1
            density, vx, vy, vz = moments(g)
            eq = equilibria(density, vx, vy, vz)
            field = {}
            for i in range(19):
                loose = g[i] - relax_rate * (g[i] - eq[i])
                field[i] = jnp.where(wall, g[opposite[i]], loose)
            field[MASK] = jnp.where(wall, 1.0, 0.0)
            field[20], field[21], field[22], field[23] = density, vx, vy, vz
            here_z = pl.ds(8 * chunk, 8)
            for f in range(20):
                relaxed[f, y, here_z, :] = field[f]
            for half in range(2):
                fixed = jnp.zeros((8, 128), jnp.float32)
                moving = jnp.zeros((8, 128), jnp.float32)
                for k in range(HALF):
                    v = field[COLUMN[half * HALF + k]]
                    mine = slot == k
                    if half * HALF + k < SIDE:
                        fixed = jnp.where(mine, pltpu.roll(v, 2 + 8 * k, 1), fixed)
                    moving = jnp.where(mine, pltpu.roll(v, (shift0 + 8 * k) % 128, 1), moving)
                rest_of = extras[y] if half == 0 else jnp.zeros((8, 128), jnp.float32)
                packed = jnp.where(static, fixed, jnp.where(here, moving, rest_of))
                grid[pl.ds((y * 2 + half) * DEPTH + 8 * chunk, 8), :] = packed
    grid[...] = grid[...].T
    at = 0
    for c, place, many in PACKED:
        v = grid[pl.ds(8 * place + c, many, stride=8), :]
        columns[pl.ds(at, many), :] = v
        zmsg[pl.ds(at, many), :] = v
        at += many
    for f in range(20):
        for y in range(ROWS):
            at = TROWS + (f * 2 + y) * EDGE
            zmsg[pl.ds(at, 2), :] = relaxed[f, y, pl.ds(0, 2), :]
            zmsg[pl.ds(at + 2, 2), :] = relaxed[f, y, pl.ds(DEPTH - 2, 2), :]


def pack_kernel(ways, relaxed, lam, z_in, *rest):
    laid, bulk, inside = rest[0], rest[1:-1], rest[-1]
    for f in range(20):
        for y in range(ROWS):
            at = TROWS + (f * 2 + y) * EDGE
            laid[f, y, pl.ds(0, 2), :] = z_in[pl.ds(at + 2, 2), :]
            laid[f, y, pl.ds(2, DEPTH), :] = relaxed[f, y, :, :]
            laid[f, y, pl.ds(DEPTH + 2, 2), :] = z_in[pl.ds(at, 2), :]
    lane = lanes((8, 128))
    zone = jnp.broadcast_to(lam[0:1, :], (8, 128))
    zero = jnp.zeros((8, 128), jnp.float32)

    def pack(way, to):
        inner = 0
        for n, (f, near) in enumerate(up_down(way)):
            y = 1 if near == way else 0
            to[pl.ds(n * EDGE, EDGE), :] = z_in[pl.ds(TROWS + (f * 2 + y) * EDGE, EDGE), :]
            if f not in FLAT_Y:
                to[pl.ds(BLOCK_AT + inner * DEPTH, DEPTH), :] = relaxed[f, y, :, :]
                inner += 1
        y = 1 if way else 0
        for chunk in range(DEPTH // 8):
            rows = pl.ds(8 * chunk, 8)
            keep = 1.0 - (1.0 - relaxed[MASK, y, rows, :]) * zone
            for n, i in enumerate(FLAT_Y):
                inside[n, pl.ds(8 + 8 * chunk, 8), :] = relaxed[i, y, rows, :] * keep
        for n in range(len(FLAT_Y)):
            inside[n, pl.ds(0, 8), :] = zero
            inside[n, pl.ds(8 + DEPTH, 16), :] = jnp.zeros((16, 128), jnp.float32)
        for chunk in range(5):
            g = {}
            for n, i in enumerate(FLAT_Y):
                cx, _, cz = lattice_vel[i]
                v = inside[n, pl.ds(7 + 8 * chunk - cz, 8), :]
                if cx == 1:
                    v = jnp.where(lane == 0, 0.0, pltpu.roll(v, 1, 1))
                if cx == -1:
                    v = jnp.where(lane == COLS - 1, 0.0, pltpu.roll(v, COLS - 1, 1))
                g[i] = v
            w0, w1, w2 = lattice_weight[0], lattice_weight[1], lattice_weight[7]
            d12, d56 = g[1] - g[2], g[5] - g[6]
            d1112, d1314 = g[11] - g[12], g[13] - g[14]
            totals = (
                w0 * g[0] + w1 * ((g[1] + g[2]) + (g[5] + g[6])) + w2 * ((g[11] + g[12]) + (g[13] + g[14])),
                w1 * d12 + w2 * (d1112 + d1314),
                w1 * d56 + w2 * (d1112 - d1314),
            )
            many = min(8, DEPTH + 2 - 8 * chunk)
            for n, v in enumerate(totals):
                to[pl.ds(SUMS_AT + n * (DEPTH + 2) + 8 * chunk, many), :] = v[:many]

    for at, way in enumerate(ways):
        if way is None:
            gy = lax.axis_index("gy")

            @pl.when(gy == 0)
            def _():
                pack(True, bulk[at])

            @pl.when(gy != 0)
            def _():
                pack(False, bulk[at])

        else:
            pack(way, bulk[at])


def join(mine, other):
    even = (lanes(mine.shape) // DEPTH) % 2 == 0
    first = jnp.where(even, mine, pltpu.roll(other, DEPTH, 1))
    second = jnp.where(even, pltpu.roll(mine, 128 - DEPTH, 1), other)
    return first, second


def apart(v):
    low = lanes(v.shape) < SPAN
    turned = pltpu.roll(v, SPAN, 1)
    return jnp.where(low, v, turned), jnp.where(low, turned, v)


def shifted(v, i):
    _, cy, cz = lattice_vel[i]
    if cz:
        v = pltpu.roll(v, cz % 128, 1)
    if cy:
        v = pltpu.roll(v, cy % v.shape[0], 0)
    return v


def strip(value, row, total_y, edge):
    held = {}

    def middle(i):
        if i not in held:
            held[i] = value(1, i)
        return held[i]

    bottom, top = row == 0, row == total_y - 1
    g = []
    for i in range(19):
        cx, cy, _ = lattice_vel[i]
        v = shifted(middle(i) if cx == 0 else value(1 - cx, i), i)
        if cx == -1 and edge is not None:
            v = jnp.where(edge, middle(i), v)
        if cy == 1:
            v = jnp.where(bottom, middle(opposite[i]), v)
        if cy == -1:
            v = jnp.where(top, middle(mirror_pop[i]), v)
        g.append(v)
    return middle, g


def lam_at(lam, c, rows):
    return jnp.broadcast_to(lam[1:2, c : c + 1], (rows, 128))


def at_outlet(lam, rows):
    return jnp.broadcast_to(lam[2:3, 0:1], (rows, 128)) == 1.0


def cross_kernel(slots, swap, total_y, lam, *refs):
    pairs = len(slots)
    blocks = refs[: 2 * pairs]
    full, right, left, plane, gains, deck = refs[2 * pairs :]
    gy = lax.axis_index("gy")
    if swap:
        deck[...] = jnp.zeros_like(deck)
    for n in range(pairs):
        first, second = join(
            blocks[2 * n][pl.ds(0, TROWS), :], blocks[2 * n + 1][pl.ds(0, TROWS), :]
        )
        at = 0
        for c, place, many in PACKED:
            full[n, pl.ds(8 * place + c, many, stride=8), :] = first[at : at + many]
            if at < WHOLE:
                full[n, pl.ds(8 * HALF + c, many, stride=8), :] = second[at : at + many]
            at += many
        at = n * TRAVEL
        for (c, place, many), (d, spot, count) in zip(TO_EAST, TO_WEST):
            right[pl.ds(at, many), :] = full[n, pl.ds(8 * place + 1 - c, many, stride=8), :]
            left[pl.ds(at, count), :] = full[n, pl.ds(8 * spot + 2 + d, count, stride=8), :]
            at += many
        slot = 4 - 4 * gy if slots[n] is None else slots[n]
        at = 0
        for c, place, many in DECK:
            top, bottom = apart(full[n, pl.ds(8 * place + c, many, stride=8), :])
            deck[pl.ds(8 * at + slot, many, stride=8), :] = top
            deck[pl.ds(8 * at + slot + 1, many, stride=8), :] = bottom
            at += many

    def deck_at(row):
        return deck[pl.ds(8 * row, 8), :]

    def read(c, f):
        return deck_at(DECK_AT[4 + c] + PLACE[f])

    keep = [1.0 - (1.0 - read(c, MASK)) * lam_at(lam, 6 + c, 8) for c in range(3)]
    row = lax.broadcasted_iota(jnp.int32, (8, 128), 0) + 2 * gy - 2
    _, g = strip(lambda c, i: read(c, i) * keep[c], row, total_y, at_outlet(lam, 8))
    fields = list(sums(g)) + [read(c, MASK) for c in range(3)] + [read(1, 20 + k) for k in range(4)]
    params = [deck_at(36 + k) for k in range(4)]
    if not swap:
        for n, v in enumerate(fields + params):
            plane[pl.ds(8 * n, 8), :] = v
        return

    def settle(v):
        return jnp.where(gy == 0, pltpu.roll(v, 6, 0), v)

    for n, v in enumerate(params):
        gains[pl.ds(8 * n, 8), :] = settle(v)
    fields = [settle(v) for v in fields] + [jnp.zeros((8, 128), jnp.float32)]
    low, upper = lanes((8, 128)) < SPAN, lax.broadcasted_iota(jnp.int32, (8, 128), 0) < 4
    for n in range(3):
        a, b, c, d = fields[4 * n : 4 * n + 4]
        lower = pltpu.roll(jnp.where(low, c, d), 4, 0)
        plane[pl.ds(8 * n, 8), :] = jnp.where(upper, jnp.where(low, a, b), lower)
    tail = right.shape[0] - 24
    right[pl.ds(tail, 24), :] = plane[...]
    left[pl.ds(tail, 24), :] = plane[...]


def strips_kernel(slots, swap, total_y, total_x, lam, full, west, east, plane, gains, out, side, shelf):
    gx, gy = lax.axis_index("gx"), lax.axis_index("gy")
    last_x = total_x // COLS - 1
    deep = max(8, total_y)
    if swap:
        side[...] = jnp.zeros_like(side)
        shelf[...] = jnp.zeros_like(shelf)

    def lay(s, c, first, place, v):
        top, bottom = apart(v)
        many = v.shape[0]
        side[s, c, pl.ds(8 * place + first, many, stride=8), :] = top
        side[s, c, pl.ds(8 * place + first + 1, many, stride=8), :] = bottom

    for n, slot in enumerate(slots):
        slot = 4 - 4 * gy if slot is None else slot
        lay(0, 2, slot, 0, full[n, pl.ds(2, SIDE, stride=8), :])
        lay(1, 0, slot, 0, full[n, pl.ds(1, SIDE, stride=8), :])
        at = n * TRAVEL
        for (c, place, many), (d, spot, count) in zip(TO_EAST, TO_WEST):
            lay(0, 1 - c, slot, place, west[pl.ds(at, many), :])
            lay(1, 1 + d, slot, spot, east[pl.ds(at, count), :])
            at += many

    if swap:
        fields = []
        low = lanes((8, 128)) < SPAN
        for n in range(3):
            v = plane[pl.ds(8 * n, 8), :]
            for w in (v, pltpu.roll(v, 4, 0)):
                turned = pltpu.roll(w, SPAN, 1)
                fields += [jnp.where(low, w, turned), jnp.where(low, turned, w)]
        which, ratio, mean_gain, fluct_gain = (gains[pl.ds(8 * k, 8), :] for k in range(4))
    else:
        fields = [plane[pl.ds(deep * n, deep), :] for n in range(SUMS + 4)]
        which, ratio, mean_gain, fluct_gain = fields[SUMS:]

    def target(fields):
        def blend(v):
            low, high = v[0:1], v[1:2]
            low = jnp.broadcast_to(low, v.shape)
            high = jnp.broadcast_to(high, v.shape)
            for r in range(1, total_y - 1):
                chosen = which == float(r)
                low = jnp.where(chosen, jnp.broadcast_to(v[r : r + 1], v.shape), low)
                high = jnp.where(chosen, jnp.broadcast_to(v[r + 1 : r + 2], v.shape), high)
            return (1.0 - ratio) * low + ratio * high

        result = [blend(fields[0])]
        for v in fields[1:]:
            mean = jnp.sum(v, axis=1, keepdims=True) * (1.0 / 128.0)
            mean = blend(jnp.broadcast_to(mean, v.shape))
            result.append(mean_gain * mean + fluct_gain * (blend(v) - mean))
        return result

    def local(fields):
        got = []
        for k, v in enumerate(fields):
            shelf[k, pl.ds(8, deep), :] = v
            got.append(shelf[k, pl.ds(6 + 2 * gy, 8), :])
        return got

    target0 = target(fields[7:11])
    teq0 = equilibria(*target0)
    gates = [(1.0 - fields[4 + c]) * lam_at(lam, 6 + c, deep) for c in range(3)]
    row = lax.broadcasted_iota(jnp.int32, (deep, 128), 0)
    _, g = strip(lambda c, i: gates[c] * teq0[i], row, total_y, at_outlet(lam, deep))
    total = [a + b for a, b in zip(sums(g), fields[:4])]
    target1 = target(list(velocity(*total)))
    near0, near1 = local(target0), local(target1)
    goal0, goal1 = equilibria(*near0), equilibria(*near1)

    row = lax.broadcasted_iota(jnp.int32, (8, 128), 0) + 2 * gy - 2
    first, second = [], []
    for s, wanted in ((0, EAST), (1, WEST)):

        def read(c, f):
            return side[s, c, pl.ds(PLACE[f] * 8, 8), :]

        gate = [(1.0 - read(c, MASK)) * lam_at(lam, 3 * s + c, 8) for c in range(3)]

        def value(c, i):
            v = read(c, i)
            return v + gate[c] * (goal0[i] - v)

        middle, g = strip(value, row, total_y, None)
        eq = equilibria(*moments(g), wanted)
        wall = read(1, MASK) == 1.0
        for i in wanted:
            loose = g[i] - relax_rate * (g[i] - eq[i])
            v = jnp.where(wall, g[opposite[i]], loose)
            a, b = shifted(middle(i), i), shifted(v + gate[1] * (goal1[i] - v), i)
            if s == 0:
                a, b = jnp.where(gx == 0, goal0[i], a), jnp.where(gx == 0, goal1[i], b)
            else:
                a = jnp.where(gx == last_x, value(0, i), a)
            first.append(a)
            second.append(b)
    blank = [jnp.zeros((16, 128), jnp.float32)]
    for n, rows in enumerate((first + near0 + blank, second + near1 + blank)):
        turned = pltpu.roll(jnp.concatenate(rows, axis=0), 2, 1).T
        out[pl.ds(48 * n, 48), :] = turned[:48]


def steps_kernel(ways, total_y, total_x, lam, laid, cols, *rest):
    count = len(ways)
    bulk = rest[:count]
    result, early, late, out, sem = rest[count:]
    gx, gy = lax.axis_index("gx"), lax.axis_index("gy")
    at_end = gx == total_x // COLS - 1
    bottom, top = gy == 0, gy == total_y // ROWS - 1
    lane = lanes((8, 128))
    at_first, at_last = lane == 0, lane == COLS - 1
    zone = jnp.broadcast_to(lam[0:1, :], (8, 128))

    def column(step, index, at):
        return jnp.broadcast_to(cols[pl.ds(48 * step + at, 8), index : index + 1], (8, 128))

    def goals(step, slot, at, wanted, gate):
        density, vx, vy, vz = (column(step, 80 + 8 * k + slot, at) for k in range(4))
        return equilibria(gate * density, vx, vy, vz, wanted)

    def field(i, slot, rows):
        return laid[i, slot - 2, rows, :] if slot in (2, 3) else early[i, slot, rows, :]

    def finish(slot, fields):
        for chunk in range(5):
            rows = pl.ds(8 * chunk, 8)
            gate = (1.0 - field(MASK, slot, rows)) * zone
            goal = goals(0, slot, 8 * chunk, fields, gate)
            keep = 1.0 - gate
            for i in fields:
                early[i, slot, rows, :] = keep * field(i, slot, rows) + goal[i]

    def pull(ref, slot, lead, step, at, lift, mine):
        r = at - lift
        g = []
        for i in range(19):
            cx, cy, cz = lattice_vel[i]
            v = ref[i, slot - cy - lead, pl.ds(r - cz, 8), :]
            if cx == 1:
                edge = column(step, EAST.index(i) * 8 + slot, at)
                v = jnp.where(at_first, edge, pltpu.roll(v, 1, 1))
            if cx == -1:
                edge = column(step, 40 + WEST.index(i) * 8 + slot, at)
                if step == 1:
                    edge = jnp.where(at_end, ref[i, slot - lead, pl.ds(r, 8), :], edge)
                v = jnp.where(at_last, edge, pltpu.roll(v, COLS - 1, 1))
            if mine and cy == 1 and slot == 2:
                v = jnp.where(bottom, ref[opposite[i], slot - lead, pl.ds(r, 8), :], v)
            if mine and cy == -1 and slot == 3:
                v = jnp.where(top, ref[mirror_pop[i], slot - lead, pl.ds(r, 8), :], v)
            g.append(v)
        return g

    def collide(slot, wanted, chunk, came=None):
        at = 1 + 8 * chunk
        g = pull(early, slot, 0, 0, at, 0, came is None)
        total = sums(g)
        if came is not None:
            density, mx, mz = (came[pl.ds(SUMS_AT + n * (DEPTH + 2) + 8 * chunk, 8), :] for n in range(3))
            total = (total[0] + density, total[1] + mx, total[2], total[3] + mz)
        density, vx, vy, vz = velocity(*total)
        eq = equilibria(relax_rate * density, vx, vy, vz, wanted)
        solid = field(MASK, slot, pl.ds(at, 8))
        gate = (1.0 - solid) * zone
        goal = goals(1, slot, at, wanted, gate)
        keep = 1.0 - gate
        wall = solid == 1.0
        for i in wanted:
            v = jnp.where(wall, g[opposite[i]], (1.0 - relax_rate) * g[i] + eq[i])
            late[i, slot - 1, pl.ds(8 * chunk, 8), :] = keep * v + goal[i]

    for slot in (2, 3):
        finish(slot, range(19))

    def beside(n, came_up):
        near_slot, far_slot = (1, 0) if came_up else (4, 5)
        inner = 0
        for k, (f, near) in enumerate(up_down(came_up)):
            slot = near_slot if near else far_slot
            at = k * EDGE
            early[f, slot, pl.ds(0, 2), :] = bulk[n][pl.ds(at + 2, 2), :]
            early[f, slot, pl.ds(DEPTH + 2, 2), :] = bulk[n][pl.ds(at, 2), :]
            if f in FLAT_Y:
                early[f, slot, pl.ds(2, DEPTH), :] = jnp.zeros((DEPTH, 128), jnp.float32)
            else:
                early[f, slot, pl.ds(2, DEPTH), :] = bulk[n][pl.ds(BLOCK_AT + inner * DEPTH, DEPTH), :]
                inner += 1
        moving = UP if came_up else DOWN
        finish(near_slot, FLAT_Y + moving)
        finish(far_slot, moving)
        for chunk in range(5):
            collide(near_slot, moving, chunk, bulk[n])

    for n, way in enumerate(ways):
        if way is not False:

            @pl.when(jnp.logical_not(bottom))
            def _():
                beside(n, True)

        if way is not True:

            @pl.when(jnp.logical_not(top))
            def _():
                beside(n, False)

    stores = []
    for chunk in range(5):
        for slot in (2, 3):
            collide(slot, range(19), chunk)
    for chunk in range(1, 5):
        for y in range(ROWS):
            g = pull(late, 2 + y, 1, 1, 8 * chunk - 6, 1, True)
            for i in range(19):
                out[i, pl.ds(16 * (chunk - 1) + y, 8, stride=2), :] = g[i]
        rows = pl.ds(16 * (chunk - 1), 16)
        stores.append(pltpu.make_async_copy(out.at[:, rows, :], result.at[:, rows, :], sem.at[chunk - 1]))
        stores[-1].start()
    for copy in stores:
        copy.wait()


def call(kernel, outs, scratch, limit, *args, held=False, leave=False):
    near = pl.BlockSpec(memory_space=pltpu.VMEM)
    far = pl.BlockSpec(memory_space=pltpu.HBM)
    inputs = [near] * len(args)
    if held:
        inputs = [pl.BlockSpec(memory_space=pltpu.SMEM)] + [far] * (len(args) - 1)
        args = [args[0]] + [pltpu.with_memory_space_constraint(v, pltpu.HBM) for v in args[1:]]
    return pl.pallas_call(
        kernel,
        out_shape=[jax.ShapeDtypeStruct(s, jnp.float32) for s in outs],
        in_specs=inputs,
        out_specs=[far if leave else near] * len(outs),
        scratch_shapes=[pltpu.VMEM(s, jnp.float32) if isinstance(s, tuple) else s for s in scratch],
        compiler_params=pltpu.CompilerParams(vmem_limit_bytes=limit << 20),
    )(*args)


def ring(count, step):
    return [(i, (i + step) % count) for i in range(count)]


def body(populations, solid_mask, recycle_plane, fringe_bounds, interp_rows, interp_weights, mean_scale, fluct_scale):
    size_x, size_y = lax.axis_size("gx"), lax.axis_size("gy")
    total_x, total_y = COLS * size_x, ROWS * size_y
    swap = size_y == 2
    ways = (None,) if swap else (True, False)
    slots = (2,) + ((None,) if swap else (0, 4))
    pairs = len(slots)
    pops = populations.reshape(19, DEPTH * ROWS, COLS)
    solid = solid_mask.reshape(DEPTH * ROWS, COLS)

    relaxed, lam, columns, z_out = call(
        functools.partial(relax_kernel, total_x),
        [(20, ROWS, DEPTH, COLS), (8, 128), (TROWS, 128), (TROWS + 40 * EDGE, 128)],
        [
            (128, 128),
            pops.shape,
            pltpu.VMEM(solid.shape, jnp.int32),
            pltpu.SMEM((2,), jnp.int32),
            pltpu.SMEM((ROWS,), jnp.int32),
            pltpu.SMEM((ROWS,), jnp.float32),
            pltpu.SMEM((ROWS,), jnp.float32),
            pltpu.SMEM((ROWS,), jnp.float32),
            pltpu.SemaphoreType.DMA((2 * PIECES + 5,)),
        ],
        8,
        recycle_plane,
        pops,
        solid,
        fringe_bounds,
        interp_rows,
        interp_weights,
        mean_scale,
        fluct_scale,
        held=True,
    )
    def across(v, way):
        if way is None:
            return lax.ppermute(v, "gy", ring(2, 1))
        step = 1 if way else -1
        return lax.ppermute(v, "gy", [(i, i + step) for i in range(size_y) if 0 <= i + step < size_y])

    beside = [across(columns, way) for way in ways]
    z_in = lax.ppermute(z_out, "gz", ring(2, 1))
    laid, *bulk_out = call(
        functools.partial(pack_kernel, ways),
        [(20, ROWS, DEPTH + 16, COLS)] + [(BULK, 128)] * len(ways),
        [(len(FLAT_Y), DEPTH + 24, 128)],
        4,
        relaxed,
        lam,
        z_in,
    )
    bulk = [across(v, way) for v, way in zip(bulk_out, ways)]
    beside_other = [lax.ppermute(v, "gz", ring(2, 1)) for v in beside]

    blocks = [columns, z_in]
    for a, b in zip(beside, beside_other):
        blocks += [a, b]
    edge_rows = 72
    full, right, left, plane, gains = call(
        functools.partial(cross_kernel, slots, swap, total_y),
        [(pairs, 16 * HALF, 128), (edge_rows, 128), (edge_rows, 128), (24 if swap else 8 * (SUMS + 4), 128), (32, 128)],
        [(8 * DECK_ROWS, 128)],
        4,
        lam,
        *blocks,
    )
    west = lax.ppermute(right, "gx", ring(size_x, 1))
    east = lax.ppermute(left, "gx", ring(size_x, -1))
    if swap and size_x == 4:
        far = lax.ppermute(plane, "gx", ring(4, 2))
        plane = plane + far + west[edge_rows - 24 :] + east[edge_rows - 24 :]
    elif swap:
        plane = lax.psum(plane, "gx")
    else:
        own = plane.reshape(SUMS + 4, 8, 128)[:, 2:4]
        first = (lax.axis_index("gx") == 0) | (jnp.arange(SUMS + 4) < SUMS)
        own = jnp.where(first[:, None, None], own, 0.0)
        whole = lax.dynamic_update_slice(
            jnp.zeros((SUMS + 4, total_y, 128), jnp.float32), own, (0, 2 * lax.axis_index("gy"), 0)
        )
        plane = lax.psum(whole, ("gx", "gy")).reshape((SUMS + 4) * total_y, 128)

    (cols,) = call(
        functools.partial(strips_kernel, slots, swap, total_y, total_x),
        [(96, 128)],
        [(2, 3, SIDE * 8, 128), (4, 16 + max(8, total_y), 128)],
        8,
        lam,
        full,
        west,
        east,
        plane,
        gains,
    )
    (out,) = call(
        functools.partial(steps_kernel, ways, total_y, total_x),
        [(19, DEPTH * ROWS, COLS)],
        [(20, 6, 48, 128), (19, 4, 40, 128), (19, DEPTH * ROWS, COLS), pltpu.SemaphoreType.DMA((DEPTH // 8,))],
        12,
        lam,
        laid,
        cols,
        *bulk,
        leave=True,
    )
    return out.reshape(populations.shape)


def solution(mesh):
    placed = (
        P(None, ("parts", "gz"), "gy", "gx"),
        P(("parts", "gz"), "gy", "gx"),
        P(),
        P(),
        P("gy"),
        P("gy"),
        P("gy"),
        P("gy"),
    )
    return jax.shard_map(
        body,
        mesh=mesh,
        in_specs=placed,
        out_specs=P(None, ("parts", "gz"), "gy", "gx"),
        check_vma=False,
    )
```

```python
import functools
import math

import jax
import jax.numpy as jnp
from jax import lax
from jax.experimental import pallas as pl
from jax.experimental.pallas import tpu as pltpu
from jax.sharding import PartitionSpec as P

lattice_vel = (
    (0, 0, 0),
    (1, 0, 0),
    (-1, 0, 0),
    (0, 1, 0),
    (0, -1, 0),
    (0, 0, 1),
    (0, 0, -1),
    (1, 1, 0),
    (-1, -1, 0),
    (1, -1, 0),
    (-1, 1, 0),
    (1, 0, 1),
    (-1, 0, -1),
    (1, 0, -1),
    (-1, 0, 1),
    (0, 1, 1),
    (0, -1, -1),
    (0, 1, -1),
    (0, -1, 1),
)
lattice_weight = (1.0 / 3.0,) + (1.0 / 18.0,) * 6 + (1.0 / 36.0,) * 12
opposite = (0, 2, 1, 4, 3, 6, 5, 8, 7, 10, 9, 12, 11, 14, 13, 16, 15, 18, 17)
mirror_pop = (0, 1, 2, 4, 3, 5, 6, 9, 10, 7, 8, 11, 12, 13, 14, 18, 17, 16, 15)
relax_rate = 1.25
fringe_peak = 0.8

DEPTH, ROWS, COLS = 32, 2, 128
SPAN = 2 * DEPTH
MASK = 19
EAST = (1, 11, 13, 7, 9)
WEST = (8, 10, 2, 12, 14)
FLAT_X = tuple(i for i in range(19) if lattice_vel[i][0] == 0)
UP = tuple(i for i in range(19) if lattice_vel[i][1] == 1)
DOWN = tuple(i for i in range(19) if lattice_vel[i][1] == -1)
FLAT_Y = tuple(i for i in range(19) if lattice_vel[i][1] == 0)

COLUMN = EAST + (MASK,) + WEST + FLAT_X + (20, 21, 22, 23)
PLACE = {field: at for at, field in enumerate(COLUMN)}
HALF = len(COLUMN) // 2
PACKED = ((1, 0, 12), (2, 0, 12), (5, 0, 12), (0, 0, 6), (4, 0, 6), (3, 5, 6), (6, 5, 6), (7, 0, 4))
WHOLE = 36
TROWS = 64
SIDE = 20
TO_EAST = ((0, 0, 8), (0, 11, 9), (1, 0, 6))
TO_WEST = ((0, 3, 8), (0, 11, 9), (1, 5, 6))
TRAVEL = 23
DECK = ((4, 0, 6), (5, 0, 24), (6, 5, 6), (7, 0, 4))
DECK_AT = {4: 0, 5: 6, 6: 30 - 5, 7: 36}
DECK_ROWS = 40
SUMS = 11
EDGE = 4
BLOCK_AT = 88
SUMS_AT = BLOCK_AT + 12 * DEPTH
BULK = SUMS_AT + 2 * (DEPTH + 2) + 44
PIECES = 2


def up_down(rows_up):
    moving = UP if rows_up else DOWN
    near = FLAT_Y + moving + (MASK,)
    far = moving + (MASK,)
    return [(f, True) for f in near] + [(f, False) for f in far]


def sums(g):
    w0, w1, w2 = lattice_weight[0], lattice_weight[1], lattice_weight[7]
    axis = g[1] + g[2] + g[3] + g[4] + g[5] + g[6]
    diag = (g[7] + g[8] + g[9] + g[10]) + (g[11] + g[12] + g[13] + g[14]) + (g[15] + g[16] + g[17] + g[18])
    density = w0 * g[0] + w1 * axis + w2 * diag
    d78, d910 = g[7] - g[8], g[9] - g[10]
    d1112, d1314 = g[11] - g[12], g[13] - g[14]
    d1516, d1718 = g[15] - g[16], g[17] - g[18]
    mx = w1 * (g[1] - g[2]) + w2 * ((d78 + d910) + (d1112 + d1314))
    my = w1 * (g[3] - g[4]) + w2 * ((d78 - d910) + (d1516 + d1718))
    mz = w1 * (g[5] - g[6]) + w2 * ((d1112 - d1314) + (d1516 - d1718))
    return density, mx, my, mz


def velocity(density, mx, my, mz):
    inverse = 1.0 / density
    return density, mx * inverse, my * inverse, mz * inverse


def moments(g):
    return velocity(*sums(g))


def equilibria(density, vx, vy, vz, wanted=range(19)):
    base = density - 1.5 * density * (vx * vx + vy * vy + vz * vz)
    linear = 3.0 * density
    square = 4.5 * density
    out = {}
    for i in wanted:
        if i in out:
            continue
        if i == 0:
            out[0] = base
            continue
        first = i if i % 2 == 1 else i - 1
        cx, cy, cz = lattice_vel[first]
        p = None
        for c, v in ((cx, vx), (cy, vy), (cz, vz)):
            if c == 0:
                continue
            p = (v if c == 1 else -v) if p is None else (p + v if c == 1 else p - v)
        even = base + square * p * p
        odd = linear * p
        out[first] = even + odd
        out[first + 1] = even - odd
    return out


def lanes(shape):
    return lax.broadcasted_iota(jnp.int32, shape, len(shape) - 1)


def ramp(x, start, finish):
    width = (finish - start).astype(jnp.float32)
    angle = math.pi * ((x - start).astype(jnp.float32) + 0.5) / width
    inside = (x >= start) & (x < finish)
    return jnp.where(inside, fringe_peak * jnp.sin(angle) ** 2, 0.0)


def relax_kernel(total_x, *refs):
    recycle, pops_in, solid_in = refs[:3]
    small_in = refs[3:8]
    relaxed, lam, columns, zmsg = refs[8:12]
    grid, pops, solid = refs[12:15]
    small, sem = refs[15:-1], refs[-1]
    loads = [
        [pltpu.make_async_copy(a.at[..., rows, :], b.at[..., rows, :], sem.at[2 * n + m]) for m, (a, b) in enumerate(((pops_in, pops), (solid_in, solid)))]
        for n, rows in enumerate(pl.ds(n * 2 * DEPTH // PIECES, 2 * DEPTH // PIECES) for n in range(PIECES))
    ]
    pieces = DEPTH // 8
    scalars = [pltpu.make_async_copy(a, b, sem.at[2 * PIECES + n]) for n, (a, b) in enumerate(zip(small_in, small))]
    for copy in loads[0] + scalars:
        copy.start()
    for load in loads[1:]:
        for copy in load:
            copy.start()
    for copy in scalars:
        copy.wait()
    bounds, rows_in, weights_in, mean_in, fluct_in = small
    gx, rp = lax.axis_index("gx"), recycle[0]
    x0 = gx * COLS
    off = rp - x0
    lane = lanes((8, 128))
    sub = lax.broadcasted_iota(jnp.int32, (8, 128), 0)
    special = jnp.where(
        lane < 3, x0 - 2 + lane, jnp.where(lane < 6, x0 + COLS - 4 + lane, rp - 7 + lane)
    )
    shares = ramp(jnp.where(sub == 0, x0 + lane, special), bounds[0], bounds[1])
    lam[...] = jnp.where(sub < 2, shares, jnp.where(rp == total_x - 1, 1.0, 0.0))

    col = lane % 8
    slot = lane // 8
    place = off + col - 5
    here = (place >= 0) & (place < COLS) & (col >= 4) & (col < 7)
    static = col < 4
    shift0 = 5 - off + 8 * 128 * 64
    extras = []
    for y in range(ROWS):
        values = jnp.zeros((8, 128), jnp.float32)
        for k, v in enumerate((rows_in[y].astype(jnp.float32), weights_in[y], mean_in[y], fluct_in[y])):
            values = jnp.where((slot == k) & (col == 7), v, values)
        extras.append(values)
    for chunk in range(pieces):
        if chunk % (pieces // PIECES) == 0:
            for copy in loads[chunk // (pieces // PIECES)]:
                copy.wait()
        for y in range(ROWS):
            rows = pl.ds(16 * chunk + y, 8, stride=2)
            g = [pops[i, rows, :] for i in range(19)]
            wall = solid[rows, :] == 1
            density, vx, vy, vz = moments(g)
            eq = equilibria(density, vx, vy, vz)
            field = {}
            for i in range(19):
                loose = g[i] - relax_rate * (g[i] - eq[i])
                field[i] = jnp.where(wall, g[opposite[i]], loose)
            field[MASK] = jnp.where(wall, 1.0, 0.0)
            field[20], field[21], field[22], field[23] = density, vx, vy, vz
            here_z = pl.ds(8 * chunk, 8)
            for f in range(20):
                relaxed[f, y, here_z, :] = field[f]
            for half in range(2):
                fixed = jnp.zeros((8, 128), jnp.float32)
                moving = jnp.zeros((8, 128), jnp.float32)
                for k in range(HALF):
                    v = field[COLUMN[half * HALF + k]]
                    mine = slot == k
                    if half * HALF + k < SIDE:
                        fixed = jnp.where(mine, pltpu.roll(v, 2 + 8 * k, 1), fixed)
                    moving = jnp.where(mine, pltpu.roll(v, (shift0 + 8 * k) % 128, 1), moving)
                rest_of = extras[y] if half == 0 else jnp.zeros((8, 128), jnp.float32)
                packed = jnp.where(static, fixed, jnp.where(here, moving, rest_of))
                grid[pl.ds((y * 2 + half) * DEPTH + 8 * chunk, 8), :] = packed
    grid[...] = grid[...].T
    at = 0
    for c, place, many in PACKED:
        v = grid[pl.ds(8 * place + c, many, stride=8), :]
        columns[pl.ds(at, many), :] = v
        zmsg[pl.ds(at, many), :] = v
        at += many
    for f in range(20):
        for y in range(ROWS):
            at = TROWS + (f * 2 + y) * EDGE
            zmsg[pl.ds(at, 2), :] = relaxed[f, y, pl.ds(0, 2), :]
            zmsg[pl.ds(at + 2, 2), :] = relaxed[f, y, pl.ds(DEPTH - 2, 2), :]


def pack_kernel(ways, relaxed, lam, z_in, *rest):
    laid, bulk, inside = rest[0], rest[1:-1], rest[-1]
    for f in range(20):
        for y in range(ROWS):
            at = TROWS + (f * 2 + y) * EDGE
            laid[f, y, pl.ds(0, 2), :] = z_in[pl.ds(at + 2, 2), :]
            laid[f, y, pl.ds(2, DEPTH), :] = relaxed[f, y, :, :]
            laid[f, y, pl.ds(DEPTH + 2, 2), :] = z_in[pl.ds(at, 2), :]
    lane = lanes((8, 128))
    zone = jnp.broadcast_to(lam[0:1, :], (8, 128))
    zero = jnp.zeros((8, 128), jnp.float32)

    def pack(way, to):
        inner = 0
        for n, (f, near) in enumerate(up_down(way)):
            y = 1 if near == way else 0
            to[pl.ds(n * EDGE, EDGE), :] = z_in[pl.ds(TROWS + (f * 2 + y) * EDGE, EDGE), :]
            if f not in FLAT_Y:
                to[pl.ds(BLOCK_AT + inner * DEPTH, DEPTH), :] = relaxed[f, y, :, :]
                inner += 1
        y = 1 if way else 0
        for chunk in range(DEPTH // 8):
            rows = pl.ds(8 * chunk, 8)
            keep = 1.0 - (1.0 - relaxed[MASK, y, rows, :]) * zone
            for n, i in enumerate(FLAT_Y):
                inside[n, pl.ds(8 + 8 * chunk, 8), :] = relaxed[i, y, rows, :] * keep
        for n in range(len(FLAT_Y)):
            inside[n, pl.ds(0, 8), :] = zero
            inside[n, pl.ds(8 + DEPTH, 16), :] = jnp.zeros((16, 128), jnp.float32)
        for chunk in range(5):
            g = {}
            for n, i in enumerate(FLAT_Y):
                cx, _, cz = lattice_vel[i]
                v = inside[n, pl.ds(7 + 8 * chunk - cz, 8), :]
                if cx == 1:
                    v = jnp.where(lane == 0, 0.0, pltpu.roll(v, 1, 1))
                if cx == -1:
                    v = jnp.where(lane == COLS - 1, 0.0, pltpu.roll(v, COLS - 1, 1))
                g[i] = v
            w0, w1, w2 = lattice_weight[0], lattice_weight[1], lattice_weight[7]
            d12, d56 = g[1] - g[2], g[5] - g[6]
            d1112, d1314 = g[11] - g[12], g[13] - g[14]
            totals = (
                w0 * g[0] + w1 * ((g[1] + g[2]) + (g[5] + g[6])) + w2 * ((g[11] + g[12]) + (g[13] + g[14])),
                w1 * d12 + w2 * (d1112 + d1314),
                w1 * d56 + w2 * (d1112 - d1314),
            )
            many = min(8, DEPTH + 2 - 8 * chunk)
            for n, v in enumerate(totals):
                to[pl.ds(SUMS_AT + n * (DEPTH + 2) + 8 * chunk, many), :] = v[:many]

    for at, way in enumerate(ways):
        if way is None:
            gy = lax.axis_index("gy")

            @pl.when(gy == 0)
            def _():
                pack(True, bulk[at])

            @pl.when(gy != 0)
            def _():
                pack(False, bulk[at])

        else:
            pack(way, bulk[at])


def join(mine, other):
    even = (lanes(mine.shape) // DEPTH) % 2 == 0
    first = jnp.where(even, mine, pltpu.roll(other, DEPTH, 1))
    second = jnp.where(even, pltpu.roll(mine, 128 - DEPTH, 1), other)
    return first, second


def apart(v):
    low = lanes(v.shape) < SPAN
    turned = pltpu.roll(v, SPAN, 1)
    return jnp.where(low, v, turned), jnp.where(low, turned, v)


def shifted(v, i):
    _, cy, cz = lattice_vel[i]
    if cz:
        v = pltpu.roll(v, cz % 128, 1)
    if cy:
        v = pltpu.roll(v, cy % v.shape[0], 0)
    return v


def strip(value, row, total_y, edge):
    held = {}

    def middle(i):
        if i not in held:
            held[i] = value(1, i)
        return held[i]

    bottom, top = row == 0, row == total_y - 1
    g = []
    for i in range(19):
        cx, cy, _ = lattice_vel[i]
        v = shifted(middle(i) if cx == 0 else value(1 - cx, i), i)
        if cx == -1 and edge is not None:
            v = jnp.where(edge, middle(i), v)
        if cy == 1:
            v = jnp.where(bottom, middle(opposite[i]), v)
        if cy == -1:
            v = jnp.where(top, middle(mirror_pop[i]), v)
        g.append(v)
    return middle, g


def lam_at(lam, c, rows):
    return jnp.broadcast_to(lam[1:2, c : c + 1], (rows, 128))


def at_outlet(lam, rows):
    return jnp.broadcast_to(lam[2:3, 0:1], (rows, 128)) == 1.0


def cross_kernel(slots, swap, total_y, lam, *refs):
    pairs = len(slots)
    blocks = refs[: 2 * pairs]
    full, right, left, plane, gains, deck = refs[2 * pairs :]
    gy = lax.axis_index("gy")
    if swap:
        deck[...] = jnp.zeros_like(deck)
    for n in range(pairs):
        first, second = join(
            blocks[2 * n][pl.ds(0, TROWS), :], blocks[2 * n + 1][pl.ds(0, TROWS), :]
        )
        at = 0
        for c, place, many in PACKED:
            full[n, pl.ds(8 * place + c, many, stride=8), :] = first[at : at + many]
            if at < WHOLE:
                full[n, pl.ds(8 * HALF + c, many, stride=8), :] = second[at : at + many]
            at += many
        at = n * TRAVEL
        for (c, place, many), (d, spot, count) in zip(TO_EAST, TO_WEST):
            right[pl.ds(at, many), :] = full[n, pl.ds(8 * place + 1 - c, many, stride=8), :]
            left[pl.ds(at, count), :] = full[n, pl.ds(8 * spot + 2 + d, count, stride=8), :]
            at += many
        slot = 4 - 4 * gy if slots[n] is None else slots[n]
        at = 0
        for c, place, many in DECK:
            top, bottom = apart(full[n, pl.ds(8 * place + c, many, stride=8), :])
            deck[pl.ds(8 * at + slot, many, stride=8), :] = top
            deck[pl.ds(8 * at + slot + 1, many, stride=8), :] = bottom
            at += many

    def deck_at(row):
        return deck[pl.ds(8 * row, 8), :]

    def read(c, f):
        return deck_at(DECK_AT[4 + c] + PLACE[f])

    keep = [1.0 - (1.0 - read(c, MASK)) * lam_at(lam, 6 + c, 8) for c in range(3)]
    row = lax.broadcasted_iota(jnp.int32, (8, 128), 0) + 2 * gy - 2
    _, g = strip(lambda c, i: read(c, i) * keep[c], row, total_y, at_outlet(lam, 8))
    fields = list(sums(g)) + [read(c, MASK) for c in range(3)] + [read(1, 20 + k) for k in range(4)]
    params = [deck_at(36 + k) for k in range(4)]
    if not swap:
        for n, v in enumerate(fields + params):
            plane[pl.ds(8 * n, 8), :] = v
        return

    def settle(v):
        return jnp.where(gy == 0, pltpu.roll(v, 6, 0), v)

    for n, v in enumerate(params):
        gains[pl.ds(8 * n, 8), :] = settle(v)
    fields = [settle(v) for v in fields] + [jnp.zeros((8, 128), jnp.float32)]
    low, upper = lanes((8, 128)) < SPAN, lax.broadcasted_iota(jnp.int32, (8, 128), 0) < 4
    for n in range(3):
        a, b, c, d = fields[4 * n : 4 * n + 4]
        lower = pltpu.roll(jnp.where(low, c, d), 4, 0)
        plane[pl.ds(8 * n, 8), :] = jnp.where(upper, jnp.where(low, a, b), lower)
    tail = right.shape[0] - 24
    right[pl.ds(tail, 24), :] = plane[...]
    left[pl.ds(tail, 24), :] = plane[...]


def strips_kernel(slots, swap, total_y, total_x, lam, full, west, east, plane, gains, out, side, shelf):
    gx, gy = lax.axis_index("gx"), lax.axis_index("gy")
    last_x = total_x // COLS - 1
    deep = max(8, total_y)
    if swap:
        side[...] = jnp.zeros_like(side)
        shelf[...] = jnp.zeros_like(shelf)

    def lay(s, c, first, place, v):
        top, bottom = apart(v)
        many = v.shape[0]
        side[s, c, pl.ds(8 * place + first, many, stride=8), :] = top
        side[s, c, pl.ds(8 * place + first + 1, many, stride=8), :] = bottom

    for n, slot in enumerate(slots):
        slot = 4 - 4 * gy if slot is None else slot
        lay(0, 2, slot, 0, full[n, pl.ds(2, SIDE, stride=8), :])
        lay(1, 0, slot, 0, full[n, pl.ds(1, SIDE, stride=8), :])
        at = n * TRAVEL
        for (c, place, many), (d, spot, count) in zip(TO_EAST, TO_WEST):
            lay(0, 1 - c, slot, place, west[pl.ds(at, many), :])
            lay(1, 1 + d, slot, spot, east[pl.ds(at, count), :])
            at += many

    if swap:
        fields = []
        low = lanes((8, 128)) < SPAN
        for n in range(3):
            v = plane[pl.ds(8 * n, 8), :]
            for w in (v, pltpu.roll(v, 4, 0)):
                turned = pltpu.roll(w, SPAN, 1)
                fields += [jnp.where(low, w, turned), jnp.where(low, turned, w)]
        which, ratio, mean_gain, fluct_gain = (gains[pl.ds(8 * k, 8), :] for k in range(4))
    else:
        fields = [plane[pl.ds(deep * n, deep), :] for n in range(SUMS + 4)]
        which, ratio, mean_gain, fluct_gain = fields[SUMS:]

    def target(fields):
        def blend(v):
            low, high = v[0:1], v[1:2]
            low = jnp.broadcast_to(low, v.shape)
            high = jnp.broadcast_to(high, v.shape)
            for r in range(1, total_y - 1):
                chosen = which == float(r)
                low = jnp.where(chosen, jnp.broadcast_to(v[r : r + 1], v.shape), low)
                high = jnp.where(chosen, jnp.broadcast_to(v[r + 1 : r + 2], v.shape), high)
            return (1.0 - ratio) * low + ratio * high

        result = [blend(fields[0])]
        for v in fields[1:]:
            mean = jnp.sum(v, axis=1, keepdims=True) * (1.0 / 128.0)
            mean = blend(jnp.broadcast_to(mean, v.shape))
            result.append(mean_gain * mean + fluct_gain * (blend(v) - mean))
        return result

    def local(fields):
        got = []
        for k, v in enumerate(fields):
            shelf[k, pl.ds(8, deep), :] = v
            got.append(shelf[k, pl.ds(6 + 2 * gy, 8), :])
        return got

    target0 = target(fields[7:11])
    teq0 = equilibria(*target0)
    gates = [(1.0 - fields[4 + c]) * lam_at(lam, 6 + c, deep) for c in range(3)]
    row = lax.broadcasted_iota(jnp.int32, (deep, 128), 0)
    _, g = strip(lambda c, i: gates[c] * teq0[i], row, total_y, at_outlet(lam, deep))
    total = [a + b for a, b in zip(sums(g), fields[:4])]
    target1 = target(list(velocity(*total)))
    near0, near1 = local(target0), local(target1)
    goal0, goal1 = equilibria(*near0), equilibria(*near1)

    row = lax.broadcasted_iota(jnp.int32, (8, 128), 0) + 2 * gy - 2
    first, second = [], []
    for s, wanted in ((0, EAST), (1, WEST)):

        def read(c, f):
            return side[s, c, pl.ds(PLACE[f] * 8, 8), :]

        gate = [(1.0 - read(c, MASK)) * lam_at(lam, 3 * s + c, 8) for c in range(3)]

        def value(c, i):
            v = read(c, i)
            return v + gate[c] * (goal0[i] - v)

        middle, g = strip(value, row, total_y, None)
        eq = equilibria(*moments(g), wanted)
        wall = read(1, MASK) == 1.0
        for i in wanted:
            loose = g[i] - relax_rate * (g[i] - eq[i])
            v = jnp.where(wall, g[opposite[i]], loose)
            a, b = shifted(middle(i), i), shifted(v + gate[1] * (goal1[i] - v), i)
            if s == 0:
                a, b = jnp.where(gx == 0, goal0[i], a), jnp.where(gx == 0, goal1[i], b)
            else:
                a = jnp.where(gx == last_x, value(0, i), a)
            first.append(a)
            second.append(b)
    blank = [jnp.zeros((16, 128), jnp.float32)]
    for n, rows in enumerate((first + near0 + blank, second + near1 + blank)):
        turned = pltpu.roll(jnp.concatenate(rows, axis=0), 2, 1).T
        out[pl.ds(48 * n, 48), :] = turned[:48]


def steps_kernel(ways, total_y, total_x, lam, laid, cols, *rest):
    count = len(ways)
    bulk = rest[:count]
    result, early, late, out, sem = rest[count:]
    gx, gy = lax.axis_index("gx"), lax.axis_index("gy")
    at_end = gx == total_x // COLS - 1
    lane = lanes((8, 128))
    at_first, at_last = lane == 0, lane == COLS - 1
    zone = jnp.broadcast_to(lam[0:1, :], (8, 128))

    def column(step, index, at):
        return jnp.broadcast_to(cols[pl.ds(48 * step + at, 8), index : index + 1], (8, 128))

    def turned(step, index, at, lane_at):
        return pltpu.roll(cols[pl.ds(48 * step + at, 8), :], (lane_at - index) % 128, 1)

    def goals(step, slot, at, wanted, gate):
        density, vx, vy, vz = (column(step, 80 + 8 * k + slot, at) for k in range(4))
        return equilibria(gate * density, vx, vy, vz, wanted)

    def field(i, slot, rows):
        return laid[i, slot - 2, rows, :] if slot in (2, 3) else early[i, slot, rows, :]

    def finish(slot, fields):
        for chunk in range(5):
            rows = pl.ds(8 * chunk, 8)
            gate = (1.0 - field(MASK, slot, rows)) * zone
            goal = goals(0, slot, 8 * chunk, fields, gate)
            keep = 1.0 - gate
            for i in fields:
                early[i, slot, rows, :] = keep * field(i, slot, rows) + goal[i]

    def pull(ref, slot, lead, step, at, lift, mine, bottom=False, top=False):
        r = at - lift
        g = []
        for i in range(19):
            cx, cy, cz = lattice_vel[i]
            wall, kept = False, i
            if mine and cy == 1 and slot == 2:
                wall, kept = bottom, opposite[i]
            if mine and cy == -1 and slot == 3:
                wall, kept = top, mirror_pop[i]
            if wall is True:
                g.append(ref[kept, slot - lead, pl.ds(r, 8), :])
                continue
            v = ref[i, slot - cy - lead, pl.ds(r - cz, 8), :]
            if cx == 1:
                edge = turned(step, EAST.index(i) * 8 + slot, at, 0)
                v = jnp.where(at_first, edge, pltpu.roll(v, 1, 1))
            if cx == -1:
                edge = turned(step, 40 + WEST.index(i) * 8 + slot, at, COLS - 1)
                if step == 1:
                    edge = jnp.where(at_end, ref[i, slot - lead, pl.ds(r, 8), :], edge)
                v = jnp.where(at_last, edge, pltpu.roll(v, COLS - 1, 1))
            if wall is not False:
                v = jnp.where(wall, ref[kept, slot - lead, pl.ds(r, 8), :], v)
            g.append(v)
        return g

    def collide(slot, wanted, chunk, came=None, **walls):
        at = 1 + 8 * chunk
        g = pull(early, slot, 0, 0, at, 0, came is None, **walls)
        total = sums(g)
        if came is not None:
            density, mx, mz = (came[pl.ds(SUMS_AT + n * (DEPTH + 2) + 8 * chunk, 8), :] for n in range(3))
            total = (total[0] + density, total[1] + mx, total[2], total[3] + mz)
        density, vx, vy, vz = velocity(*total)
        eq = equilibria(relax_rate * density, vx, vy, vz, wanted)
        solid = field(MASK, slot, pl.ds(at, 8))
        gate = (1.0 - solid) * zone
        goal = goals(1, slot, at, wanted, gate)
        keep = 1.0 - gate
        wall = solid == 1.0
        for i in wanted:
            v = jnp.where(wall, g[opposite[i]], (1.0 - relax_rate) * g[i] + eq[i])
            late[i, slot - 1, pl.ds(8 * chunk, 8), :] = keep * v + goal[i]

    def beside(n, came_up):
        near_slot, far_slot = (1, 0) if came_up else (4, 5)
        inner = 0
        for k, (f, near) in enumerate(up_down(came_up)):
            slot = near_slot if near else far_slot
            at = k * EDGE
            early[f, slot, pl.ds(0, 2), :] = bulk[n][pl.ds(at + 2, 2), :]
            early[f, slot, pl.ds(DEPTH + 2, 2), :] = bulk[n][pl.ds(at, 2), :]
            if f in FLAT_Y:
                early[f, slot, pl.ds(2, DEPTH), :] = jnp.zeros((DEPTH, 128), jnp.float32)
            else:
                early[f, slot, pl.ds(2, DEPTH), :] = bulk[n][pl.ds(BLOCK_AT + inner * DEPTH, DEPTH), :]
                inner += 1
        moving = UP if came_up else DOWN
        finish(near_slot, FLAT_Y + moving)
        finish(far_slot, moving)
        return near_slot, moving

    def advance(near, **walls):
        for chunk in range(5):
            for came, slot, moving in near:
                collide(slot, moving, chunk, came)
            for slot in (2, 3):
                collide(slot, range(19), chunk, **walls)
        stores = []
        for chunk in range(DEPTH // 8):
            for y in range(ROWS):
                g = pull(late, 2 + y, 1, 1, 2 + 8 * chunk, 1, True, **walls)
                for i in range(19):
                    out[i, pl.ds(16 * chunk + y, 8, stride=2), :] = g[i]
            rows = pl.ds(16 * chunk, 16)
            stores.append(pltpu.make_async_copy(out.at[:, rows, :], result.at[:, rows, :], sem.at[chunk]))
            stores[-1].start()
        for copy in stores:
            copy.wait()

    if ways == (None,):
        for came_up in (False, True):

            @pl.when(gy == int(came_up))
            def _():
                for slot in (2, 3):
                    finish(slot, range(19))
                slot, moving = beside(0, came_up)
                advance([(bulk[0], slot, moving)], bottom=not came_up, top=came_up)

        return
    for slot in (2, 3):
        finish(slot, range(19))
    bottom, top = gy == 0, gy == total_y // ROWS - 1
    for n, way in enumerate(ways):

        @pl.when(jnp.logical_not(bottom if way else top))
        def _():
            slot, moving = beside(n, way)
            for chunk in range(5):
                collide(slot, moving, chunk, bulk[n])

    advance([], bottom=bottom, top=top)


def call(kernel, outs, scratch, limit, *args, held=False, leave=False):
    near = pl.BlockSpec(memory_space=pltpu.VMEM)
    far = pl.BlockSpec(memory_space=pltpu.HBM)
    inputs = [near] * len(args)
    if held:
        inputs = [pl.BlockSpec(memory_space=pltpu.SMEM)] + [far] * (len(args) - 1)
        args = [args[0]] + [pltpu.with_memory_space_constraint(v, pltpu.HBM) for v in args[1:]]
    return pl.pallas_call(
        kernel,
        out_shape=[jax.ShapeDtypeStruct(s, jnp.float32) for s in outs],
        in_specs=inputs,
        out_specs=[far if leave else near] * len(outs),
        scratch_shapes=[pltpu.VMEM(s, jnp.float32) if isinstance(s, tuple) else s for s in scratch],
        compiler_params=pltpu.CompilerParams(vmem_limit_bytes=limit << 20),
    )(*args)


def ring(count, step):
    return [(i, (i + step) % count) for i in range(count)]


def body(populations, solid_mask, recycle_plane, fringe_bounds, interp_rows, interp_weights, mean_scale, fluct_scale):
    size_x, size_y = lax.axis_size("gx"), lax.axis_size("gy")
    total_x, total_y = COLS * size_x, ROWS * size_y
    swap = size_y == 2
    ways = (None,) if swap else (True, False)
    slots = (2,) + ((None,) if swap else (0, 4))
    pairs = len(slots)
    pops = populations.reshape(19, DEPTH * ROWS, COLS)
    solid = solid_mask.reshape(DEPTH * ROWS, COLS)

    relaxed, lam, columns, z_out = call(
        functools.partial(relax_kernel, total_x),
        [(20, ROWS, DEPTH, COLS), (8, 128), (TROWS, 128), (TROWS + 40 * EDGE, 128)],
        [
            (128, 128),
            pops.shape,
            pltpu.VMEM(solid.shape, jnp.int32),
            pltpu.SMEM((2,), jnp.int32),
            pltpu.SMEM((ROWS,), jnp.int32),
            pltpu.SMEM((ROWS,), jnp.float32),
            pltpu.SMEM((ROWS,), jnp.float32),
            pltpu.SMEM((ROWS,), jnp.float32),
            pltpu.SemaphoreType.DMA((2 * PIECES + 5,)),
        ],
        8,
        recycle_plane,
        pops,
        solid,
        fringe_bounds,
        interp_rows,
        interp_weights,
        mean_scale,
        fluct_scale,
        held=True,
    )
    def across(v, way):
        if way is None:
            return lax.ppermute(v, "gy", ring(2, 1))
        step = 1 if way else -1
        return lax.ppermute(v, "gy", [(i, i + step) for i in range(size_y) if 0 <= i + step < size_y])

    beside = [across(columns, way) for way in ways]
    z_in = lax.ppermute(z_out, "gz", ring(2, 1))
    laid, *bulk_out = call(
        functools.partial(pack_kernel, ways),
        [(20, ROWS, DEPTH + 16, COLS)] + [(BULK, 128)] * len(ways),
        [(len(FLAT_Y), DEPTH + 24, 128)],
        4,
        relaxed,
        lam,
        z_in,
    )
    bulk = [across(v, way) for v, way in zip(bulk_out, ways)]
    beside_other = [lax.ppermute(v, "gz", ring(2, 1)) for v in beside]

    blocks = [columns, z_in]
    for a, b in zip(beside, beside_other):
        blocks += [a, b]
    edge_rows = 72
    full, right, left, plane, gains = call(
        functools.partial(cross_kernel, slots, swap, total_y),
        [(pairs, 16 * HALF, 128), (edge_rows, 128), (edge_rows, 128), (24 if swap else 8 * (SUMS + 4), 128), (32, 128)],
        [(8 * DECK_ROWS, 128)],
        4,
        lam,
        *blocks,
    )
    west = lax.ppermute(right, "gx", ring(size_x, 1))
    east = lax.ppermute(left, "gx", ring(size_x, -1))
    if swap and size_x == 4:
        far = lax.ppermute(plane, "gx", ring(4, 2))
        plane = plane + far + west[edge_rows - 24 :] + east[edge_rows - 24 :]
    elif swap:
        plane = lax.psum(plane, "gx")
    else:
        own = plane.reshape(SUMS + 4, 8, 128)[:, 2:4]
        first = (lax.axis_index("gx") == 0) | (jnp.arange(SUMS + 4) < SUMS)
        own = jnp.where(first[:, None, None], own, 0.0)
        whole = lax.dynamic_update_slice(
            jnp.zeros((SUMS + 4, total_y, 128), jnp.float32), own, (0, 2 * lax.axis_index("gy"), 0)
        )
        plane = lax.psum(whole, ("gx", "gy")).reshape((SUMS + 4) * total_y, 128)

    (cols,) = call(
        functools.partial(strips_kernel, slots, swap, total_y, total_x),
        [(96, 128)],
        [(2, 3, SIDE * 8, 128), (4, 16 + max(8, total_y), 128)],
        8,
        lam,
        full,
        west,
        east,
        plane,
        gains,
    )
    (out,) = call(
        functools.partial(steps_kernel, ways, total_y, total_x),
        [(19, DEPTH * ROWS, COLS)],
        [(20, 6, 48, 128), (19, 4, 40, 128), (19, DEPTH * ROWS, COLS), pltpu.SemaphoreType.DMA((DEPTH // 8,))],
        12,
        lam,
        laid,
        cols,
        *bulk,
        leave=True,
    )
    return out.reshape(populations.shape)


def solution(mesh):
    placed = (
        P(None, ("parts", "gz"), "gy", "gx"),
        P(("parts", "gz"), "gy", "gx"),
        P(),
        P(),
        P("gy"),
        P("gy"),
        P("gy"),
        P("gy"),
    )
    return jax.shard_map(
        body,
        mesh=mesh,
        in_specs=placed,
        out_specs=P(None, ("parts", "gz"), "gy", "gx"),
        check_vma=False,
    )
```

```python
import functools
import math

import jax
import jax.numpy as jnp
from jax import lax
from jax.experimental import pallas as pl
from jax.experimental.pallas import tpu as pltpu
from jax.sharding import PartitionSpec as P

lattice_vel = (
    (0, 0, 0),
    (1, 0, 0),
    (-1, 0, 0),
    (0, 1, 0),
    (0, -1, 0),
    (0, 0, 1),
    (0, 0, -1),
    (1, 1, 0),
    (-1, -1, 0),
    (1, -1, 0),
    (-1, 1, 0),
    (1, 0, 1),
    (-1, 0, -1),
    (1, 0, -1),
    (-1, 0, 1),
    (0, 1, 1),
    (0, -1, -1),
    (0, 1, -1),
    (0, -1, 1),
)
lattice_weight = (1.0 / 3.0,) + (1.0 / 18.0,) * 6 + (1.0 / 36.0,) * 12
opposite = (0, 2, 1, 4, 3, 6, 5, 8, 7, 10, 9, 12, 11, 14, 13, 16, 15, 18, 17)
mirror_pop = (0, 1, 2, 4, 3, 5, 6, 9, 10, 7, 8, 11, 12, 13, 14, 18, 17, 16, 15)
relax_rate = 1.25
fringe_peak = 0.8

DEPTH, ROWS, COLS = 32, 2, 128
SPAN = 2 * DEPTH
MASK = 19
EAST = (1, 11, 13, 7, 9)
WEST = (8, 10, 2, 12, 14)
FLAT_X = tuple(i for i in range(19) if lattice_vel[i][0] == 0)
UP = tuple(i for i in range(19) if lattice_vel[i][1] == 1)
DOWN = tuple(i for i in range(19) if lattice_vel[i][1] == -1)
FLAT_Y = tuple(i for i in range(19) if lattice_vel[i][1] == 0)

COLUMN = EAST + (MASK,) + WEST + FLAT_X + (20, 21, 22, 23)
PLACE = {field: at for at, field in enumerate(COLUMN)}
HALF = len(COLUMN) // 2
PACKED = ((1, 0, 12), (2, 0, 12), (5, 0, 12), (0, 0, 6), (4, 0, 6), (3, 5, 6), (6, 5, 6), (7, 0, 4))
WHOLE = 36
TROWS = 64
SIDE = 20
TO_EAST = ((0, 0, 8), (0, 11, 9), (1, 0, 6))
TO_WEST = ((0, 3, 8), (0, 11, 9), (1, 5, 6))
TRAVEL = 23
DECK = ((4, 0, 6), (5, 0, 24), (6, 5, 6), (7, 0, 4))
DECK_AT = {4: 0, 5: 6, 6: 30 - 5, 7: 36}
DECK_ROWS = 40
SUMS = 11
EDGE = 4
BLOCK_AT = 88
SUMS_AT = BLOCK_AT + 12 * DEPTH
BULK = SUMS_AT + 2 * (DEPTH + 2) + 44
PIECES = 2


def up_down(rows_up):
    moving = UP if rows_up else DOWN
    near = FLAT_Y + moving + (MASK,)
    far = moving + (MASK,)
    return [(f, True) for f in near] + [(f, False) for f in far]


def sums(g):
    w0, w1, w2 = lattice_weight[0], lattice_weight[1], lattice_weight[7]
    axis = g[1] + g[2] + g[3] + g[4] + g[5] + g[6]
    diag = (g[7] + g[8] + g[9] + g[10]) + (g[11] + g[12] + g[13] + g[14]) + (g[15] + g[16] + g[17] + g[18])
    density = w0 * g[0] + w1 * axis + w2 * diag
    d78, d910 = g[7] - g[8], g[9] - g[10]
    d1112, d1314 = g[11] - g[12], g[13] - g[14]
    d1516, d1718 = g[15] - g[16], g[17] - g[18]
    mx = w1 * (g[1] - g[2]) + w2 * ((d78 + d910) + (d1112 + d1314))
    my = w1 * (g[3] - g[4]) + w2 * ((d78 - d910) + (d1516 + d1718))
    mz = w1 * (g[5] - g[6]) + w2 * ((d1112 - d1314) + (d1516 - d1718))
    return density, mx, my, mz


def velocity(density, mx, my, mz):
    inverse = 1.0 / density
    return density, mx * inverse, my * inverse, mz * inverse


def moments(g):
    return velocity(*sums(g))


def equilibria(density, vx, vy, vz, wanted=range(19)):
    base = density - 1.5 * density * (vx * vx + vy * vy + vz * vz)
    linear = 3.0 * density
    square = 4.5 * density
    out = {}
    for i in wanted:
        if i in out:
            continue
        if i == 0:
            out[0] = base
            continue
        first = i if i % 2 == 1 else i - 1
        cx, cy, cz = lattice_vel[first]
        p = None
        for c, v in ((cx, vx), (cy, vy), (cz, vz)):
            if c == 0:
                continue
            p = (v if c == 1 else -v) if p is None else (p + v if c == 1 else p - v)
        even = base + square * p * p
        odd = linear * p
        out[first] = even + odd
        out[first + 1] = even - odd
    return out


def lanes(shape):
    return lax.broadcasted_iota(jnp.int32, shape, len(shape) - 1)


def ramp(x, start, finish):
    width = (finish - start).astype(jnp.float32)
    angle = math.pi * ((x - start).astype(jnp.float32) + 0.5) / width
    inside = (x >= start) & (x < finish)
    return jnp.where(inside, fringe_peak * jnp.sin(angle) ** 2, 0.0)


def relax_kernel(total_x, *refs):
    recycle, pops_in, solid_in = refs[:3]
    small_in = refs[3:8]
    relaxed, lam, columns, zmsg = refs[8:12]
    grid, pops, solid = refs[12:15]
    small, sem = refs[15:-1], refs[-1]
    loads = [
        [pltpu.make_async_copy(a.at[..., rows, :], b.at[..., rows, :], sem.at[2 * n + m]) for m, (a, b) in enumerate(((pops_in, pops), (solid_in, solid)))]
        for n, rows in enumerate(pl.ds(n * 2 * DEPTH // PIECES, 2 * DEPTH // PIECES) for n in range(PIECES))
    ]
    pieces = DEPTH // 8
    scalars = [pltpu.make_async_copy(a, b, sem.at[2 * PIECES + n]) for n, (a, b) in enumerate(zip(small_in, small))]
    for copy in loads[0] + scalars:
        copy.start()
    for load in loads[1:]:
        for copy in load:
            copy.start()
    for copy in scalars:
        copy.wait()
    bounds, rows_in, weights_in, mean_in, fluct_in = small
    gx, rp = lax.axis_index("gx"), recycle[0]
    x0 = gx * COLS
    off = rp - x0
    lane = lanes((8, 128))
    sub = lax.broadcasted_iota(jnp.int32, (8, 128), 0)
    special = jnp.where(
        lane < 3, x0 - 2 + lane, jnp.where(lane < 6, x0 + COLS - 4 + lane, rp - 7 + lane)
    )
    shares = ramp(jnp.where(sub == 0, x0 + lane, special), bounds[0], bounds[1])
    lam[...] = jnp.where(sub < 2, shares, jnp.where(rp == total_x - 1, 1.0, 0.0))

    col = lane % 8
    slot = lane // 8
    place = off + col - 5
    here = (place >= 0) & (place < COLS) & (col >= 4) & (col < 7)
    static = col < 4
    shift0 = 5 - off + 8 * 128 * 64
    extras = []
    for y in range(ROWS):
        values = jnp.zeros((8, 128), jnp.float32)
        for k, v in enumerate((rows_in[y].astype(jnp.float32), weights_in[y], mean_in[y], fluct_in[y])):
            values = jnp.where((slot == k) & (col == 7), v, values)
        extras.append(values)
    for chunk in range(pieces):
        if chunk % (pieces // PIECES) == 0:
            for copy in loads[chunk // (pieces // PIECES)]:
                copy.wait()
        for y in range(ROWS):
            rows = pl.ds(16 * chunk + y, 8, stride=2)
            g = [pops[i, rows, :] for i in range(19)]
            wall = solid[rows, :] == 1
            density, vx, vy, vz = moments(g)
            eq = equilibria(density, vx, vy, vz)
            field = {}
            for i in range(19):
                loose = g[i] - relax_rate * (g[i] - eq[i])
                field[i] = jnp.where(wall, g[opposite[i]], loose)
            field[MASK] = jnp.where(wall, 1.0, 0.0)
            field[20], field[21], field[22], field[23] = density, vx, vy, vz
            here_z = pl.ds(8 * chunk, 8)
            for f in range(20):
                relaxed[f, y, here_z, :] = field[f]
                at = TROWS + (f * 2 + y) * EDGE
                if chunk == 0:
                    zmsg[pl.ds(at, 2), :] = field[f][:2]
                if chunk == pieces - 1:
                    zmsg[pl.ds(at + 2, 2), :] = field[f][6:]
            for half in range(2):
                fixed = jnp.zeros((8, 128), jnp.float32)
                moving = jnp.zeros((8, 128), jnp.float32)
                for k in range(HALF):
                    v = field[COLUMN[half * HALF + k]]
                    mine = slot == k
                    if half * HALF + k < SIDE:
                        fixed = jnp.where(mine, pltpu.roll(v, 2 + 8 * k, 1), fixed)
                    moving = jnp.where(mine, pltpu.roll(v, (shift0 + 8 * k) % 128, 1), moving)
                rest_of = extras[y] if half == 0 else jnp.zeros((8, 128), jnp.float32)
                packed = jnp.where(static, fixed, jnp.where(here, moving, rest_of))
                grid[pl.ds((y * 2 + half) * DEPTH + 8 * chunk, 8), :] = packed
    grid[...] = grid[...].T
    at = 0
    for c, place, many in PACKED:
        v = grid[pl.ds(8 * place + c, many, stride=8), :]
        columns[pl.ds(at, many), :] = v
        zmsg[pl.ds(at, many), :] = v
        at += many


def pack_kernel(ways, relaxed, lam, z_in, *rest):
    laid, bulk, inside = rest[0], rest[1:-1], rest[-1]
    row = lam[0:1, :]
    for y in range(ROWS):
        at = TROWS + (MASK * 2 + y) * EDGE
        keep = 1.0 - (1.0 - relaxed[MASK, y, :, :]) * jnp.broadcast_to(row, (DEPTH, 128))
        keep_edge = 1.0 - (1.0 - z_in[pl.ds(at, EDGE), :]) * jnp.broadcast_to(row, (EDGE, 128))
        for f in range(20):
            at = TROWS + (f * 2 + y) * EDGE
            v, edge = relaxed[f, y, :, :], z_in[pl.ds(at, EDGE), :]
            if f != MASK:
                v, edge = v * keep, edge * keep_edge
            laid[f, y, pl.ds(0, 2), :] = edge[2:]
            laid[f, y, pl.ds(2, DEPTH), :] = v
            laid[f, y, pl.ds(DEPTH + 2, 2), :] = edge[:2]
    lane = lanes((8, 128))
    zone = jnp.broadcast_to(lam[0:1, :], (8, 128))
    zero = jnp.zeros((8, 128), jnp.float32)

    def pack(way, to):
        inner = 0
        for n, (f, near) in enumerate(up_down(way)):
            y = 1 if near == way else 0
            to[pl.ds(n * EDGE, EDGE), :] = z_in[pl.ds(TROWS + (f * 2 + y) * EDGE, EDGE), :]
            if f not in FLAT_Y:
                to[pl.ds(BLOCK_AT + inner * DEPTH, DEPTH), :] = relaxed[f, y, :, :]
                inner += 1
        y = 1 if way else 0
        for chunk in range(DEPTH // 8):
            rows = pl.ds(8 * chunk, 8)
            keep = 1.0 - (1.0 - relaxed[MASK, y, rows, :]) * zone
            for n, i in enumerate(FLAT_Y):
                inside[n, pl.ds(8 + 8 * chunk, 8), :] = relaxed[i, y, rows, :] * keep
        for n in range(len(FLAT_Y)):
            inside[n, pl.ds(0, 8), :] = zero
            inside[n, pl.ds(8 + DEPTH, 16), :] = jnp.zeros((16, 128), jnp.float32)
        for chunk in range(5):
            g = {}
            for n, i in enumerate(FLAT_Y):
                cx, _, cz = lattice_vel[i]
                v = inside[n, pl.ds(7 + 8 * chunk - cz, 8), :]
                if cx == 1:
                    v = jnp.where(lane == 0, 0.0, pltpu.roll(v, 1, 1))
                if cx == -1:
                    v = jnp.where(lane == COLS - 1, 0.0, pltpu.roll(v, COLS - 1, 1))
                g[i] = v
            w0, w1, w2 = lattice_weight[0], lattice_weight[1], lattice_weight[7]
            d12, d56 = g[1] - g[2], g[5] - g[6]
            d1112, d1314 = g[11] - g[12], g[13] - g[14]
            totals = (
                w0 * g[0] + w1 * ((g[1] + g[2]) + (g[5] + g[6])) + w2 * ((g[11] + g[12]) + (g[13] + g[14])),
                w1 * d12 + w2 * (d1112 + d1314),
                w1 * d56 + w2 * (d1112 - d1314),
            )
            many = min(8, DEPTH + 2 - 8 * chunk)
            for n, v in enumerate(totals):
                to[pl.ds(SUMS_AT + n * (DEPTH + 2) + 8 * chunk, many), :] = v[:many]

    for at, way in enumerate(ways):
        if way is None:
            gy = lax.axis_index("gy")

            @pl.when(gy == 0)
            def _():
                pack(True, bulk[at])

            @pl.when(gy != 0)
            def _():
                pack(False, bulk[at])

        else:
            pack(way, bulk[at])


def join(mine, other):
    even = (lanes(mine.shape) // DEPTH) % 2 == 0
    first = jnp.where(even, mine, pltpu.roll(other, DEPTH, 1))
    second = jnp.where(even, pltpu.roll(mine, 128 - DEPTH, 1), other)
    return first, second


def apart(v):
    low = lanes(v.shape) < SPAN
    turned = pltpu.roll(v, SPAN, 1)
    return jnp.where(low, v, turned), jnp.where(low, turned, v)


def shifted(v, i):
    _, cy, cz = lattice_vel[i]
    if cz:
        v = pltpu.roll(v, cz % 128, 1)
    if cy:
        v = pltpu.roll(v, cy % v.shape[0], 0)
    return v


def strip(value, row, total_y, edge):
    held = {}

    def middle(i):
        if i not in held:
            held[i] = value(1, i)
        return held[i]

    bottom, top = row == 0, row == total_y - 1
    g = []
    for i in range(19):
        cx, cy, _ = lattice_vel[i]
        v = shifted(middle(i) if cx == 0 else value(1 - cx, i), i)
        if cx == -1 and edge is not None:
            v = jnp.where(edge, middle(i), v)
        if cy == 1:
            v = jnp.where(bottom, middle(opposite[i]), v)
        if cy == -1:
            v = jnp.where(top, middle(mirror_pop[i]), v)
        g.append(v)
    return middle, g


def lam_at(lam, c, rows):
    return jnp.broadcast_to(lam[1:2, c : c + 1], (rows, 128))


def at_outlet(lam, rows):
    return jnp.broadcast_to(lam[2:3, 0:1], (rows, 128)) == 1.0


def cross_kernel(slots, swap, total_y, lam, *refs):
    pairs = len(slots)
    blocks = refs[: 2 * pairs]
    full, right, left, plane, gains, deck = refs[2 * pairs :]
    gy = lax.axis_index("gy")
    if swap:
        deck[...] = jnp.zeros_like(deck)
    for n in range(pairs):
        first, second = join(
            blocks[2 * n][pl.ds(0, TROWS), :], blocks[2 * n + 1][pl.ds(0, TROWS), :]
        )
        at = 0
        for c, place, many in PACKED:
            full[n, pl.ds(8 * place + c, many, stride=8), :] = first[at : at + many]
            if at < WHOLE:
                full[n, pl.ds(8 * HALF + c, many, stride=8), :] = second[at : at + many]
            at += many
        at = n * TRAVEL
        for (c, place, many), (d, spot, count) in zip(TO_EAST, TO_WEST):
            right[pl.ds(at, many), :] = full[n, pl.ds(8 * place + 1 - c, many, stride=8), :]
            left[pl.ds(at, count), :] = full[n, pl.ds(8 * spot + 2 + d, count, stride=8), :]
            at += many
        slot = 4 - 4 * gy if slots[n] is None else slots[n]
        at = 0
        for c, place, many in DECK:
            top, bottom = apart(full[n, pl.ds(8 * place + c, many, stride=8), :])
            deck[pl.ds(8 * at + slot, many, stride=8), :] = top
            deck[pl.ds(8 * at + slot + 1, many, stride=8), :] = bottom
            at += many

    def deck_at(row):
        return deck[pl.ds(8 * row, 8), :]

    def read(c, f):
        return deck_at(DECK_AT[4 + c] + PLACE[f])

    keep = [1.0 - (1.0 - read(c, MASK)) * lam_at(lam, 6 + c, 8) for c in range(3)]
    row = lax.broadcasted_iota(jnp.int32, (8, 128), 0) + 2 * gy - 2
    _, g = strip(lambda c, i: read(c, i) * keep[c], row, total_y, at_outlet(lam, 8))
    fields = list(sums(g)) + [read(c, MASK) for c in range(3)] + [read(1, 20 + k) for k in range(4)]
    params = [deck_at(36 + k) for k in range(4)]
    if not swap:
        for n, v in enumerate(fields + params):
            plane[pl.ds(8 * n, 8), :] = v
        return

    def settle(v):
        return jnp.where(gy == 0, pltpu.roll(v, 6, 0), v)

    for n, v in enumerate(params):
        gains[pl.ds(8 * n, 8), :] = settle(v)
    fields = [settle(v) for v in fields] + [jnp.zeros((8, 128), jnp.float32)]
    low, upper = lanes((8, 128)) < SPAN, lax.broadcasted_iota(jnp.int32, (8, 128), 0) < 4
    for n in range(3):
        a, b, c, d = fields[4 * n : 4 * n + 4]
        lower = pltpu.roll(jnp.where(low, c, d), 4, 0)
        plane[pl.ds(8 * n, 8), :] = jnp.where(upper, jnp.where(low, a, b), lower)
    tail = right.shape[0] - 24
    right[pl.ds(tail, 24), :] = plane[...]
    left[pl.ds(tail, 24), :] = plane[...]


def strips_kernel(slots, swap, total_y, total_x, lam, full, west, east, plane, gains, out, side, shelf):
    gx, gy = lax.axis_index("gx"), lax.axis_index("gy")
    last_x = total_x // COLS - 1
    deep = max(8, total_y)
    if swap:
        side[...] = jnp.zeros_like(side)
        shelf[...] = jnp.zeros_like(shelf)

    def lay(s, c, first, place, v):
        top, bottom = apart(v)
        many = v.shape[0]
        side[s, c, pl.ds(8 * place + first, many, stride=8), :] = top
        side[s, c, pl.ds(8 * place + first + 1, many, stride=8), :] = bottom

    for n, slot in enumerate(slots):
        slot = 4 - 4 * gy if slot is None else slot
        lay(0, 2, slot, 0, full[n, pl.ds(2, SIDE, stride=8), :])
        lay(1, 0, slot, 0, full[n, pl.ds(1, SIDE, stride=8), :])
        at = n * TRAVEL
        for (c, place, many), (d, spot, count) in zip(TO_EAST, TO_WEST):
            lay(0, 1 - c, slot, place, west[pl.ds(at, many), :])
            lay(1, 1 + d, slot, spot, east[pl.ds(at, count), :])
            at += many

    if swap:
        fields = []
        low = lanes((8, 128)) < SPAN
        for n in range(3):
            v = plane[pl.ds(8 * n, 8), :]
            for w in (v, pltpu.roll(v, 4, 0)):
                turned = pltpu.roll(w, SPAN, 1)
                fields += [jnp.where(low, w, turned), jnp.where(low, turned, w)]
        which, ratio, mean_gain, fluct_gain = (gains[pl.ds(8 * k, 8), :] for k in range(4))
    else:
        fields = [plane[pl.ds(deep * n, deep), :] for n in range(SUMS + 4)]
        which, ratio, mean_gain, fluct_gain = fields[SUMS:]

    def target(fields):
        def blend(v):
            low, high = v[0:1], v[1:2]
            low = jnp.broadcast_to(low, v.shape)
            high = jnp.broadcast_to(high, v.shape)
            for r in range(1, total_y - 1):
                chosen = which == float(r)
                low = jnp.where(chosen, jnp.broadcast_to(v[r : r + 1], v.shape), low)
                high = jnp.where(chosen, jnp.broadcast_to(v[r + 1 : r + 2], v.shape), high)
            return (1.0 - ratio) * low + ratio * high

        result = [blend(fields[0])]
        for v in fields[1:]:
            mean = jnp.sum(v, axis=1, keepdims=True) * (1.0 / 128.0)
            mean = blend(jnp.broadcast_to(mean, v.shape))
            result.append(mean_gain * mean + fluct_gain * (blend(v) - mean))
        return result

    def local(fields):
        got = []
        for k, v in enumerate(fields):
            shelf[k, pl.ds(8, deep), :] = v
            got.append(shelf[k, pl.ds(6 + 2 * gy, 8), :])
        return got

    target0 = target(fields[7:11])
    teq0 = equilibria(*target0)
    gates = [(1.0 - fields[4 + c]) * lam_at(lam, 6 + c, deep) for c in range(3)]
    row = lax.broadcasted_iota(jnp.int32, (deep, 128), 0)
    _, g = strip(lambda c, i: gates[c] * teq0[i], row, total_y, at_outlet(lam, deep))
    total = [a + b for a, b in zip(sums(g), fields[:4])]
    target1 = target(list(velocity(*total)))
    near0, near1 = local(target0), local(target1)
    goal0, goal1 = equilibria(*near0), equilibria(*near1)

    row = lax.broadcasted_iota(jnp.int32, (8, 128), 0) + 2 * gy - 2
    first, second = [], []
    for s, wanted in ((0, EAST), (1, WEST)):

        def read(c, f):
            return side[s, c, pl.ds(PLACE[f] * 8, 8), :]

        gate = [(1.0 - read(c, MASK)) * lam_at(lam, 3 * s + c, 8) for c in range(3)]

        def value(c, i):
            v = read(c, i)
            return v + gate[c] * (goal0[i] - v)

        middle, g = strip(value, row, total_y, None)
        eq = equilibria(*moments(g), wanted)
        wall = read(1, MASK) == 1.0
        for i in wanted:
            loose = g[i] - relax_rate * (g[i] - eq[i])
            v = jnp.where(wall, g[opposite[i]], loose)
            a, b = shifted(middle(i), i), shifted(v + gate[1] * (goal1[i] - v), i)
            if s == 0:
                a, b = jnp.where(gx == 0, goal0[i], a), jnp.where(gx == 0, goal1[i], b)
            else:
                a = jnp.where(gx == last_x, value(0, i), a)
            first.append(a)
            second.append(b)
    blank = [jnp.zeros((16, 128), jnp.float32)]
    for n, rows in enumerate((first + near0 + blank, second + near1 + blank)):
        turned = pltpu.roll(jnp.concatenate(rows, axis=0), 2, 1).T
        out[pl.ds(48 * n, 48), :] = turned[:48]


def steps_kernel(ways, total_y, total_x, lam, laid, cols, *rest):
    count = len(ways)
    bulk = rest[:count]
    result, early, late, out, sem = rest[count:]
    gx, gy = lax.axis_index("gx"), lax.axis_index("gy")
    at_end = gx == total_x // COLS - 1
    lane = lanes((8, 128))
    at_first, at_last = lane == 0, lane == COLS - 1
    zone = jnp.broadcast_to(lam[0:1, :], (8, 128))

    def column(step, index, at):
        return jnp.broadcast_to(cols[pl.ds(48 * step + at, 8), index : index + 1], (8, 128))

    def turned(step, index, at, lane_at):
        return pltpu.roll(cols[pl.ds(48 * step + at, 8), :], (lane_at - index) % 128, 1)

    def goals(step, slot, at, wanted, gate):
        density, vx, vy, vz = (column(step, 80 + 8 * k + slot, at) for k in range(4))
        return equilibria(gate * density, vx, vy, vz, wanted)

    def field(i, slot, rows):
        return laid[i, slot - 2, rows, :] if slot in (2, 3) else early[i, slot, rows, :]

    def finish(slot, fields):
        for chunk in range(5):
            rows = pl.ds(8 * chunk, 8)
            gate = (1.0 - field(MASK, slot, rows)) * zone
            goal = goals(0, slot, 8 * chunk, fields, gate)
            keep = 1.0 - gate
            for i in fields:
                v = field(i, slot, rows)
                early[i, slot, rows, :] = goal[i] + (v if slot in (2, 3) else keep * v)

    def pull(ref, slot, lead, step, at, lift, mine, bottom=False, top=False):
        r = at - lift
        g = []
        for i in range(19):
            cx, cy, cz = lattice_vel[i]
            wall, kept = False, i
            if mine and cy == 1 and slot == 2:
                wall, kept = bottom, opposite[i]
            if mine and cy == -1 and slot == 3:
                wall, kept = top, mirror_pop[i]
            if wall is True:
                g.append(ref[kept, slot - lead, pl.ds(r, 8), :])
                continue
            v = ref[i, slot - cy - lead, pl.ds(r - cz, 8), :]
            if cx == 1:
                edge = turned(step, EAST.index(i) * 8 + slot, at, 0)
                v = jnp.where(at_first, edge, pltpu.roll(v, 1, 1))
            if cx == -1:
                edge = turned(step, 40 + WEST.index(i) * 8 + slot, at, COLS - 1)
                if step == 1:
                    edge = jnp.where(at_end, ref[i, slot - lead, pl.ds(r, 8), :], edge)
                v = jnp.where(at_last, edge, pltpu.roll(v, COLS - 1, 1))
            if wall is not False:
                v = jnp.where(wall, ref[kept, slot - lead, pl.ds(r, 8), :], v)
            g.append(v)
        return g

    def collide(slot, wanted, chunk, came=None, **walls):
        at = 1 + 8 * chunk
        g = pull(early, slot, 0, 0, at, 0, came is None, **walls)
        total = sums(g)
        if came is not None:
            density, mx, mz = (came[pl.ds(SUMS_AT + n * (DEPTH + 2) + 8 * chunk, 8), :] for n in range(3))
            total = (total[0] + density, total[1] + mx, total[2], total[3] + mz)
        density, vx, vy, vz = velocity(*total)
        eq = equilibria(relax_rate * density, vx, vy, vz, wanted)
        solid = field(MASK, slot, pl.ds(at, 8))
        gate = (1.0 - solid) * zone
        goal = goals(1, slot, at, wanted, gate)
        keep = 1.0 - gate
        wall = solid == 1.0
        for i in wanted:
            v = jnp.where(wall, g[opposite[i]], (1.0 - relax_rate) * g[i] + eq[i])
            late[i, slot - 1, pl.ds(8 * chunk, 8), :] = keep * v + goal[i]

    def beside(n, came_up):
        near_slot, far_slot = (1, 0) if came_up else (4, 5)
        inner = 0
        for k, (f, near) in enumerate(up_down(came_up)):
            slot = near_slot if near else far_slot
            at = k * EDGE
            early[f, slot, pl.ds(0, 2), :] = bulk[n][pl.ds(at + 2, 2), :]
            early[f, slot, pl.ds(DEPTH + 2, 2), :] = bulk[n][pl.ds(at, 2), :]
            if f in FLAT_Y:
                early[f, slot, pl.ds(2, DEPTH), :] = jnp.zeros((DEPTH, 128), jnp.float32)
            else:
                early[f, slot, pl.ds(2, DEPTH), :] = bulk[n][pl.ds(BLOCK_AT + inner * DEPTH, DEPTH), :]
                inner += 1
        moving = UP if came_up else DOWN
        finish(near_slot, FLAT_Y + moving)
        finish(far_slot, moving)
        return near_slot, moving

    def advance(near, **walls):
        for chunk in range(5):
            for came, slot, moving in near:
                collide(slot, moving, chunk, came)
            for slot in (2, 3):
                collide(slot, range(19), chunk, **walls)
        stores = []
        for chunk in range(DEPTH // 8):
            for y in range(ROWS):
                g = pull(late, 2 + y, 1, 1, 2 + 8 * chunk, 1, True, **walls)
                for i in range(19):
                    out[i, pl.ds(16 * chunk + y, 8, stride=2), :] = g[i]
            rows = pl.ds(16 * chunk, 16)
            stores.append(pltpu.make_async_copy(out.at[:, rows, :], result.at[:, rows, :], sem.at[chunk]))
            stores[-1].start()
        for copy in stores:
            copy.wait()

    if ways == (None,):
        for came_up in (False, True):

            @pl.when(gy == int(came_up))
            def _():
                for slot in (2, 3):
                    finish(slot, range(19))
                slot, moving = beside(0, came_up)
                advance([(bulk[0], slot, moving)], bottom=not came_up, top=came_up)

        return
    for slot in (2, 3):
        finish(slot, range(19))
    bottom, top = gy == 0, gy == total_y // ROWS - 1
    for n, way in enumerate(ways):

        @pl.when(jnp.logical_not(bottom if way else top))
        def _():
            slot, moving = beside(n, way)
            for chunk in range(5):
                collide(slot, moving, chunk, bulk[n])

    advance([], bottom=bottom, top=top)


def call(kernel, outs, scratch, limit, *args, held=False, leave=False):
    near = pl.BlockSpec(memory_space=pltpu.VMEM)
    far = pl.BlockSpec(memory_space=pltpu.HBM)
    inputs = [near] * len(args)
    if held:
        inputs = [pl.BlockSpec(memory_space=pltpu.SMEM)] + [far] * (len(args) - 1)
        args = [args[0]] + [pltpu.with_memory_space_constraint(v, pltpu.HBM) for v in args[1:]]
    return pl.pallas_call(
        kernel,
        out_shape=[jax.ShapeDtypeStruct(s, jnp.float32) for s in outs],
        in_specs=inputs,
        out_specs=[far if leave else near] * len(outs),
        scratch_shapes=[pltpu.VMEM(s, jnp.float32) if isinstance(s, tuple) else s for s in scratch],
        compiler_params=pltpu.CompilerParams(vmem_limit_bytes=limit << 20),
    )(*args)


def ring(count, step):
    return [(i, (i + step) % count) for i in range(count)]


def body(populations, solid_mask, recycle_plane, fringe_bounds, interp_rows, interp_weights, mean_scale, fluct_scale):
    size_x, size_y = lax.axis_size("gx"), lax.axis_size("gy")
    total_x, total_y = COLS * size_x, ROWS * size_y
    swap = size_y == 2
    ways = (None,) if swap else (True, False)
    slots = (2,) + ((None,) if swap else (0, 4))
    pairs = len(slots)
    pops = populations.reshape(19, DEPTH * ROWS, COLS)
    solid = solid_mask.reshape(DEPTH * ROWS, COLS)

    relaxed, lam, columns, z_out = call(
        functools.partial(relax_kernel, total_x),
        [(20, ROWS, DEPTH, COLS), (8, 128), (TROWS, 128), (TROWS + 40 * EDGE, 128)],
        [
            (128, 128),
            pops.shape,
            pltpu.VMEM(solid.shape, jnp.int32),
            pltpu.SMEM((2,), jnp.int32),
            pltpu.SMEM((ROWS,), jnp.int32),
            pltpu.SMEM((ROWS,), jnp.float32),
            pltpu.SMEM((ROWS,), jnp.float32),
            pltpu.SMEM((ROWS,), jnp.float32),
            pltpu.SemaphoreType.DMA((2 * PIECES + 5,)),
        ],
        8,
        recycle_plane,
        pops,
        solid,
        fringe_bounds,
        interp_rows,
        interp_weights,
        mean_scale,
        fluct_scale,
        held=True,
    )
    def across(v, way):
        if way is None:
            return lax.ppermute(v, "gy", ring(2, 1))
        step = 1 if way else -1
        return lax.ppermute(v, "gy", [(i, i + step) for i in range(size_y) if 0 <= i + step < size_y])

    beside = [across(columns, way) for way in ways]
    z_in = lax.ppermute(z_out, "gz", ring(2, 1))
    laid, *bulk_out = call(
        functools.partial(pack_kernel, ways),
        [(20, ROWS, DEPTH + 16, COLS)] + [(BULK, 128)] * len(ways),
        [(len(FLAT_Y), DEPTH + 24, 128)],
        4,
        relaxed,
        lam,
        z_in,
    )
    bulk = [across(v, way) for v, way in zip(bulk_out, ways)]
    beside_other = [lax.ppermute(v, "gz", ring(2, 1)) for v in beside]

    blocks = [columns, z_in]
    for a, b in zip(beside, beside_other):
        blocks += [a, b]
    edge_rows = 72
    full, right, left, plane, gains = call(
        functools.partial(cross_kernel, slots, swap, total_y),
        [(pairs, 16 * HALF, 128), (edge_rows, 128), (edge_rows, 128), (24 if swap else 8 * (SUMS + 4), 128), (32, 128)],
        [(8 * DECK_ROWS, 128)],
        4,
        lam,
        *blocks,
    )
    west = lax.ppermute(right, "gx", ring(size_x, 1))
    east = lax.ppermute(left, "gx", ring(size_x, -1))
    if swap and size_x == 4:
        far = lax.ppermute(plane, "gx", ring(4, 2))
        plane = plane + far + west[edge_rows - 24 :] + east[edge_rows - 24 :]
    elif swap:
        plane = lax.psum(plane, "gx")
    else:
        own = plane.reshape(SUMS + 4, 8, 128)[:, 2:4]
        first = (lax.axis_index("gx") == 0) | (jnp.arange(SUMS + 4) < SUMS)
        own = jnp.where(first[:, None, None], own, 0.0)
        whole = lax.dynamic_update_slice(
            jnp.zeros((SUMS + 4, total_y, 128), jnp.float32), own, (0, 2 * lax.axis_index("gy"), 0)
        )
        plane = lax.psum(whole, ("gx", "gy")).reshape((SUMS + 4) * total_y, 128)

    (cols,) = call(
        functools.partial(strips_kernel, slots, swap, total_y, total_x),
        [(96, 128)],
        [(2, 3, SIDE * 8, 128), (4, 16 + max(8, total_y), 128)],
        8,
        lam,
        full,
        west,
        east,
        plane,
        gains,
    )
    (out,) = call(
        functools.partial(steps_kernel, ways, total_y, total_x),
        [(19, DEPTH * ROWS, COLS)],
        [(20, 6, 48, 128), (19, 4, 40, 128), (19, DEPTH * ROWS, COLS), pltpu.SemaphoreType.DMA((DEPTH // 8,))],
        12,
        lam,
        laid,
        cols,
        *bulk,
        leave=True,
    )
    return out.reshape(populations.shape)


def solution(mesh):
    placed = (
        P(None, ("parts", "gz"), "gy", "gx"),
        P(("parts", "gz"), "gy", "gx"),
        P(),
        P(),
        P("gy"),
        P("gy"),
        P("gy"),
        P("gy"),
    )
    return jax.shard_map(
        body,
        mesh=mesh,
        in_specs=placed,
        out_specs=P(None, ("parts", "gz"), "gy", "gx"),
        check_vma=False,
    )
```
